32 devices in a mesh: dp: 16 (over z, y, core), mp: 2 (over x).
Axes of the slice: x: 2, y: 2, z: 4, core: 2. Of those that a mesh axis runs over, the one named last changes fastest.
Arguments:
- tokens: bfloat16 [16, 1024, 384], P('dp'), may hold values from -6 to 6
- cotangent: bfloat16 [16, 1024, 384], P('dp'), may hold values from -6 to 6
- task_ids: int32 [16], P('dp'), may hold values from 0 to 12
- att_routes: int32 [16, 1024, 4], P('dp'), may hold values from 0 to 14, all different within a row; in each aligned block of 1024 rows (0 to 1023, 1024 to 2047, ..., all dimensions but the last counted through in order) at most 384 rows name the same one
- mlp_routes: int32 [16, 1024, 4], P('dp'), may hold values from 0 to 14, all different within a row; in each aligned block of 1024 rows (0 to 1023, 1024 to 2047, ..., all dimensions but the last counted through in order) at most 384 rows name the same one
- valid: int32 [16, 1024], P('dp'), may hold values from 0 to 1, as said below
- gain_one: float32 [384], replicated, may hold values from 0.5 to 1.5
- w_query: bfloat16 [15, 384, 384], P(None, 'dp', 'mp'), may hold values from -0.3125 to 0.3125
- w_key: bfloat16 [384, 384], P('dp', 'mp'), may hold values from -0.3125 to 0.3125
- w_value: bfloat16 [384, 384], P('dp', 'mp'), may hold values from -0.3125 to 0.3125
- w_out: bfloat16 [15, 384, 384], P(None, 'mp', 'dp'), may hold values from -4 to 4
- router_att: float32 [13, 384, 15], replicated, may hold values from -0.15 to 0.15
- gain_two: float32 [384], replicated, may hold values from 0.5 to 1.5
- w_up: bfloat16 [15, 384, 1536], P(None, 'dp', 'mp'), may hold values from -0.3125 to 0.3125
- w_down: bfloat16 [15, 1536, 384], P(None, 'mp', 'dp'), may hold values from -0.15625 to 0.15625
- router_mlp: float32 [13, 384, 15], replicated, may hold values from -0.15 to 0.15
Outputs:
- layer_out: bfloat16 [16, 1024, 384], P('dp')
- grad_tokens: float32 [16, 1024, 384], P('dp')
- grad_gain_one: float32 [384], replicated
- grad_query: float32 [15, 384, 384], P(None, 'dp', 'mp')
- grad_key: float32 [384, 384], P('dp', 'mp')
- grad_value: float32 [384, 384], P('dp', 'mp')
- grad_out: float32 [15, 384, 384], P(None, 'mp', 'dp')
- grad_router_att: float32 [13, 384, 15], replicated
- grad_gain_two: float32 [384], replicated
- grad_up: float32 [15, 384, 1536], P(None, 'dp', 'mp')
- grad_down: float32 [15, 1536, 384], P(None, 'mp', 'dp')
- grad_router_mlp: float32 [13, 384, 15], replicated
The draws below stay inside these ranges and needn't reach their ends.
Inputs may be any that keep to these rules, and one draw needn't show every extreme that they name: `att_routes`: each patch names 4 different experts; within one image no expert is named by more than 384 patches, a bound that some block reaches. `mlp_routes`: each patch names 4 different experts; within one image no expert is named by more than 384 patches, a bound that some block reaches. The share of valid patches differs from image to image.
All inputs are finite; a program needn't handle non-finite values.
Results may differ from the reference program's by a relative error of at most 0.014.
Values may be sent and summed in bfloat16 or wider, within the bound.
No kernel may reach another device: no remote copies, remote signals or barrier semaphores. Data moves between devices by JAX's collectives and lax.ppermute only.
A program may use at most 256 MiB of HBM per device.

```python
import math
import jax
import jax.numpy as jnp
import numpy as np
from jax import lax

D = 384
HEADS = 6
HDIM = 64
FF = 1536
EXPERTS = 15
TOP = 4
TASKS = 13
PATCHES = 1024
CAP = 384
HD = 384
IMAGES = 16


def draw_valid(key, part):
    key = jax.random.fold_in(key, 11)
    first_key, second_key = jax.random.split(key)
    rates = jax.random.randint(first_key, (IMAGES, 1), 2, 10)
    rolls = jax.random.randint(second_key, (IMAGES, PATCHES), 0, 10)
    return (rolls < rates).astype(jnp.int32)


def place_ends(entries, stream_key, smallest, top_value):
    longest = entries.shape.index(max(entries.shape))
    spots = []
    for shift in (0, 1):
        where = [jax.random.randint(jax.random.fold_in(stream_key, axis), (), 0, length) for axis, length in enumerate(entries.shape)]
        where[longest] = (where[longest] + shift) % entries.shape[longest]
        spots.append(tuple(where))
    return entries.at[spots[0]].set(smallest).at[spots[1]].set(top_value)


def block_levels(rng, dims, cuts, low, top_value):
    loudness = 1.0
    for position, parts in cuts:
        steps = jax.random.uniform(jax.random.fold_in(jax.random.fold_in(rng, 6), position), (parts,), jnp.float32, low / len(cuts), top_value / len(cuts))
        loudness = loudness * jnp.repeat(jnp.exp(steps), dims[position] // parts).reshape((-1,) + (1,) * (len(dims) - 1 - position))
    return loudness


def deal_out(key, own, number, rows, number_of, top, limit, slope):
    order = jax.random.permutation(key, number_of)
    crowded, usual = load_shares(number_of, rows * top, limit, slope, True), load_shares(number_of, rows * top, limit, slope, False)
    places = jnp.arange(number_of)

    def named(lengths, offset_by):
        used = int((lengths > 0).sum())
        fixed = max(1, used // 4)
        passed = fixed + (places - fixed + offset_by * (used - fixed)) % max(1, number_of - fixed)
        return jnp.zeros((number_of,), jnp.int32).at[order[jnp.where(places < fixed, places, passed)]].set(jnp.asarray(lengths, jnp.int32))

    lengths = jnp.where(number % 4 == 0, named(crowded, number // 4), named(usual, number - number // 4 - 1))
    mixed = jax.random.permutation(jax.random.fold_in(own, 3), number_of)
    giver, taker = mixed[0:number_of // 2 * 2:2], mixed[1:number_of // 2 * 2:2]
    margin = jnp.minimum(lengths[giver] - 1, limit - lengths[taker]) // 2
    margin = jnp.where((giver == order[0]) | (taker == order[0]) | (lengths[taker] == 0), 0, jnp.maximum(margin, 0))
    passed = jax.random.randint(jax.random.fold_in(own, 4), (number_of // 2,), 0, 1 << 20) % (margin + 1)
    lengths = lengths.at[giver].add(-passed).at[taker].add(passed)
    labels = jnp.searchsorted(jnp.cumsum(lengths), jnp.arange(rows * top), side="right").astype(jnp.int32)
    listing = labels.reshape(top, rows).T
    listing = listing[jax.random.permutation(jax.random.fold_in(own, 1), rows)]
    offset_by = jax.random.randint(jax.random.fold_in(own, 2), (rows, 1), 0, top)
    return jnp.take_along_axis(listing, (jnp.arange(top)[None, :] + offset_by) % top, axis=1)


def load_shares(amount, total, most, lean, full):
    loads = [(1 << 20) // math.isqrt(standing ** lean) + 1 for standing in range(1, amount + 1)]
    largest = most if full else min(most, max(-(-total // amount), total * loads[0] // sum(loads)))
    least = 1 if total - largest >= amount - 1 else 0
    holding, spare = [largest] + [least] * (amount - 1), total - largest - least * (amount - 1)
    while spare > 0:
        movable = [i for i in range(1, amount) if holding[i] < largest] or [i for i in range(1, amount) if holding[i] < most]
        mass, left = sum([loads[i] for i in movable]), spare
        for i in movable:
            more = min(most - holding[i], max(1, left * loads[i] // mass), spare)
            holding[i] = holding[i] + more
            spare = spare - more
    return np.array(holding)


def noise(key, extent, scale, limit, shards=(), kind=jnp.bfloat16):
    values = scale * jax.random.normal(key, extent, jnp.float32)
    if shards:
        values = values * block_levels(key, extent, shards, -0.22, 0.18)
    return jnp.clip(values, -limit, limit).astype(kind)


def setup_inputs(seed: int = 0) -> dict:
    key_of = jax.random.split(jax.random.key(seed), 17)
    tokens = noise(key_of[0], (IMAGES, PATCHES, D), 1.0, 6.0, ((0, 16),))
    cotangent = noise(key_of[1], (IMAGES, PATCHES, D), 1.0, 6.0, ((0, 16),))
    task_ids = place_ends(jax.random.randint(key_of[2], (IMAGES,), 0, TASKS), jax.random.fold_in(key_of[2], 1), 0, TASKS - 1).astype(jnp.int32)
    att_routes_keys = jax.random.split(jax.random.fold_in(key_of[3], 1), IMAGES * PATCHES // PATCHES)
    att_routes_turns = jax.random.permutation(jax.random.fold_in(key_of[3], 3), IMAGES * PATCHES // PATCHES)
    att_routes = jax.vmap(lambda own, number: deal_out(jax.random.fold_in(key_of[3], 2), own, number, PATCHES, EXPERTS, TOP, CAP, 1))(att_routes_keys, att_routes_turns).reshape((IMAGES, PATCHES, TOP))
    mlp_routes_keys = jax.random.split(jax.random.fold_in(key_of[4], 1), IMAGES * PATCHES // PATCHES)
    mlp_routes_turns = jax.random.permutation(jax.random.fold_in(key_of[4], 3), IMAGES * PATCHES // PATCHES)
    mlp_routes = jax.vmap(lambda own, number: deal_out(jax.random.fold_in(key_of[4], 2), own, number, PATCHES, EXPERTS, TOP, CAP, 1))(mlp_routes_keys, mlp_routes_turns).reshape((IMAGES, PATCHES, TOP))
    valid = draw_valid(jax.random.fold_in(key_of[16], 71), 0)
    gain_one = jnp.clip(1.0 + 0.1 * jax.random.normal(key_of[6], (D,), jnp.float32), 0.5, 1.5)
    w_query = noise(key_of[7], (EXPERTS, D, HD), D ** -0.5, 0.3125, ((1, 16), (2, 2)))
    w_key = noise(key_of[8], (D, HD), D ** -0.5, 0.3125, ((0, 16), (1, 2)))
    w_value = noise(key_of[9], (D, HD), D ** -0.5, 0.3125, ((0, 16), (1, 2)))
    w_out = noise(key_of[10], (EXPERTS, HD, D), 2 ** -0.5, 4.0, ((1, 2), (2, 16)))
    router_att = noise(key_of[11], (TASKS, D, EXPERTS), 0.0255, 0.15, (), jnp.float32)
    gain_two = jnp.clip(1.0 + 0.1 * jax.random.normal(key_of[12], (D,), jnp.float32), 0.5, 1.5)
    w_up = noise(key_of[13], (EXPERTS, D, FF), D ** -0.5, 0.3125, ((1, 16), (2, 2)))
    w_down = noise(key_of[14], (EXPERTS, FF, D), FF ** -0.5, 0.15625, ((1, 2), (2, 16)))
    router_mlp = noise(key_of[15], (TASKS, D, EXPERTS), 0.0255, 0.15, (), jnp.float32)
    return {"tokens": tokens, "cotangent": cotangent, "task_ids": task_ids, "att_routes": att_routes, "mlp_routes": mlp_routes, "valid": valid, "gain_one": gain_one, "w_query": w_query, "w_key": w_key, "w_value": w_value, "w_out": w_out, "router_att": router_att, "gain_two": gain_two, "w_up": w_up, "w_down": w_down, "router_mlp": router_mlp}


@jax.custom_vjp
def low(v):
    return lax.optimization_barrier(v.astype(jnp.bfloat16)).astype(jnp.float32)

@jax.custom_vjp
def low_back(v):
    return v

def low_keep(v):
    return (low(v), None)

def low_pass(kept, grad):
    return (grad,)

def back_keep(v):
    return (v, None)

def back_low(kept, grad):
    return (low(grad),)
low.defvjp(low_keep, low_pass)
low_back.defvjp(back_keep, back_low)
norm_eps = 1e-06
highest = lax.Precision.HIGHEST

def layer_norm(values_in, gain):
    centre = lax.optimization_barrier(jnp.mean(values_in, axis=-1, keepdims=True))
    shifted = values_in - centre
    spread = lax.optimization_barrier(jnp.mean(shifted * shifted, axis=-1, keepdims=True))
    return shifted * lax.rsqrt(spread + norm_eps) * gain

def softmax_rows(scores):
    row_max = lax.optimization_barrier(jnp.max(scores, axis=-1, keepdims=True))
    lifted = jnp.exp(scores - row_max)
    return lifted / lax.optimization_barrier(jnp.sum(lifted, axis=-1, keepdims=True))

def slots(routes):
    flat_ids = routes.reshape(-1)
    matches = (flat_ids[:, None] == jnp.arange(EXPERTS, dtype=jnp.int32)[None, :]).astype(jnp.int32)
    ranks = lax.optimization_barrier(jnp.sum((jnp.cumsum(matches, axis=0) - 1) * matches, axis=1))
    placed = (flat_ids * CAP + ranks).astype(jnp.int32)
    serial = jnp.arange(PATCHES * TOP, dtype=jnp.int32)
    owners = jnp.zeros((EXPERTS * CAP,), jnp.int32).at[placed].set(serial)
    filled = jnp.zeros((EXPERTS * CAP,), jnp.int32).at[placed].set(1)
    return (placed.reshape(PATCHES, TOP), owners, filled)

def gate_weights(normed, router, routes):
    logits = jnp.dot(normed, router, precision=highest)
    chosen = jnp.take_along_axis(logits, routes, axis=1)
    return softmax_rows(chosen)

def dispatch(inputs, owners, filled):
    return inputs[owners // TOP] * filled[:, None].astype(jnp.float32)

def combine(outputs, placed, gates):
    return lax.optimization_barrier(jnp.sum(outputs[placed] * gates[:, :, None], axis=1))

def attend(queries, keys, values):
    scores = low_back(jnp.einsum('rhd,khd->hrk', queries, keys, precision=highest) * 0.125)
    probs = low(softmax_rows(scores))
    return jnp.einsum('hrk,khd->rhd', probs, values, precision=highest).reshape(EXPERTS * CAP, HD)

def one_image(image, task_id, att_ids, mlp_ids, params):
    gain_one, w_query, w_key, w_value, w_out, router_att, gain_two, w_up, w_down, router_mlp = params
    placed_att, owners_att, filled_att = slots(att_ids)
    placed_mlp, owners_mlp, filled_mlp = slots(mlp_ids)
    normed_one = layer_norm(image, gain_one)
    input_one = low(normed_one)
    keys = low(low_back(jnp.dot(input_one, w_key, precision=highest))).reshape(PATCHES, HEADS, HDIM)
    values = low(low_back(jnp.dot(input_one, w_value, precision=highest))).reshape(PATCHES, HEADS, HDIM)
    gates_att = gate_weights(normed_one, router_att[task_id], att_ids)
    rows_att = dispatch(input_one, owners_att, filled_att).reshape(EXPERTS, CAP, D)
    queries = low(low_back(jnp.einsum('ecd,edh->ech', rows_att, w_query, precision=highest)))
    mixed = low(low_back(attend(queries.reshape(EXPERTS * CAP, HEADS, HDIM), keys, values)))
    outs_att = low_back(jnp.einsum('ech,ehd->ecd', mixed.reshape(EXPERTS, CAP, HD), w_out, precision=highest))
    middle = image + combine(outs_att.reshape(EXPERTS * CAP, D), placed_att, gates_att)
    normed_two = layer_norm(middle, gain_two)
    input_two = low(normed_two)
    gates_mlp = gate_weights(normed_two, router_mlp[task_id], mlp_ids)
    rows_mlp = dispatch(input_two, owners_mlp, filled_mlp).reshape(EXPERTS, CAP, D)
    hidden = low_back(jnp.einsum('ecd,edf->ecf', rows_mlp, w_up, precision=highest))
    acts = low(jax.nn.gelu(hidden))
    outs_mlp = low_back(jnp.einsum('ecf,efd->ecd', acts, w_down, precision=highest))
    return middle + combine(outs_mlp.reshape(EXPERTS * CAP, D), placed_mlp, gates_mlp)

def reference(tokens, cotangent, task_ids, att_routes, mlp_routes, valid, gain_one, w_query, w_key, w_value, w_out, router_att, gain_two, w_up, w_down, router_mlp):
    params = (gain_one.astype(jnp.float32), w_query.astype(jnp.float32), w_key.astype(jnp.float32), w_value.astype(jnp.float32), w_out.astype(jnp.float32), router_att.astype(jnp.float32), gain_two.astype(jnp.float32), w_up.astype(jnp.float32), w_down.astype(jnp.float32), router_mlp.astype(jnp.float32))

    def forward(inputs, weights):

        def per_image(packed):
            return one_image(packed[0], packed[1], packed[2], packed[3], weights)
        return lax.map(jax.checkpoint(per_image), (inputs, task_ids, att_routes, mlp_routes))
    result, pull = jax.vjp(forward, tokens.astype(jnp.float32), params)
    masked_grad = cotangent.astype(jnp.float32) * valid.astype(jnp.float32)[:, :, None]
    grad_tokens, grads = pull(masked_grad)
    return (result.astype(jnp.bfloat16), grad_tokens, grads[0], grads[1], grads[2], grads[3], grads[4], grads[5], grads[6], grads[7], grads[8], grads[9])
```

```python
import jax
import jax.numpy as jnp
from jax import lax
from jax.experimental import pallas as pl
from jax.experimental.pallas import tpu as pltpu
from jax.sharding import PartitionSpec as P

HDIM = 64
EXPERTS = 15
SLOTS = 16
TOP = 4
CAP = 384
PACK = 16
QT = 256
WIDE = 256

norm_eps = 1e-06
f32 = jnp.float32
bf16 = jnp.bfloat16
highest = lax.Precision.HIGHEST
log2e = 1.4426950408889634
score_scale = 0.125 * log2e
vmem_bytes = 56 * 1024 * 1024


def nn(a, b):
    return jnp.dot(a, b, preferred_element_type=f32)


def nt(a, b):
    return lax.dot_general(a, b, (((1,), (1,)), ((), ())), preferred_element_type=f32)


def params(limit=vmem_bytes):
    return pltpu.CompilerParams(vmem_limit_bytes=limit)


def cost(flops, moved):
    return pl.CostEstimate(flops=int(flops), bytes_accessed=int(moved), transcendentals=0)


def vspec():
    return pl.BlockSpec(memory_space=pltpu.VMEM)


def sds(shape, dtype):
    return jax.ShapeDtypeStruct(shape, dtype)


def norm_stats(x):
    centre = jnp.mean(x, axis=-1, keepdims=True)
    shifted = x - centre
    spread = jnp.mean(shifted * shifted, axis=-1, keepdims=True)
    inv = lax.rsqrt(spread + norm_eps)
    return shifted * inv, inv


def dense_gates(logits, chosen):
    top = jnp.max(jnp.where(chosen, logits, -jnp.inf), axis=0, keepdims=True)
    lifted = jnp.where(chosen, jnp.exp(logits - top), 0.0)
    return lifted / jnp.sum(lifted, axis=0, keepdims=True)


def prep_kernel(tok_ref, gain_ref, router_ref, ra_ref, rm_ref, x_ref, gate_ref, cma_ref, cmm_ref, meta_ref):
    patches = tok_ref.shape[0]
    xhat, _ = norm_stats(tok_ref[...].astype(f32))
    normed = xhat * gain_ref[...]
    x_ref[...] = normed.astype(bf16)
    ids = lax.broadcasted_iota(jnp.int32, (SLOTS, patches), 0)
    before = (
        lax.broadcasted_iota(jnp.int32, (patches, patches), 0)
        < lax.broadcasted_iota(jnp.int32, (patches, patches), 1)
    )
    tri = jnp.where(before, 1.0, 0.0).astype(bf16)
    small = lax.broadcasted_iota(jnp.int32, (SLOTS, SLOTS), 1) < lax.broadcasted_iota(
        jnp.int32, (SLOTS, SLOTS), 0
    )
    lower = jnp.where(small, 1.0, 0.0)
    for routes, cm_ref, at in ((ra_ref, cma_ref, 0), (rm_ref, cmm_ref, 2)):
        named = jnp.zeros((SLOTS, patches), f32)
        for k in range(TOP):
            named = named + jnp.where(routes[k : k + 1, :] == ids, 1.0, 0.0)
        ranks = nn(named.astype(bf16), tri)
        cm_ref[...] = jnp.where(named > 0.0, ranks, -1.0).astype(jnp.int32)
        count = jnp.sum(named, axis=1, keepdims=True)
        packed = jnp.ceil(count * (1.0 / PACK)) * PACK
        packed = jnp.broadcast_to(packed, (SLOTS, 128))
        offs = jnp.dot(lower, packed, precision=highest, preferred_element_type=f32)
        meta_ref[at] = offs.astype(jnp.int32)
        meta_ref[at + 1] = jnp.broadcast_to(count, (SLOTS, 128)).astype(jnp.int32)
    logits = lax.dot_general(
        router_ref[...], normed, (((1,), (1,)), ((), ())), precision=highest, preferred_element_type=f32
    )
    gate_ref[...] = dense_gates(logits, cma_ref[...] >= 0)


def prep(tokens, gain, router_t, ra_t, rm_t):
    patches, width = tokens.shape
    return pl.pallas_call(
        prep_kernel,
        out_shape=(
            sds((patches, width), bf16),
            sds((SLOTS, patches), f32),
            sds((SLOTS, patches), jnp.int32),
            sds((SLOTS, patches), jnp.int32),
            sds((4, SLOTS, 128), jnp.int32),
        ),
        in_specs=[vspec()] * 5,
        out_specs=[vspec()] * 5,
        compiler_params=params(),
        cost_estimate=cost(8e9, 4e6),
        name="prep",
    )(tokens, gain, router_t, ra_t, rm_t)


def one_hot(cm_row, rows):
    return cm_row == lax.broadcasted_iota(jnp.int32, (rows, cm_row.shape[1]), 0)


def masks(heads):
    lane = lax.broadcasted_iota(jnp.int32, (1, WIDE), 1)
    return [(lane >= h * HDIM) & (lane < (h + 1) * HDIM) for h in range(heads)], lane


def attend_kernel(
    meta, x_ref, cm_ref, wq_ref, wk_ref, wv_ref, o_ref, q_ref, lse_ref, k_ref, v_ref, rows_ref, km, vm
):
    heads = km.shape[0]
    local = heads * HDIM
    x = x_ref[...]
    head_mask, lane = masks(heads)
    k = nn(x, wk_ref[...]).astype(bf16)
    v = nn(x, wv_ref[...]).astype(bf16)
    k_ref[...] = k
    v_ref[...] = v
    for h in range(heads):
        km[h] = jnp.where(head_mask[h], k.astype(f32), 0.0).astype(bf16)
        ones = jnp.where(lane == local + h, 1.0, 0.0)
        vm[h] = jnp.where(head_mask[h], v.astype(f32), ones).astype(bf16)
    q_ref[...] = jnp.zeros(q_ref.shape, bf16)

    def project(e, carry):
        off = pl.multiple_of(meta[0, e], PACK)
        hot = jnp.where(one_hot(cm_ref[pl.ds(e, 1), :], CAP), 1.0, 0.0).astype(bf16)
        rows = nn(hot, x).astype(bf16)
        rows_ref[e] = rows
        q_ref[pl.ds(off, CAP), :local] = nn(rows, wq_ref[e]).astype(bf16)
        return carry

    lax.fori_loop(0, EXPERTS, project, 0)
    tiles = (meta[0, EXPERTS] + (QT - 1)) // QT

    def tile(i, carry):
        start = pl.multiple_of(i * QT, QT)
        q = q_ref[pl.ds(start, QT), :]
        out = jnp.zeros((QT, WIDE), f32)
        stats = jnp.zeros((QT, 128), f32)
        lane_s = lax.broadcasted_iota(jnp.int32, (1, 128), 1)
        for h in range(heads):
            s = nt(q, km[h])
            top = jnp.max(s, axis=1, keepdims=True) * score_scale
            p = jnp.exp2(s * score_scale - top).astype(bf16)
            oh = nn(p, vm[h])
            total = oh[:, local + h : local + h + 1]
            out = jnp.where(head_mask[h], oh * (1.0 / total), out)
            stats = jnp.where(lane_s == h, top + jnp.log2(total), stats)
        o_ref[pl.ds(start, QT), :] = out.astype(bf16)
        lse_ref[pl.ds(start, QT), :] = stats
        return carry

    o_ref[...] = jnp.zeros(o_ref.shape, bf16)
    lax.fori_loop(0, tiles, tile, 0)


def packed_rows(patches):
    return -(-(patches * TOP + EXPERTS * PACK + CAP) // QT) * QT


def attend(meta, x, cm, wq, wk, wv):
    patches, width = x.shape
    heads = wq.shape[2] // HDIM
    rows = packed_rows(patches)
    return pl.pallas_call(
        attend_kernel,
        out_shape=(
            sds((rows, WIDE), bf16),
            sds((rows, WIDE), bf16),
            sds((rows, 128), f32),
            sds((patches, WIDE), bf16),
            sds((patches, WIDE), bf16),
            sds((EXPERTS, CAP, width), bf16),
        ),
        in_specs=[pl.BlockSpec(memory_space=pltpu.SMEM)] + [vspec()] * 5,
        out_specs=[vspec()] * 6,
        scratch_shapes=[pltpu.VMEM((heads, patches, WIDE), bf16), pltpu.VMEM((heads, patches, WIDE), bf16)],
        compiler_params=params(),
        cost_estimate=cost(30e9, 2e7),
        name="attend",
    )(meta, x, cm, wq, wk, wv)


def out_kernel(meta, o_ref, cm_ref, gate_ref, wo_ref, part_ref, acc):
    local = wo_ref.shape[2]
    acc[...] = jnp.zeros(acc.shape, f32)

    def expert(e, carry):
        off = pl.multiple_of(meta[0, e], PACK)
        mixed = o_ref[pl.ds(off, CAP), :local]
        outs = nt(wo_ref[e], mixed).astype(bf16)
        hot = one_hot(cm_ref[pl.ds(e, 1), :], CAP)
        gated = jnp.where(hot, gate_ref[pl.ds(e, 1), :], 0.0).astype(bf16)
        acc[...] += nn(outs, gated)
        return carry

    lax.fori_loop(0, EXPERTS, expert, 0)
    part_ref[...] = acc[...].T.astype(bf16)


def out_project(meta, o, cm, gates, wo_t):
    patches = cm.shape[1]
    width = wo_t.shape[1]
    return pl.pallas_call(
        out_kernel,
        out_shape=sds((patches, width), bf16),
        in_specs=[pl.BlockSpec(memory_space=pltpu.SMEM)] + [vspec()] * 4,
        out_specs=vspec(),
        scratch_shapes=[pltpu.VMEM((width, patches), f32)],
        compiler_params=params(),
        cost_estimate=cost(8e9, 8e6),
        name="out_project",
    )(meta, o, cm, gates, wo_t)


def middle_kernel(tok_ref, mine_ref, other_ref, gain_ref, router_ref, cm_ref, grad_ref, mid_ref, x_ref, gate_ref):
    width = tok_ref.shape[1]
    middle = tok_ref[...].astype(f32) + (mine_ref[...].astype(f32) + other_ref[...].astype(f32))
    mid_ref[...] = middle
    xhat, _ = norm_stats(middle)
    normed = xhat * gain_ref[...]
    x_ref[:, :width] = normed.astype(bf16)
    x_ref[:, width:] = grad_ref[...]
    logits = lax.dot_general(
        router_ref[...], normed, (((1,), (1,)), ((), ())), precision=highest, preferred_element_type=f32
    )
    gate_ref[...] = dense_gates(logits, cm_ref[...] >= 0)


def middle_step(tokens, mine, other, gain, router_t, cm, masked):
    patches, width = tokens.shape
    return pl.pallas_call(
        middle_kernel,
        out_shape=(
            sds((patches, width), f32),
            sds((patches, 2 * width), bf16),
            sds((SLOTS, patches), f32),
        ),
        in_specs=[vspec()] * 7,
        out_specs=[vspec()] * 3,
        compiler_params=params(),
        cost_estimate=cost(4e9, 6e6),
        name="middle",
    )(tokens, mine, other, gain, router_t, cm, masked)


def gelu_parts(x):
    c = 0.7978845608028654
    square = x * x
    t = jnp.tanh(x * (c + (c * 0.044715) * square))
    half = 0.5 * (1.0 + t)
    slope = half + (0.5 * x) * (1.0 - t * t) * (c + (3.0 * c * 0.044715) * square)
    return x * half, slope


def feed_kernel(meta, x_ref, cm_ref, gate_ref, up_ref, down_ref, grad_ref, part_ref, gg_ref, acc):
    e = pl.program_id(0)
    width = x_ref.shape[1] // 2

    @pl.when(e == 0)
    def _():
        acc[...] = jnp.zeros(acc.shape, f32)
        gg_ref[...] = jnp.zeros(gg_ref.shape, f32)

    def work(rows_n):
        eq = one_hot(cm_ref[pl.ds(e, 1), :], rows_n)
        hot = jnp.where(eq, 1.0, 0.0).astype(bf16)
        gsel = jnp.where(eq, gate_ref[pl.ds(e, 1), :], 0.0)
        grow = jnp.sum(gsel, axis=1, keepdims=True)
        gated = gsel.astype(bf16)
        got = nn(hot, x_ref[...])
        rows = got[:, :width]
        grads = got[:, width:]
        up = up_ref[0]
        down = down_ref[0]
        hidden = nn(rows.astype(bf16), up)
        act, slope = gelu_parts(hidden)
        acts = act.astype(bf16)
        raw = nn(grads.astype(bf16), down)
        gg = jnp.sum(raw * acts.astype(f32), axis=1, keepdims=True)
        gg_ref[pl.ds(e, 1), :] = jnp.sum(jnp.where(eq, gg, 0.0), axis=0, keepdims=True)
        hidden_grad = (raw * grow * slope).astype(bf16)
        out_grad = (grads * grow).T.astype(bf16)
        grad_ref[1, 0] = nn(out_grad, acts).astype(bf16)
        grad_ref[0, 0] = nn(rows.T.astype(bf16), hidden_grad).astype(bf16)
        outs = nt(down, acts).astype(bf16)
        acc[:width] += nn(outs, gated)
        back = nt(up, hidden_grad).astype(bf16)
        acc[width:] += nn(back, hot)

    few = meta[1, e] <= 256

    @pl.when(few)
    def _():
        work(256)

    @pl.when(jnp.logical_not(few))
    def _():
        work(CAP)

    @pl.when(e == EXPERTS - 1)
    def _():
        part_ref[0] = acc[:width].T.astype(bf16)
        part_ref[1] = acc[width:].T.astype(bf16)


def feed(meta, x, cm, gates, weights):
    patches, double = x.shape
    width = double // 2
    hidden = weights.shape[2]
    return pl.pallas_call(
        feed_kernel,
        out_shape=(
            sds((2, EXPERTS, width, hidden), bf16),
            sds((2, patches, width), bf16),
            sds((SLOTS, patches), f32),
        ),
        grid_spec=pltpu.PrefetchScalarGridSpec(
            num_scalar_prefetch=1,
            grid=(EXPERTS,),
            in_specs=[
                pl.BlockSpec((patches, double), lambda e, m: (0, 0)),
                pl.BlockSpec((SLOTS, patches), lambda e, m: (0, 0)),
                pl.BlockSpec((SLOTS, patches), lambda e, m: (0, 0)),
                pl.BlockSpec((1, width, hidden), lambda e, m: (e, 0, 0)),
                pl.BlockSpec((1, width, hidden), lambda e, m: (e + EXPERTS, 0, 0)),
            ],
            out_specs=[
                pl.BlockSpec((2, 1, width, hidden), lambda e, m: (0, e, 0, 0)),
                pl.BlockSpec((2, patches, width), lambda e, m: (0, 0, 0)),
                pl.BlockSpec((SLOTS, patches), lambda e, m: (0, 0)),
            ],
            scratch_shapes=[pltpu.VMEM((double, patches), f32)],
        ),
        compiler_params=params(),
        cost_estimate=cost(38e9, 4e7),
        name="feed",
    )(meta, x, cm, gates, weights, weights)


def gate_back(gates, gg):
    return gates * (gg - jnp.sum(gates * gg, axis=0, keepdims=True))


def norm_back(xhat, inv, grad, gain):
    lifted = grad * gain
    first = jnp.mean(lifted, axis=-1, keepdims=True)
    second = jnp.mean(lifted * xhat, axis=-1, keepdims=True)
    return inv * (lifted - first - xhat * second)


def tn_high(a, b):
    return lax.dot_general(a, b, (((0,), (0,)), ((), ())), precision=highest, preferred_element_type=f32)


def second_back_kernel(
    mid_ref, mine_ref, other_ref, ggm_ref, ggo_ref, gate_ref, router_ref, gain_ref, masked_ref,
    mg_ref, mgb_ref, groute_ref, ggain_ref,
):
    xhat, inv = norm_stats(mid_ref[...])
    logit_grad = gate_back(gate_ref[...], ggm_ref[...] + ggo_ref[...])
    grad = (mine_ref[...].astype(f32) + other_ref[...].astype(f32)) + tn_high(logit_grad, router_ref[...])
    groute_ref[...] = jnp.dot(
        logit_grad, xhat * gain_ref[...], precision=highest, preferred_element_type=f32
    )
    ggain_ref[...] = jnp.sum(grad * xhat, axis=0, keepdims=True)
    middle_grad = masked_ref[...].astype(f32) + norm_back(xhat, inv, grad, gain_ref[...])
    mg_ref[...] = middle_grad
    mgb_ref[...] = middle_grad.astype(bf16)


def second_back(middle, mine, other, gg_mine, gg_other, gates, router_t, gain, masked):
    patches, width = middle.shape
    return pl.pallas_call(
        second_back_kernel,
        out_shape=(
            sds((patches, width), f32),
            sds((patches, width), bf16),
            sds((SLOTS, width), f32),
            sds((1, width), f32),
        ),
        in_specs=[vspec()] * 9,
        out_specs=[vspec()] * 4,
        compiler_params=params(),
        cost_estimate=cost(4e9, 8e6),
        name="second_back",
    )(middle, mine, other, gg_mine, gg_other, gates, router_t, gain, masked)


def out_back_kernel(meta, mg_ref, cm_ref, gate_ref, wo_ref, o_ref, do_ref, delta_ref, gg_ref, grad_ref):
    e = pl.program_id(0)
    local = wo_ref.shape[2]

    @pl.when(e == 0)
    def _():
        do_ref[...] = jnp.zeros(do_ref.shape, bf16)
        delta_ref[...] = jnp.zeros(delta_ref.shape, f32)
        gg_ref[...] = jnp.zeros(gg_ref.shape, f32)

    off = pl.multiple_of(meta[0, e], PACK)
    eq = one_hot(cm_ref[pl.ds(e, 1), :], CAP)
    hot = jnp.where(eq, 1.0, 0.0).astype(bf16)
    grow = jnp.sum(jnp.where(eq, gate_ref[pl.ds(e, 1), :], 0.0), axis=1, keepdims=True)
    grads = nn(hot, mg_ref[...])
    mixed = o_ref[pl.ds(off, CAP), :local]
    mixed_f = mixed.astype(f32)
    raw = nn(grads.astype(bf16), wo_ref[0])
    gg = jnp.sum(raw * mixed_f, axis=1, keepdims=True)
    gg_ref[pl.ds(e, 1), :] = jnp.sum(jnp.where(eq, gg, 0.0), axis=0, keepdims=True)
    mixed_grad = (raw * grow).astype(bf16)
    do_ref[pl.ds(off, CAP), :local] = mixed_grad
    weighed = mixed_grad.astype(f32) * mixed_f
    lane = lax.broadcasted_iota(jnp.int32, (1, local), 1)
    lane_s = lax.broadcasted_iota(jnp.int32, (1, 128), 1)
    delta = jnp.zeros((CAP, 128), f32)
    for h in range(local // HDIM):
        here = (lane >= h * HDIM) & (lane < (h + 1) * HDIM)
        total = jnp.sum(jnp.where(here, weighed, 0.0), axis=1, keepdims=True)
        delta = jnp.where(lane_s == h, total, delta)
    delta_ref[pl.ds(off, CAP), :] = delta
    grad_ref[0] = nn((grads * grow).T.astype(bf16), mixed).astype(bf16)


def out_back(meta, mg, cm, gates, wo_t, o):
    patches, width = mg.shape
    local = wo_t.shape[2]
    rows = o.shape[0]
    return pl.pallas_call(
        out_back_kernel,
        out_shape=(
            sds((rows, WIDE), bf16),
            sds((rows, 128), f32),
            sds((SLOTS, patches), f32),
            sds((EXPERTS, width, local), bf16),
        ),
        grid_spec=pltpu.PrefetchScalarGridSpec(
            num_scalar_prefetch=1,
            grid=(EXPERTS,),
            in_specs=[
                pl.BlockSpec((patches, width), lambda e, m: (0, 0)),
                pl.BlockSpec((SLOTS, patches), lambda e, m: (0, 0)),
                pl.BlockSpec((SLOTS, patches), lambda e, m: (0, 0)),
                pl.BlockSpec((1, width, local), lambda e, m: (e, 0, 0)),
                pl.BlockSpec((rows, WIDE), lambda e, m: (0, 0)),
            ],
            out_specs=[
                pl.BlockSpec((rows, WIDE), lambda e, m: (0, 0)),
                pl.BlockSpec((rows, 128), lambda e, m: (0, 0)),
                pl.BlockSpec((SLOTS, patches), lambda e, m: (0, 0)),
                pl.BlockSpec((1, width, local), lambda e, m: (e, 0, 0)),
            ],
        ),
        compiler_params=params(),
        cost_estimate=cost(10e9, 2e7),
        name="out_back",
    )(meta, mg, cm, gates, wo_t, o)


def attend_back_kernel(meta, q_ref, do_ref, lse_ref, delta_ref, k_ref, v_ref, dq_ref, dk_ref, dv_ref, km, vm, dk, dv):
    heads = km.shape[0]
    head_mask, _ = masks(heads)
    k = k_ref[...].astype(f32)
    v = v_ref[...].astype(f32)
    for h in range(heads):
        km[h] = jnp.where(head_mask[h], k, 0.0).astype(bf16)
        vm[h] = jnp.where(head_mask[h], v, 0.0).astype(bf16)
    dk[...] = jnp.zeros(dk.shape, f32)
    dv[...] = jnp.zeros(dv.shape, f32)
    dq_ref[...] = jnp.zeros(dq_ref.shape, bf16)
    tiles = (meta[0, EXPERTS] + (QT - 1)) // QT

    def tile(i, carry):
        start = pl.multiple_of(i * QT, QT)
        q = q_ref[pl.ds(start, QT), :]
        do = do_ref[pl.ds(start, QT), :]
        lse = lse_ref[pl.ds(start, QT), :]
        delta = delta_ref[pl.ds(start, QT), :]
        q_t = q.astype(f32).T.astype(bf16)
        do_t = do.astype(f32).T.astype(bf16)
        dq = jnp.zeros((QT, WIDE), f32)
        for h in range(heads):
            at = slice(h * HDIM, (h + 1) * HDIM)
            s = nt(q, km[h])
            p = jnp.exp2(s * score_scale - lse[:, h : h + 1])
            dp = nt(do, vm[h])
            ds = (p * (dp - delta[:, h : h + 1])).astype(bf16)
            dq = dq + nn(ds, km[h])
            dk[at, :] += nn(q_t[at, :], ds)
            dv[at, :] += nn(do_t[at, :], p.astype(bf16))
        dq_ref[pl.ds(start, QT), :] = (dq * 0.125).astype(bf16)
        return carry

    lax.fori_loop(0, tiles, tile, 0)
    dk_ref[...] = (dk[...] * 0.125).astype(bf16)
    dv_ref[...] = dv[...].astype(bf16)


def attend_back(meta, q, do, lse, delta, k, v, heads):
    rows = q.shape[0]
    patches = k.shape[0]
    return pl.pallas_call(
        attend_back_kernel,
        out_shape=(
            sds((rows, WIDE), bf16),
            sds((heads * HDIM, patches), bf16),
            sds((heads * HDIM, patches), bf16),
        ),
        in_specs=[pl.BlockSpec(memory_space=pltpu.SMEM)] + [vspec()] * 6,
        out_specs=[vspec()] * 3,
        scratch_shapes=[
            pltpu.VMEM((heads, patches, WIDE), bf16),
            pltpu.VMEM((heads, patches, WIDE), bf16),
            pltpu.VMEM((heads * HDIM, patches), f32),
            pltpu.VMEM((heads * HDIM, patches), f32),
        ],
        compiler_params=params(),
        cost_estimate=cost(60e9, 2e7),
        name="attend_back",
    )(meta, q, do, lse, delta, k, v)


def in_back_kernel(meta, dq_ref, dk_ref, dv_ref, rows_ref, x_ref, cm_ref, wq_ref, wk_ref, wv_ref, grad_ref, part_ref, acc):
    e = pl.program_id(0)
    local = wq_ref.shape[2]

    @pl.when(e == 0)
    def _():
        dk = dk_ref[...]
        dv = dv_ref[...]
        acc[...] = nn(wk_ref[...], dk) + nn(wv_ref[...], dv)

    off = pl.multiple_of(meta[0, e], PACK)

    @pl.when(e < EXPERTS)
    def _():
        dq = dq_ref[pl.ds(off, CAP), :local]
        rows_t = rows_ref[0].astype(f32).T.astype(bf16)
        grad_ref[0] = nn(rows_t, dq).astype(bf16)
        back = nt(wq_ref[0], dq).astype(bf16)
        hot = jnp.where(one_hot(cm_ref[pl.ds(e, 1), :], CAP), 1.0, 0.0).astype(bf16)
        acc[...] += nn(back, hot)

    @pl.when(e == EXPERTS)
    def _():
        part_ref[...] = acc[...].T.astype(bf16)
        grad_ref[0] = nn(dk_ref[...], x_ref[...]).T.astype(bf16)

    @pl.when(e == EXPERTS + 1)
    def _():
        grad_ref[0] = nn(dv_ref[...], x_ref[...]).T.astype(bf16)


def in_back(meta, dq, dk, dv, rows_att, x, cm, wq, wk, wv):
    patches, width = x.shape
    local = wq.shape[2]
    rows = dq.shape[0]
    top = EXPERTS - 1
    return pl.pallas_call(
        in_back_kernel,
        out_shape=(sds((EXPERTS + 2, width, local), bf16), sds((patches, width), bf16)),
        grid_spec=pltpu.PrefetchScalarGridSpec(
            num_scalar_prefetch=1,
            grid=(EXPERTS + 2,),
            in_specs=[
                pl.BlockSpec((rows, WIDE), lambda e, m: (0, 0)),
                pl.BlockSpec((local, patches), lambda e, m: (0, 0)),
                pl.BlockSpec((local, patches), lambda e, m: (0, 0)),
                pl.BlockSpec((1, CAP, width), lambda e, m: (jnp.minimum(e, top), 0, 0)),
                pl.BlockSpec((patches, width), lambda e, m: (0, 0)),
                pl.BlockSpec((SLOTS, patches), lambda e, m: (0, 0)),
                pl.BlockSpec((1, width, local), lambda e, m: (jnp.minimum(e, top), 0, 0)),
                pl.BlockSpec((width, local), lambda e, m: (0, 0)),
                pl.BlockSpec((width, local), lambda e, m: (0, 0)),
            ],
            out_specs=[
                pl.BlockSpec((1, width, local), lambda e, m: (e, 0, 0)),
                pl.BlockSpec((patches, width), lambda e, m: (0, 0)),
            ],
            scratch_shapes=[pltpu.VMEM((width, patches), f32)],
        ),
        compiler_params=params(),
        cost_estimate=cost(10e9, 2e7),
        name="in_back",
    )(meta, dq, dk, dv, rows_att, x, cm, wq, wk, wv)


def route_back_kernel(tok_ref, ggm_ref, ggo_ref, gate_ref, gain_ref, lg_ref, groute_ref):
    xhat, _ = norm_stats(tok_ref[...].astype(f32))
    logit_grad = gate_back(gate_ref[...], ggm_ref[...] + ggo_ref[...])
    lg_ref[...] = logit_grad
    groute_ref[...] = jnp.dot(
        logit_grad, xhat * gain_ref[...], precision=highest, preferred_element_type=f32
    )


def route_back(tokens, gg_mine, gg_other, gates, gain):
    patches, width = tokens.shape
    return pl.pallas_call(
        route_back_kernel,
        out_shape=(sds((SLOTS, patches), f32), sds((SLOTS, width), f32)),
        in_specs=[vspec()] * 5,
        out_specs=[vspec()] * 2,
        compiler_params=params(),
        cost_estimate=cost(3e9, 2e6),
        name="route_back",
    )(tokens, gg_mine, gg_other, gates, gain)


def first_back_kernel(tok_ref, mine_ref, other_ref, lg_ref, router_ref, gain_ref, mg_ref, gt_ref, ggain_ref):
    xhat, inv = norm_stats(tok_ref[...].astype(f32))
    grad = (mine_ref[...].astype(f32) + other_ref[...].astype(f32)) + tn_high(lg_ref[...], router_ref[...])
    ggain_ref[...] = jnp.sum(grad * xhat, axis=0, keepdims=True)
    gt_ref[...] = mg_ref[...] + norm_back(xhat, inv, grad, gain_ref[...])


def first_back(tokens, mine, other, logit_grad, router_t, gain, middle_grad):
    patches, width = tokens.shape
    return pl.pallas_call(
        first_back_kernel,
        out_shape=(sds((patches, width), f32), sds((1, width), f32)),
        in_specs=[vspec()] * 7,
        out_specs=[vspec()] * 2,
        compiler_params=params(),
        cost_estimate=cost(3e9, 6e6),
        name="first_back",
    )(tokens, mine, other, logit_grad, router_t, gain, middle_grad)


def other_half(x):
    return lax.ppermute(x, "mp", [(0, 1), (1, 0)])


def cube_steps(size):
    steps = []
    step = 1
    while step < size:
        steps.append(step)
        step *= 2
    return steps


def cube_sum(x, size):
    for step in cube_steps(size):
        x = x + lax.ppermute(x, "dp", [(i, i ^ step) for i in range(size)])
    return x


def cube_gather(x, size):
    index = lax.axis_index("dp")
    x = x[None]
    for step in cube_steps(size):
        got = lax.ppermute(x, "dp", [(i, i ^ step) for i in range(size)])
        upper = (index // step) % 2 == 1
        x = jnp.where(
            upper, jnp.concatenate([got, x], axis=0), jnp.concatenate([x, got], axis=0)
        )
    return x


def body(dp_size, tokens, cotangent, task_ids, att_routes, mlp_routes, valid, gain_one, w_query, w_key,
         w_value, w_out, router_att, gain_two, w_up, w_down, router_mlp):
    tokens = tokens[0]
    patches, width = tokens.shape
    local = w_key.shape[1]
    heads = local // HDIM
    tasks = router_att.shape[0]

    att_shard = jnp.concatenate([w_query, jnp.swapaxes(w_out, 1, 2), w_key[None], w_value[None]], axis=0)
    feed_shard = jnp.concatenate([w_up, jnp.swapaxes(w_down, 1, 2)], axis=0)
    att_full = lax.all_gather(att_shard, "dp", axis=1, tiled=True)
    feed_full = lax.all_gather(feed_shard, "dp", axis=1, tiled=True)

    gain_1 = gain_one[None]
    gain_2 = gain_two[None]
    task = task_ids[0]
    pick = lambda router: jnp.pad(
        lax.dynamic_index_in_dim(router, task, 0, keepdims=False).T, ((0, SLOTS - EXPERTS), (0, 0))
    )
    route_1 = pick(router_att)
    route_2 = pick(router_mlp)
    masked = cotangent[0] * valid[0][:, None].astype(bf16)

    x_one, gates_1, cm_1, cm_2, meta = prep(tokens, gain_1, route_1, att_routes[0].T, mlp_routes[0].T)
    meta_1 = meta[0:2, :, 0]
    meta_2 = meta[2:4, :, 0]

    wq = att_full[:EXPERTS]
    wo_t = att_full[EXPERTS : 2 * EXPERTS]
    wk = att_full[2 * EXPERTS]
    wv = att_full[2 * EXPERTS + 1]
    grow = ((0, 0), (0, WIDE - local))
    o, q, lse, k, v, rows_att = attend(meta_1, x_one, cm_1, wq, jnp.pad(wk, grow), jnp.pad(wv, grow))
    part = out_project(meta_1, o, cm_1, gates_1, wo_t)
    middle, x_two, gates_2 = middle_step(tokens, part, other_half(part), gain_2, route_2, cm_2, masked)
    feed_grads, parts, gg_2 = feed(meta_2, x_two, cm_2, gates_2, feed_full)
    back_two = parts[1]
    middle_grad, mg, groute_2, ggain_2 = second_back(
        middle, back_two, other_half(back_two), gg_2, other_half(gg_2), gates_2, route_2, gain_2, masked
    )
    layer_out = (middle + (parts[0].astype(f32) + other_half(parts[0]).astype(f32))).astype(bf16)
    do, delta, gg_1, grad_out = out_back(meta_1, mg, cm_1, gates_1, wo_t, o)
    logit_grad, groute_1 = route_back(tokens, gg_1, other_half(gg_1), gates_1, gain_1)
    dq, dk, dv = attend_back(meta_1, q, do, lse, delta, k, v, heads)
    grad_in, back_one = in_back(meta_1, dq, dk, dv, rows_att, x_one, cm_1, wq, wk, wv)
    grad_tokens, ggain_1 = first_back(
        tokens, back_one, other_half(back_one), logit_grad, route_1, gain_1, middle_grad
    )

    scatter = lambda g: lax.psum_scatter(g, "dp", scatter_dimension=1, tiled=True).astype(f32)
    feed_mine = scatter(feed_grads.reshape(2 * EXPERTS, width, w_up.shape[2]))
    out_mine = scatter(grad_out)
    in_mine = scatter(grad_in)

    mark = (jnp.arange(width) == task).astype(f32)[None]
    small = jnp.concatenate([groute_1[:EXPERTS], mark, groute_2[:EXPERTS], ggain_2], axis=0)
    every = cube_gather(small, dp_size)
    marks = every[:, EXPERTS, :tasks]
    route_sum = lambda g: jnp.swapaxes(
        jnp.einsum("it,ied->ted", marks, g, precision=highest, preferred_element_type=f32), 1, 2
    )
    grad_router_att = route_sum(every[:, :EXPERTS])
    grad_router_mlp = route_sum(every[:, SLOTS : SLOTS + EXPERTS])
    grad_gain_two = jnp.sum(every[:, 2 * SLOTS - 1], axis=0)
    grad_gain_one = cube_sum(ggain_1, dp_size)[0]
    return (
        layer_out[None],
        grad_tokens[None],
        grad_gain_one,
        in_mine[:EXPERTS],
        in_mine[EXPERTS],
        in_mine[EXPERTS + 1],
        jnp.swapaxes(out_mine, 1, 2),
        grad_router_att,
        grad_gain_two,
        feed_mine[:EXPERTS],
        jnp.swapaxes(feed_mine[EXPERTS:], 1, 2),
        grad_router_mlp,
    )


def solution(mesh):
    dp_size = mesh.shape["dp"]

    def run(*args):
        return body(dp_size, *args)

    return jax.shard_map(
        run,
        mesh=mesh,
        in_specs=(
            P("dp", None, None), P("dp", None, None), P("dp"), P("dp", None, None), P("dp", None, None),
            P("dp", None), P(), P(None, "dp", "mp"), P("dp", "mp"), P("dp", "mp"), P(None, "mp", "dp"),
            P(), P(), P(None, "dp", "mp"), P(None, "mp", "dp"), P(),
        ),
        out_specs=(
            P("dp", None, None), P("dp", None, None), P(), P(None, "dp", "mp"), P("dp", "mp"), P("dp", "mp"),
            P(None, "mp", "dp"), P(), P(), P(None, "dp", "mp"), P(None, "mp", "dp"), P(),
        ),
        check_vma=False,
    )
```

```python
import functools

import jax
import jax.numpy as jnp
from jax import lax
from jax.experimental import pallas as pl
from jax.experimental.pallas import tpu as pltpu
from jax.sharding import PartitionSpec as P

HDIM = 64
EXPERTS = 15
SLOTS = 16
TOP = 4
CAP = 384
PACK = 16
QT = 256
WIDE = 256
HOLD = 2
GROUP = 4
QT2 = 512
EXTRA = 16

norm_eps = 1e-06
f32 = jnp.float32
bf16 = jnp.bfloat16
highest = lax.Precision.HIGHEST
log2e = 1.4426950408889634
score_scale = 0.125 * log2e
vmem_bytes = 56 * 1024 * 1024


def nn(a, b):
    return jnp.dot(a, b, preferred_element_type=f32)


def nt(a, b):
    return lax.dot_general(a, b, (((1,), (1,)), ((), ())), preferred_element_type=f32)


def params(limit=vmem_bytes):
    return pltpu.CompilerParams(vmem_limit_bytes=limit)


def cost(flops, moved):
    return pl.CostEstimate(flops=int(flops), bytes_accessed=int(moved), transcendentals=0)


def vspec():
    return pl.BlockSpec(memory_space=pltpu.VMEM)


def sds(shape, dtype):
    return jax.ShapeDtypeStruct(shape, dtype)


def norm_stats(x):
    centre = jnp.mean(x, axis=-1, keepdims=True)
    shifted = x - centre
    spread = jnp.mean(shifted * shifted, axis=-1, keepdims=True)
    inv = lax.rsqrt(spread + norm_eps)
    return shifted * inv, inv


def dense_gates(logits, chosen):
    top = jnp.max(jnp.where(chosen, logits, -jnp.inf), axis=0, keepdims=True)
    lifted = jnp.where(chosen, jnp.exp(logits - top), 0.0)
    return lifted / jnp.sum(lifted, axis=0, keepdims=True)


def prep_kernel(tok_ref, gain_ref, router_ref, ra_ref, rm_ref, x_ref, gate_ref, cma_ref, cmm_ref, meta_ref):
    patches = tok_ref.shape[0]
    xhat, _ = norm_stats(tok_ref[...].astype(f32))
    normed = xhat * gain_ref[...]
    x_ref[...] = normed.astype(bf16)
    ids = lax.broadcasted_iota(jnp.int32, (SLOTS, patches), 0)
    before = (
        lax.broadcasted_iota(jnp.int32, (patches, patches), 0)
        < lax.broadcasted_iota(jnp.int32, (patches, patches), 1)
    )
    tri = jnp.where(before, 1.0, 0.0).astype(bf16)
    small = lax.broadcasted_iota(jnp.int32, (SLOTS, SLOTS), 1) < lax.broadcasted_iota(
        jnp.int32, (SLOTS, SLOTS), 0
    )
    lower = jnp.where(small, 1.0, 0.0)
    for routes, cm_ref, at in ((ra_ref, cma_ref, 0), (rm_ref, cmm_ref, 2)):
        named = jnp.zeros((SLOTS, patches), f32)
        for k in range(TOP):
            named = named + jnp.where(routes[k : k + 1, :] == ids, 1.0, 0.0)
        ranks = nn(named.astype(bf16), tri)
        cm_ref[...] = jnp.where(named > 0.0, ranks, -1.0).astype(jnp.int32)
        count = jnp.sum(named, axis=1, keepdims=True)
        packed = jnp.ceil(count * (1.0 / PACK)) * PACK
        packed = jnp.broadcast_to(packed, (SLOTS, 128))
        offs = jnp.dot(lower, packed, precision=highest, preferred_element_type=f32)
        meta_ref[at] = offs.astype(jnp.int32)
        meta_ref[at + 1] = jnp.broadcast_to(count, (SLOTS, 128)).astype(jnp.int32)
    logits = lax.dot_general(
        router_ref[...], normed, (((1,), (1,)), ((), ())), precision=highest, preferred_element_type=f32
    )
    gate_ref[...] = dense_gates(logits, cma_ref[...] >= 0)


def prep(tokens, gain, router_t, ra_t, rm_t):
    patches, width = tokens.shape
    return pl.pallas_call(
        prep_kernel,
        out_shape=(
            sds((patches, width), bf16),
            sds((SLOTS, patches), f32),
            sds((SLOTS, patches), jnp.int32),
            sds((SLOTS, patches), jnp.int32),
            sds((4, SLOTS, 128), jnp.int32),
        ),
        in_specs=[vspec()] * 5,
        out_specs=[vspec()] * 5,
        compiler_params=params(),
        cost_estimate=cost(8e9, 4e6),
        name="prep",
    )(tokens, gain, router_t, ra_t, rm_t)


def one_hot(cm_row, rows):
    return cm_row == lax.broadcasted_iota(jnp.int32, (rows, cm_row.shape[1]), 0)


def group(first):
    return range(first, min(first + GROUP, EXPERTS))


def masks(heads):
    lane = lax.broadcasted_iota(jnp.int32, (1, WIDE), 1)
    return [(lane >= h * HDIM) & (lane < (h + 1) * HDIM) for h in range(heads)], lane


def attend_kernel(
    meta, x_ref, cm_ref, wq_ref, wv_ref, o_ref, q_out, lse_ref, k_ref, v_ref, rows_out,
    km, vt, wide, hots, got, q_ref, rows_ref, sems,
):
    heads = km.shape[0]
    local = heads * HDIM
    x = x_ref[...]
    head_mask, lane = masks(heads)
    wide[...] = jnp.zeros(wide.shape, bf16)
    wide[:, :local] = wq_ref[EXPERTS]
    k = nn(x, wide[...]).astype(bf16)
    wide[:, :local] = wv_ref[0]
    v = nn(x, wide[...])
    k_ref[...] = k
    v_ref[...] = v.astype(bf16)
    v_t = v.T
    ones = jnp.ones((EXTRA, v_t.shape[1]), bf16)
    for h in range(heads):
        km[h] = jnp.where(head_mask[h], k.astype(f32), 0.0).astype(bf16)
        vt[h, :HDIM, :] = v_t[h * HDIM : (h + 1) * HDIM, :].astype(bf16)
        vt[h, HDIM:, :] = ones
    q_ref[...] = jnp.zeros(q_ref.shape, bf16)
    for at, first in enumerate(range(0, SLOTS, GROUP)):
        slot = at % 2
        count = len(group(first))
        for i, e in enumerate(group(first)):
            hot = one_hot(cm_ref[e : e + 1, :], CAP)
            hots[slot, i * CAP : (i + 1) * CAP, :] = jnp.where(hot, 1.0, 0.0).astype(bf16)
        got[slot, : count * CAP, :] = nn(hots[slot, : count * CAP, :], x).astype(bf16)
        for i, e in enumerate(group(first)):
            off = pl.multiple_of(meta[0, e], PACK)
            rows = got[slot, i * CAP : (i + 1) * CAP, :]
            rows_ref[e] = rows.T
            q_ref[pl.ds(off, CAP), :local] = nn(rows, wq_ref[e]).astype(bf16)
    send_q = pltpu.make_async_copy(q_ref, q_out, sems.at[0])
    send_rows = pltpu.make_async_copy(rows_ref, rows_out, sems.at[1])
    send_q.start()
    send_rows.start()
    tiles = (meta[0, EXPERTS] + (QT2 - 1)) // QT2

    def tile(i, carry):
        start = pl.multiple_of(i * QT2, QT2)
        q = q_ref[pl.ds(start, QT2), :]
        scores = [nt(km[h], q) for h in range(heads)]
        outs = []
        stats = []
        for h in range(heads):
            s = scores[h]
            top = jnp.max(s.reshape(8, s.shape[0] // 8, QT2), axis=0)
            top = jnp.max(top, axis=0, keepdims=True) * score_scale
            p = jnp.exp2(s * score_scale - top).astype(bf16)
            oh = nn(vt[h], p)
            total = oh[HDIM : HDIM + 1, :]
            outs.append(oh[:HDIM] * (1.0 / total))
            stats.append(top + jnp.log2(total))
        outs.append(jnp.zeros((WIDE - local, QT2), f32))
        stats.append(jnp.zeros((128 - heads, QT2), f32))
        o_ref[pl.ds(start, QT2), :] = jnp.concatenate(outs, axis=0).astype(bf16).T
        lse_ref[pl.ds(start, QT2), :] = jnp.concatenate(stats, axis=0).T
        return carry

    o_ref[...] = jnp.zeros(o_ref.shape, bf16)
    lax.fori_loop(0, tiles, tile, 0)
    send_q.wait()
    send_rows.wait()


def packed_rows(patches):
    return -(-(patches * TOP + EXPERTS * PACK + CAP) // QT2) * QT2


def attend(meta, x, cm, weights):
    patches, width = x.shape
    local = weights.shape[2]
    heads = local // HDIM
    rows = packed_rows(patches)
    whole = lambda *shape: pl.BlockSpec(shape, lambda i, m: (0,) * len(shape))
    return pl.pallas_call(
        attend_kernel,
        out_shape=(
            sds((rows, WIDE), bf16),
            sds((rows, WIDE), bf16),
            sds((rows, 128), f32),
            sds((patches, WIDE), bf16),
            sds((patches, WIDE), bf16),
            sds((SLOTS, width, CAP), bf16),
        ),
        grid_spec=pltpu.PrefetchScalarGridSpec(
            num_scalar_prefetch=1,
            grid=(1,),
            in_specs=[
                whole(patches, width),
                whole(SLOTS, patches),
                pl.BlockSpec((SLOTS, width, local), lambda i, m: (1, 0, 0)),
                pl.BlockSpec((1, width, local), lambda i, m: (EXPERTS, 0, 0)),
            ],
            out_specs=[
                whole(rows, WIDE),
                pl.BlockSpec(memory_space=pl.ANY),
                whole(rows, 128),
                whole(patches, WIDE),
                whole(patches, WIDE),
                pl.BlockSpec(memory_space=pl.ANY),
            ],
            scratch_shapes=[
                pltpu.VMEM((heads, patches, WIDE), bf16),
                pltpu.VMEM((heads, HDIM + EXTRA, patches), bf16),
                pltpu.VMEM((width, WIDE), bf16),
                pltpu.VMEM((2, GROUP * CAP, patches), bf16),
                pltpu.VMEM((2, GROUP * CAP, width), bf16),
                pltpu.VMEM((rows, WIDE), bf16),
                pltpu.VMEM((SLOTS, width, CAP), bf16),
                pltpu.SemaphoreType.DMA((2,)),
            ],
        ),
        compiler_params=params(),
        cost_estimate=cost(30e9, 2e7),
        name="attend",
    )(meta, x, cm, weights, weights)


def out_kernel(meta, o_ref, cm_ref, gate_ref, wo_ref, part_ref, acc, outs, hots):
    local = wo_ref.shape[2]
    for at, first in enumerate(range(0, SLOTS, GROUP)):
        slot = at % 2
        count = len(group(first)) * CAP
        for i, e in enumerate(group(first)):
            rows = slice(i * CAP, (i + 1) * CAP)
            off = pl.multiple_of(meta[0, e], PACK)
            mixed = o_ref[pl.ds(off, CAP), :local]
            outs[slot, :, rows] = nt(wo_ref[e], mixed).astype(bf16)
            hot = one_hot(cm_ref[e : e + 1, :], CAP)
            hots[slot, rows, :] = jnp.where(hot, gate_ref[e : e + 1, :], 0.0).astype(bf16)
        part = nn(outs[slot, :, :count], hots[slot, :count, :])
        if at == 0:
            acc[...] = part
        else:
            acc[...] += part
    part_ref[...] = acc[...].T.astype(bf16)


def out_project(meta, o, cm, gates, weights):
    patches = cm.shape[1]
    width, local = weights.shape[1:]
    whole = lambda *shape: pl.BlockSpec(shape, lambda i, m: (0,) * len(shape))
    return pl.pallas_call(
        out_kernel,
        out_shape=sds((patches, width), bf16),
        grid_spec=pltpu.PrefetchScalarGridSpec(
            num_scalar_prefetch=1,
            grid=(1,),
            in_specs=[
                whole(*o.shape),
                whole(SLOTS, patches),
                whole(SLOTS, patches),
                pl.BlockSpec((EXPERTS, width, local), lambda i, m: (0, 0, 0)),
            ],
            out_specs=whole(patches, width),
            scratch_shapes=[
                pltpu.VMEM((width, patches), f32),
                pltpu.VMEM((2, width, GROUP * CAP), bf16),
                pltpu.VMEM((2, GROUP * CAP, patches), bf16),
            ],
        ),
        compiler_params=params(),
        cost_estimate=cost(8e9, 8e6),
        name="out_project",
    )(meta, o, cm, gates, weights)


def middle_kernel(tok_ref, mine_ref, other_ref, gain_ref, router_ref, cm_ref, grad_ref, mid_ref, x_ref, gate_ref):
    width = tok_ref.shape[1]
    middle = tok_ref[...].astype(f32) + (mine_ref[...].astype(f32) + other_ref[...].astype(f32))
    mid_ref[...] = middle
    xhat, _ = norm_stats(middle)
    normed = xhat * gain_ref[...]
    x_ref[:, :width] = normed.astype(bf16)
    x_ref[:, width:] = grad_ref[...]
    logits = lax.dot_general(
        router_ref[...], normed, (((1,), (1,)), ((), ())), precision=highest, preferred_element_type=f32
    )
    gate_ref[...] = dense_gates(logits, cm_ref[...] >= 0)


def middle_step(tokens, mine, other, gain, router_t, cm, masked):
    patches, width = tokens.shape
    return pl.pallas_call(
        middle_kernel,
        out_shape=(
            sds((patches, width), f32),
            sds((patches, 2 * width), bf16),
            sds((SLOTS, patches), f32),
        ),
        in_specs=[vspec()] * 7,
        out_specs=[vspec()] * 3,
        compiler_params=params(),
        cost_estimate=cost(4e9, 6e6),
        name="middle",
    )(tokens, mine, other, gain, router_t, cm, masked)


def gelu_parts(x):
    c = 0.7978845608028654
    square = x * x
    t = jnp.tanh(x * (c + (c * 0.044715) * square))
    half = 0.5 * (1.0 + t)
    slope = half + (0.5 * x) * (1.0 - t * t) * (c + (3.0 * c * 0.044715) * square)
    return x * half, slope


def feed_kernel(rows_of, meta, x_ref, cm_ref, gate_ref, up_ref, down_ref, keep_ref, send_ref, part_ref, gg_ref, acc):
    e = pl.program_id(0)
    width = x_ref.shape[1] // 2

    @pl.when(e == 0)
    def _():
        acc[...] = jnp.zeros(acc.shape, f32)
        gg_ref[...] = jnp.zeros(gg_ref.shape, f32)

    def work(rows_n):
        eq = one_hot(cm_ref[pl.ds(e, 1), :], rows_n)
        hot = jnp.where(eq, 1.0, 0.0).astype(bf16)
        gsel = jnp.where(eq, gate_ref[pl.ds(e, 1), :], 0.0)
        grow = jnp.sum(gsel, axis=1, keepdims=True)
        gated = gsel.astype(bf16)
        got = nn(hot, x_ref[...])
        rows = got[:, :width]
        grads = got[:, width:]
        up = up_ref[0]
        down = down_ref[0]
        hidden = nn(rows.astype(bf16), up)
        act, slope = gelu_parts(hidden)
        acts = act.astype(bf16)
        raw = nn(grads.astype(bf16), down)
        gg = jnp.sum(raw * acts.astype(f32), axis=1, keepdims=True)
        gg_ref[pl.ds(e, 1), :] = jnp.sum(jnp.where(eq, gg, 0.0), axis=0, keepdims=True)
        hidden_grad = (raw * grow * slope).astype(bf16)
        out_grad = (grads * grow).T.astype(bf16)
        grad_down = nn(out_grad, acts).astype(bf16)
        grad_up = nn(rows.T.astype(bf16), hidden_grad).astype(bf16)

        size = keep_ref.shape[2]

        @pl.when(meta[2, 0] == 0)
        def _():
            for i, at in enumerate(rows_of):
                keep_ref[i, 0] = grad_up[at : at + size]
                send_ref[i, 0] = grad_down[at : at + size]

        @pl.when(meta[2, 0] != 0)
        def _():
            for i, at in enumerate(rows_of):
                keep_ref[i, 0] = grad_down[at : at + size]
                send_ref[i, 0] = grad_up[at : at + size]

        outs = nt(down, acts).astype(bf16)
        acc[:width] += nn(outs, gated)
        back = nt(up, hidden_grad).astype(bf16)
        acc[width:] += nn(back, hot)

    few = meta[1, e] <= 256

    @pl.when(few)
    def _():
        work(256)

    @pl.when(jnp.logical_not(few))
    def _():
        work(CAP)

    @pl.when(e == EXPERTS - 1)
    def _():
        part_ref[0] = acc[:width].T.astype(bf16)
        part_ref[1] = acc[width:].T.astype(bf16)


def feed(meta, x, cm, gates, weights, rows_of):
    patches, double = x.shape
    width = double // 2
    hidden = weights.shape[2]
    parts = len(rows_of)
    return pl.pallas_call(
        functools.partial(feed_kernel, rows_of),
        out_shape=(
            sds((parts, EXPERTS, width // parts, hidden), bf16),
            sds((parts, EXPERTS, width // parts, hidden), bf16),
            sds((2, patches, width), bf16),
            sds((SLOTS, patches), f32),
        ),
        grid_spec=pltpu.PrefetchScalarGridSpec(
            num_scalar_prefetch=1,
            grid=(EXPERTS,),
            in_specs=[
                pl.BlockSpec((patches, double), lambda e, m: (0, 0)),
                pl.BlockSpec((SLOTS, patches), lambda e, m: (0, 0)),
                pl.BlockSpec((SLOTS, patches), lambda e, m: (0, 0)),
                pl.BlockSpec((1, width, hidden), lambda e, m: (e, 0, 0)),
                pl.BlockSpec((1, width, hidden), lambda e, m: (e + EXPERTS, 0, 0)),
            ],
            out_specs=[
                pl.BlockSpec((parts, 1, width // parts, hidden), lambda e, m: (0, e, 0, 0)),
                pl.BlockSpec((parts, 1, width // parts, hidden), lambda e, m: (0, e, 0, 0)),
                pl.BlockSpec((2, patches, width), lambda e, m: (0, 0, 0)),
                pl.BlockSpec((SLOTS, patches), lambda e, m: (0, 0)),
            ],
            scratch_shapes=[pltpu.VMEM((double, patches), f32)],
        ),
        compiler_params=params(),
        cost_estimate=cost(38e9, 4e7),
        name="feed",
    )(meta, x, cm, gates, weights, weights)


def gate_back(gates, gg):
    return gates * (gg - jnp.sum(gates * gg, axis=0, keepdims=True))


def norm_back(xhat, inv, grad, gain):
    lifted = grad * gain
    first = jnp.mean(lifted, axis=-1, keepdims=True)
    second = jnp.mean(lifted * xhat, axis=-1, keepdims=True)
    return inv * (lifted - first - xhat * second)


def tn_high(a, b):
    return lax.dot_general(a, b, (((0,), (0,)), ((), ())), precision=highest, preferred_element_type=f32)


def second_back_kernel(
    mid_ref, mine_ref, other_ref, ggm_ref, ggo_ref, gate_ref, router_ref, gain_ref, masked_ref,
    mg_ref, mgb_ref, groute_ref, ggain_ref,
):
    xhat, inv = norm_stats(mid_ref[...])
    logit_grad = gate_back(gate_ref[...], ggm_ref[...] + ggo_ref[...])
    grad = (mine_ref[...].astype(f32) + other_ref[...].astype(f32)) + tn_high(logit_grad, router_ref[...])
    groute_ref[...] = jnp.dot(
        logit_grad, xhat * gain_ref[...], precision=highest, preferred_element_type=f32
    )
    ggain_ref[...] = jnp.sum(grad * xhat, axis=0, keepdims=True)
    middle_grad = masked_ref[...].astype(f32) + norm_back(xhat, inv, grad, gain_ref[...])
    mg_ref[...] = middle_grad
    mgb_ref[...] = middle_grad.astype(bf16)


def second_back(middle, mine, other, gg_mine, gg_other, gates, router_t, gain, masked):
    patches, width = middle.shape
    return pl.pallas_call(
        second_back_kernel,
        out_shape=(
            sds((patches, width), f32),
            sds((patches, width), bf16),
            sds((SLOTS, width), f32),
            sds((1, width), f32),
        ),
        in_specs=[vspec()] * 9,
        out_specs=[vspec()] * 4,
        compiler_params=params(),
        cost_estimate=cost(4e9, 8e6),
        name="second_back",
    )(middle, mine, other, gg_mine, gg_other, gates, router_t, gain, masked)


def out_back_kernel(meta, mg_ref, cm_ref, gate_ref, wo_ref, o_ref, do_ref, delta_ref, gg_ref, grad_ref, hots, got, raws, turned, wide):
    step = pl.program_id(0)
    local = wo_ref.shape[2]
    width = mg_ref.shape[1]

    @pl.when(step == 0)
    def _():
        do_ref[...] = jnp.zeros(do_ref.shape, bf16)
        delta_ref[...] = jnp.zeros(delta_ref.shape, f32)
        gg_ref[...] = jnp.zeros(gg_ref.shape, f32)
        wide[:, :width] = mg_ref[...]
        gate = gate_ref[...]
        high = gate.astype(bf16)
        rest = gate - high.astype(f32)
        mid = rest.astype(bf16)
        low = (rest - mid.astype(f32)).astype(bf16)
        blank = jnp.zeros((128 - 3 * SLOTS, gate.shape[1]), f32)
        stack = jnp.concatenate([high.astype(f32), mid.astype(f32), low.astype(f32), blank], axis=0)
        wide[:, width:] = stack.T.astype(bf16)

    for i in range(GROUP):
        hot = one_hot(cm_ref[pl.ds(step * GROUP + i, 1), :], CAP)
        hots[i * CAP : (i + 1) * CAP, :] = jnp.where(hot, 1.0, 0.0).astype(bf16)
    got[...] = nn(hots[...], wide[...])
    lane = lax.broadcasted_iota(jnp.int32, (1, local), 1)
    lane_s = lax.broadcasted_iota(jnp.int32, (1, 128), 1)
    for i in range(GROUP):
        rows = slice(i * CAP, (i + 1) * CAP)
        raws[rows, :] = nn(got[rows, :width].astype(bf16), wo_ref[i])
    for i in range(GROUP):
        e = step * GROUP + i
        rows = slice(i * CAP, (i + 1) * CAP)
        gates = got[rows, width:]
        grow = jnp.sum(jnp.where(lane_s % SLOTS == e, gates, 0.0), axis=1, keepdims=True)
        turned[:, rows] = (got[rows, :width] * grow).astype(bf16).T
        off = pl.multiple_of(meta[0, e], PACK)
        mixed_f = o_ref[pl.ds(off, CAP), :local].astype(f32)
        raw = raws[rows, :]
        gg = jnp.sum(raw * mixed_f, axis=1, keepdims=True)
        eq = one_hot(cm_ref[pl.ds(e, 1), :], CAP)
        gg_ref[pl.ds(e, 1), :] = jnp.sum(jnp.where(eq, gg, 0.0), axis=0, keepdims=True)
        mixed_grad = (raw * grow).astype(bf16)
        do_ref[pl.ds(off, CAP), :local] = mixed_grad
        weighed = mixed_grad.astype(f32) * mixed_f
        delta = jnp.zeros((CAP, 128), f32)
        for h in range(local // HDIM):
            here = (lane >= h * HDIM) & (lane < (h + 1) * HDIM)
            total = jnp.sum(jnp.where(here, weighed, 0.0), axis=1, keepdims=True)
            delta = jnp.where(lane_s == h, total, delta)
        delta_ref[pl.ds(off, CAP), :] = delta
    for i in range(GROUP):
        off = pl.multiple_of(meta[0, step * GROUP + i], PACK)
        grad_ref[i] = nn(turned[:, i * CAP : (i + 1) * CAP], o_ref[pl.ds(off, CAP), :local]).astype(bf16)


def out_back(meta, mg, cm, gates, weights, o):
    patches, width = mg.shape
    local = weights.shape[2]
    rows = o.shape[0]
    return pl.pallas_call(
        out_back_kernel,
        out_shape=(
            sds((rows, WIDE), bf16),
            sds((rows, 128), f32),
            sds((SLOTS, patches), f32),
            sds((SLOTS, width, local), bf16),
        ),
        grid_spec=pltpu.PrefetchScalarGridSpec(
            num_scalar_prefetch=1,
            grid=(SLOTS // GROUP,),
            in_specs=[
                pl.BlockSpec((patches, width), lambda e, m: (0, 0)),
                pl.BlockSpec((SLOTS, patches), lambda e, m: (0, 0)),
                pl.BlockSpec((SLOTS, patches), lambda e, m: (0, 0)),
                pl.BlockSpec((GROUP, width, local), lambda e, m: (e, 0, 0)),
                pl.BlockSpec((rows, WIDE), lambda e, m: (0, 0)),
            ],
            out_specs=[
                pl.BlockSpec((rows, WIDE), lambda e, m: (0, 0)),
                pl.BlockSpec((rows, 128), lambda e, m: (0, 0)),
                pl.BlockSpec((SLOTS, patches), lambda e, m: (0, 0)),
                pl.BlockSpec((GROUP, width, local), lambda e, m: (e, 0, 0)),
            ],
            scratch_shapes=[
                pltpu.VMEM((GROUP * CAP, patches), bf16),
                pltpu.VMEM((GROUP * CAP, width + 128), f32),
                pltpu.VMEM((GROUP * CAP, local), f32),
                pltpu.VMEM((width, GROUP * CAP), bf16),
                pltpu.VMEM((patches, width + 128), bf16),
            ],
        ),
        compiler_params=params(),
        cost_estimate=cost(10e9, 2e7),
        name="out_back",
    )(meta, mg, cm, gates, weights, o)


def attend_back_kernel(
    meta, q_ref, do_ref, lse_ref, delta_ref, k_ref, v_ref, dq_ref, dk_ref, dv_ref, km, kt, vt, dk, dv
):
    heads = km.shape[0]
    head_mask, _ = masks(heads)
    k = k_ref[...].astype(f32)
    k_t = k.T
    v_t = v_ref[...].astype(f32).T
    row = lax.broadcasted_iota(jnp.int32, (WIDE, 1), 0)
    for h in range(heads):
        here = (row >= h * HDIM) & (row < (h + 1) * HDIM)
        km[h] = jnp.where(head_mask[h], k, 0.0).astype(bf16)
        kt[h] = jnp.where(here, k_t, 0.0).astype(bf16)
        vt[h] = jnp.where(here, v_t, 0.0).astype(bf16)
    dk[...] = jnp.zeros(dk.shape, f32)
    dv[...] = jnp.zeros(dv.shape, f32)
    dq_ref[...] = jnp.zeros(dq_ref.shape, bf16)
    tiles = (meta[0, EXPERTS] + (QT - 1)) // QT

    def tile(i, carry):
        start = pl.multiple_of(i * QT, QT)
        q = q_ref[pl.ds(start, QT), :]
        do = do_ref[pl.ds(start, QT), :]
        lse = lse_ref[pl.ds(start, QT), :]
        delta = delta_ref[pl.ds(start, QT), :]
        q_t = q.T
        do_t = do.T
        dq = jnp.zeros((QT, WIDE), f32)
        pairs = [(nn(q, kt[0]), nn(do, vt[0]))]
        for h in range(heads):
            at = slice(h * HDIM, (h + 1) * HDIM)
            if h + 1 < heads:
                pairs.append((nn(q, kt[h + 1]), nn(do, vt[h + 1])))
            s, dp = pairs[h]
            p = jnp.exp2(s * score_scale - lse[:, h : h + 1])
            ds = (p * (dp - delta[:, h : h + 1])).astype(bf16)
            dq = dq + nn(ds, km[h])
            dk[at, :] += nn(q_t[at, :], ds)
            dv[at, :] += nn(do_t[at, :], p.astype(bf16))
        dq_ref[pl.ds(start, QT), :] = (dq * 0.125).astype(bf16)
        return carry

    lax.fori_loop(0, tiles, tile, 0)
    dk_ref[...] = (dk[...] * 0.125).astype(bf16)
    dv_ref[...] = dv[...].astype(bf16)


def attend_back(meta, q, do, lse, delta, k, v, heads):
    rows = q.shape[0]
    patches = k.shape[0]
    return pl.pallas_call(
        attend_back_kernel,
        out_shape=(
            sds((rows, WIDE), bf16),
            sds((heads * HDIM, patches), bf16),
            sds((heads * HDIM, patches), bf16),
        ),
        in_specs=[pl.BlockSpec(memory_space=pltpu.SMEM)] + [vspec()] * 6,
        out_specs=[vspec()] * 3,
        scratch_shapes=[
            pltpu.VMEM((heads, patches, WIDE), bf16),
            pltpu.VMEM((heads, WIDE, patches), bf16),
            pltpu.VMEM((heads, WIDE, patches), bf16),
            pltpu.VMEM((heads * HDIM, patches), f32),
            pltpu.VMEM((heads * HDIM, patches), f32),
        ],
        compiler_params=params(),
        cost_estimate=cost(60e9, 2e7),
        name="attend_back",
    )(meta, q, do, lse, delta, k, v)


def in_back_kernel(
    rows_of, meta, dq_ref, dk_ref, dv_ref, rows_ref, x_ref, cm_ref, wq_ref, wv_ref, go_ref,
    keep_ref, send_ref, part_ref, acc, got, outs, hots,
):
    step = pl.program_id(0)
    local = wq_ref.shape[2]
    size = keep_ref.shape[2]

    def put(at, first, second):
        for i, row in enumerate(rows_of):
            keep_ref[i, at] = first[row : row + size]
            send_ref[i, at] = second[row : row + size]

    @pl.when(step == 0)
    def _():
        acc[...] = jnp.zeros(acc.shape, f32)

    for i in range(GROUP):
        e = step * GROUP + i
        rows = slice(i * CAP, (i + 1) * CAP)
        hot = one_hot(cm_ref[pl.ds(e, 1), :], CAP)
        hots[rows, :] = jnp.where(hot, 1.0, 0.0).astype(bf16)
        off = pl.multiple_of(meta[0, e], PACK)
        dq = dq_ref[pl.ds(off, CAP), :local]
        outs[:, rows] = nt(wq_ref[i], dq).astype(bf16)
        got[0, i] = nn(rows_ref[i], dq).astype(bf16)
        got[1, i] = go_ref[i]
    acc[...] += nn(outs[...], hots[...])

    @pl.when(step == SLOTS // GROUP - 1)
    def _():
        dk = dk_ref[...]
        dv = dv_ref[...]
        last = GROUP - 1
        acc[...] += nn(wq_ref[last], dk) + nn(wv_ref[0], dv)
        part_ref[...] = acc[...].T.astype(bf16)
        x = x_ref[...]
        got[0, last] = nn(dk, x).T.astype(bf16)
        got[1, last] = nn(dv, x).T.astype(bf16)

    @pl.when(meta[2, 0] == 0)
    def _():
        for i in range(GROUP):
            put(i, got[0, i], got[1, i])

    @pl.when(meta[2, 0] != 0)
    def _():
        for i in range(GROUP):
            put(i, got[1, i], got[0, i])


def in_back(meta, dq, dk, dv, rows_att, x, cm, weights, grad_out, rows_of):
    patches, width = x.shape
    local = weights.shape[2]
    rows = dq.shape[0]
    parts = len(rows_of)
    sums = sds((parts, SLOTS, width // parts, local), bf16)
    sums_spec = pl.BlockSpec((parts, GROUP, width // parts, local), lambda e, m: (0, e, 0, 0))
    return pl.pallas_call(
        functools.partial(in_back_kernel, rows_of),
        out_shape=(sums, sums, sds((patches, width), bf16)),
        grid_spec=pltpu.PrefetchScalarGridSpec(
            num_scalar_prefetch=1,
            grid=(SLOTS // GROUP,),
            in_specs=[
                pl.BlockSpec((rows, WIDE), lambda e, m: (0, 0)),
                pl.BlockSpec((local, patches), lambda e, m: (0, 0)),
                pl.BlockSpec((local, patches), lambda e, m: (0, 0)),
                pl.BlockSpec((GROUP, width, CAP), lambda e, m: (e, 0, 0)),
                pl.BlockSpec((patches, width), lambda e, m: (0, 0)),
                pl.BlockSpec((SLOTS, patches), lambda e, m: (0, 0)),
                pl.BlockSpec((GROUP, width, local), lambda e, m: (e + SLOTS // GROUP, 0, 0)),
                pl.BlockSpec((1, width, local), lambda e, m: (EXPERTS, 0, 0)),
                pl.BlockSpec((GROUP, width, local), lambda e, m: (e, 0, 0)),
            ],
            out_specs=[sums_spec, sums_spec, pl.BlockSpec((patches, width), lambda e, m: (0, 0))],
            scratch_shapes=[
                pltpu.VMEM((width, patches), f32),
                pltpu.VMEM((2, GROUP, width, local), bf16),
                pltpu.VMEM((width, GROUP * CAP), bf16),
                pltpu.VMEM((GROUP * CAP, patches), bf16),
            ],
        ),
        compiler_params=params(),
        cost_estimate=cost(10e9, 2e7),
        name="in_back",
    )(meta, dq, dk, dv, rows_att, x, cm, weights, weights, grad_out)


def route_back_kernel(tok_ref, ggm_ref, ggo_ref, gate_ref, gain_ref, lg_ref, groute_ref):
    xhat, _ = norm_stats(tok_ref[...].astype(f32))
    logit_grad = gate_back(gate_ref[...], ggm_ref[...] + ggo_ref[...])
    lg_ref[...] = logit_grad
    groute_ref[...] = jnp.dot(
        logit_grad, xhat * gain_ref[...], precision=highest, preferred_element_type=f32
    )


def route_back(tokens, gg_mine, gg_other, gates, gain):
    patches, width = tokens.shape
    return pl.pallas_call(
        route_back_kernel,
        out_shape=(sds((SLOTS, patches), f32), sds((SLOTS, width), f32)),
        in_specs=[vspec()] * 5,
        out_specs=[vspec()] * 2,
        compiler_params=params(),
        cost_estimate=cost(3e9, 2e6),
        name="route_back",
    )(tokens, gg_mine, gg_other, gates, gain)


def first_back_kernel(tok_ref, mine_ref, other_ref, lg_ref, router_ref, gain_ref, mg_ref, gt_ref, ggain_ref):
    xhat, inv = norm_stats(tok_ref[...].astype(f32))
    grad = (mine_ref[...].astype(f32) + other_ref[...].astype(f32)) + tn_high(lg_ref[...], router_ref[...])
    ggain_ref[...] = jnp.sum(grad * xhat, axis=0, keepdims=True)
    gt_ref[...] = mg_ref[...] + norm_back(xhat, inv, grad, gain_ref[...])


def first_back(tokens, mine, other, logit_grad, router_t, gain, middle_grad):
    patches, width = tokens.shape
    return pl.pallas_call(
        first_back_kernel,
        out_shape=(sds((patches, width), f32), sds((1, width), f32)),
        in_specs=[vspec()] * 7,
        out_specs=[vspec()] * 2,
        compiler_params=params(),
        cost_estimate=cost(3e9, 6e6),
        name="first_back",
    )(tokens, mine, other, logit_grad, router_t, gain, middle_grad)


def tie(*values):
    return lax.optimization_barrier(values)


def after(value, first):
    return lax.optimization_barrier((value, first))[0]


def other_half(x):
    return lax.ppermute(x, "mp", [(0, 1), (1, 0)])


def cube_steps(size):
    steps = []
    step = 1
    while step < size:
        steps.append(step)
        step *= 2
    return steps


def cube_sum(x, size, marks):
    for at, step in enumerate(cube_steps(size)):
        x = wait_for(x, marks, at)
        x = x + lax.ppermute(x, "dp", [(i, i ^ step) for i in range(size)])
    return x


def wait_for(x, marks, at):
    return after(x, marks[at]) if at < len(marks) else x


def cube_gather(x, size, marks):
    index = lax.axis_index("dp")
    x = x[None]
    for at, step in enumerate(cube_steps(size)):
        x = wait_for(x, marks, at)
        got = lax.ppermute(x, "dp", [(i, i ^ step) for i in range(size)])
        upper = (index // step) % 2 == 1
        x = jnp.where(
            upper, jnp.concatenate([got, x], axis=0), jnp.concatenate([x, got], axis=0)
        )
    return x


class Ring:
    def __init__(self, size):
        self.size = size
        self.chips = size // 2
        half = self.chips // 2
        self.order = [2 * i for i in range(half)] + [2 * i + 1 for i in reversed(range(half))]
        self.groups = [[2 * chip + core for chip in self.order] for core in range(2)]
        self.next = []
        for at, chip in enumerate(self.order):
            self.next.append((2 * chip, 2 * self.order[(at + 1) % self.chips]))
            self.next.append((2 * chip + 1, 2 * self.order[at - 1] + 1))
        self.back = [(b, a) for a, b in self.next]
        self.swap = [(i, i ^ 1) for i in range(size)]
        index = lax.axis_index("dp")
        self.core = index % 2
        chip = index // 2
        place = jnp.where(chip % 2 == 0, chip // 2, self.chips - 1 - chip // 2)
        self.place = jnp.where(self.core == 0, place, self.chips - place)

    def chip(self, place):
        place = jnp.where(self.core == 0, place, -place) % self.chips
        return jnp.where(place < self.chips // 2, 2 * place, 2 * (self.chips - 1 - place) + 1)

    def cross(self, x):
        return lax.ppermute(x, "dp", self.swap)

    def step(self, x):
        return lax.ppermute(x, "dp", self.next)

    def gather(self, shard, later):
        got = self.cross(shard)
        first = jnp.where(self.core == 0, shard, got)
        second = jnp.where(self.core == 0, got, shard)
        piece = jnp.concatenate([first, second], axis=1)
        pieces = [piece]
        places = [self.place]
        half = self.chips // 2
        for step in range(1, half + 1):
            piece = self.step(piece)
            if step == HOLD:
                piece, later = lax.optimization_barrier((piece, later))
            pieces.append(piece)
            places.append(self.place - step)
            if step < half:
                pieces.append(self.cross(piece))
                places.append(self.place + step)
        return join(jnp.stack([self.chip(p) for p in places]).astype(jnp.int32), pieces), later

    def before(self, keep, got):
        return (keep.astype(f32) + got.astype(f32)).astype(bf16)

    def finish(self, total):
        count, rows, columns = total.shape
        total = total.reshape(count, 2, rows // 2, columns)
        mine = lax.dynamic_index_in_dim(total, self.core, 1, keepdims=False)
        theirs = lax.dynamic_index_in_dim(total, 1 - self.core, 1, keepdims=False)
        theirs = self.cross(theirs)
        first = jnp.where(self.core == 0, mine, theirs).astype(f32)
        second = jnp.where(self.core == 0, theirs, mine).astype(f32)
        return first, second

    def offload(self, total):
        return lax.psum_scatter(
            total, "dp", scatter_dimension=0, tiled=True, axis_index_groups=self.groups
        )[0]

    def scatter_start(self, keep, got):
        def own(place):
            place = jnp.where(self.core == 0, place, -place) % self.chips
            pick = lambda g: lax.dynamic_index_in_dim(g, place, 0, keepdims=False).astype(f32)
            return pick(keep) + pick(got)

        half = self.chips // 2
        return own(self.place + half).astype(bf16), own(self.place - half + 1).astype(bf16), own

    def scatter(self, far, near, own):
        half = self.chips // 2
        marks = [far]
        for step in range(1, half):
            far = self.step(far)
            near = lax.ppermute(near, "dp", self.back)
            far = (far.astype(f32) + own(self.place + half - step)).astype(bf16)
            if step < half - 1:
                near = (near.astype(f32) + own(self.place - half + 1 + step)).astype(bf16)
            marks.append(far)
        far = self.step(far)
        return (far.astype(f32) + (near.astype(f32) + own(self.place))).astype(bf16), marks


def join_kernel(chips, *refs):
    out = refs[-1]
    for i, piece in enumerate(refs[:-1]):
        rows = piece.shape[1]
        out[:, pl.ds(pl.multiple_of(chips[i] * rows, rows), rows), :] = piece[...]


def join(chips, pieces):
    count, rows, columns = pieces[0].shape
    block = 8
    return pl.pallas_call(
        join_kernel,
        out_shape=sds((count, rows * len(pieces), columns), bf16),
        grid_spec=pltpu.PrefetchScalarGridSpec(
            num_scalar_prefetch=1,
            grid=(count // block,),
            in_specs=[pl.BlockSpec((block, rows, columns), lambda i, m: (i, 0, 0))] * len(pieces),
            out_specs=pl.BlockSpec((block, rows * len(pieces), columns), lambda i, m: (i, 0, 0)),
        ),
        compiler_params=params(),
        cost_estimate=cost(1e6, 1e7),
        name="join",
    )(chips, *pieces)


def body(dp_size, tokens, cotangent, task_ids, att_routes, mlp_routes, valid, gain_one, w_query, w_key,
         w_value, w_out, router_att, gain_two, w_up, w_down, router_mlp):
    tokens = tokens[0]
    patches, width = tokens.shape
    local = w_key.shape[1]
    heads = local // HDIM
    tasks = router_att.shape[0]

    att_shard = jnp.concatenate([jnp.swapaxes(w_out, 1, 2), w_value[None], w_query, w_key[None]], axis=0)
    feed_shard = jnp.concatenate([w_up, jnp.swapaxes(w_down, 1, 2)], axis=0)
    ring = Ring(dp_size) if dp_size == 16 else None
    if ring is None:
        att_full = lax.all_gather(att_shard, "dp", axis=1, tiled=True)
    else:
        att_full, feed_shard = ring.gather(att_shard, feed_shard)
    feed_full = lax.all_gather(feed_shard, "dp", axis=1, tiled=True)

    gain_1 = gain_one[None]
    gain_2 = gain_two[None]
    task = task_ids[0]
    pick = lambda router: jnp.pad(
        lax.dynamic_index_in_dim(router, task, 0, keepdims=False).T, ((0, SLOTS - EXPERTS), (0, 0))
    )
    route_1 = pick(router_att)
    route_2 = pick(router_mlp)
    masked = cotangent[0] * valid[0][:, None].astype(bf16)

    x_one, gates_1, cm_1, cm_2, meta = prep(tokens, gain_1, route_1, att_routes[0].T, mlp_routes[0].T)
    core = jnp.full((1, SLOTS), 0 if ring is None else ring.core, jnp.int32)
    meta_1 = jnp.concatenate([meta[0:2, :, 0], core], axis=0)
    meta_2 = jnp.concatenate([meta[2:4, :, 0], core], axis=0)

    o, q, lse, k, v, rows_att = attend(meta_1, x_one, cm_1, att_full)
    part = out_project(meta_1, o, cm_1, gates_1, att_full)
    middle, x_two, gates_2 = middle_step(tokens, part, other_half(part), gain_2, route_2, cm_2, masked)
    rows_of = [0] if ring is None else [chip * (width // ring.chips) for chip in ring.order]
    keep, send, parts, gg_2 = feed(meta_2, x_two, cm_2, gates_2, feed_full, rows_of)
    back_two = parts[1]
    middle_grad, mg, groute_2, ggain_2 = second_back(
        middle, back_two, other_half(back_two), gg_2, other_half(gg_2), gates_2, route_2, gain_2, masked
    )
    if ring is not None:
        feed_sum = ring.before(keep, ring.cross(send))
        mg, feed_sum = lax.optimization_barrier((mg, feed_sum))
        feed_sum = ring.offload(feed_sum)
    layer_out = (middle + (parts[0].astype(f32) + other_half(parts[0]).astype(f32))).astype(bf16)
    do, delta, gg_1, grad_out = out_back(meta_1, mg, cm_1, gates_1, att_full, o)
    gg_other = other_half(gg_1)
    dq, dk, dv = attend_back(meta_1, q, do, lse, delta, k, v, heads)
    dq, gg_other = tie(dq, gg_other)
    logit_grad, groute_1 = route_back(tokens, gg_1, gg_other, gates_1, gain_1)
    mark = (jnp.arange(width) == task).astype(f32)[None]
    small = jnp.concatenate([groute_1[:EXPERTS], mark, groute_2[:EXPERTS], ggain_2], axis=0).astype(bf16)
    dq, small = tie(dq, small)
    keep_att, send_att, back_one = in_back(
        meta_1, dq, dk, dv, rows_att, x_one, cm_1, att_full, grad_out, rows_of
    )
    back_other = other_half(back_one)
    if ring is None:
        marks = []
        scatter = lambda g: lax.psum_scatter(g[0], "dp", scatter_dimension=1, tiled=True).astype(f32)
        up_mine, down_mine, q_mine, o_mine = scatter(keep), scatter(send), scatter(keep_att), scatter(send_att)
    else:
        far, near, add = ring.scatter_start(keep_att, ring.cross(send_att))
        att_sum, marks = ring.scatter(far, near, add)
        back_other = after(back_other, marks[1])
        q_mine, o_mine = ring.finish(att_sum)
        up_mine, down_mine = ring.finish(feed_sum)
    grad_tokens, ggain_1 = first_back(
        tokens, back_one, back_other, logit_grad, route_1, gain_1, middle_grad
    )

    every = cube_gather(small, dp_size, marks).astype(f32)
    named = every[:, EXPERTS, :tasks]
    route_sum = lambda g: jnp.swapaxes(
        jnp.einsum("it,ied->ted", named, g, precision=highest, preferred_element_type=f32), 1, 2
    )
    grad_router_att = route_sum(every[:, :EXPERTS])
    grad_router_mlp = route_sum(every[:, SLOTS : SLOTS + EXPERTS])
    grad_gain_two = jnp.sum(every[:, 2 * SLOTS - 1], axis=0)
    grad_gain_one = cube_sum(ggain_1, dp_size, marks[2:])[0]
    return (
        layer_out[None],
        grad_tokens[None],
        grad_gain_one,
        q_mine[:EXPERTS],
        q_mine[EXPERTS],
        o_mine[EXPERTS],
        jnp.swapaxes(o_mine[:EXPERTS], 1, 2),
        grad_router_att,
        grad_gain_two,
        up_mine,
        jnp.swapaxes(down_mine, 1, 2),
        grad_router_mlp,
    )


def solution(mesh):
    dp_size = mesh.shape["dp"]

    def run(*args):
        return body(dp_size, *args)

    return jax.shard_map(
        run,
        mesh=mesh,
        in_specs=(
            P("dp", None, None), P("dp", None, None), P("dp"), P("dp", None, None), P("dp", None, None),
            P("dp", None), P(), P(None, "dp", "mp"), P("dp", "mp"), P("dp", "mp"), P(None, "mp", "dp"),
            P(), P(), P(None, "dp", "mp"), P(None, "mp", "dp"), P(),
        ),
        out_specs=(
            P("dp", None, None), P("dp", None, None), P(), P(None, "dp", "mp"), P("dp", "mp"), P("dp", "mp"),
            P(None, "mp", "dp"), P(), P(), P(None, "dp", "mp"), P(None, "mp", "dp"), P(),
        ),
        check_vma=False,
    )
```

```python
import functools

import jax
import jax.numpy as jnp
from jax import lax
from jax.experimental import pallas as pl
from jax.experimental.pallas import tpu as pltpu
from jax.sharding import PartitionSpec as P

HDIM = 64
EXPERTS = 15
SLOTS = 16
TOP = 4
CAP = 384
PACK = 16
QT = 256
WIDE = 256
HOLD = 3
SPLIT = 9
BATCH = 3
GROUP = 4
QT2 = 512
EXTRA = 16

norm_eps = 1e-06
f32 = jnp.float32
bf16 = jnp.bfloat16
highest = lax.Precision.HIGHEST
log2e = 1.4426950408889634
score_scale = 0.125 * log2e
vmem_bytes = 60 * 1024 * 1024


def nn(a, b):
    return jnp.dot(a, b, preferred_element_type=f32)


def nt(a, b):
    return lax.dot_general(a, b, (((1,), (1,)), ((), ())), preferred_element_type=f32)


def params(limit=vmem_bytes):
    return pltpu.CompilerParams(vmem_limit_bytes=limit)


def cost(flops, moved):
    return pl.CostEstimate(flops=int(flops), bytes_accessed=int(moved), transcendentals=0)


def vspec():
    return pl.BlockSpec(memory_space=pltpu.VMEM)


def sds(shape, dtype):
    return jax.ShapeDtypeStruct(shape, dtype)


def norm_stats(x):
    centre = jnp.mean(x, axis=-1, keepdims=True)
    shifted = x - centre
    spread = jnp.mean(shifted * shifted, axis=-1, keepdims=True)
    inv = lax.rsqrt(spread + norm_eps)
    return shifted * inv, inv


def dense_gates(logits, chosen):
    top = jnp.max(jnp.where(chosen, logits, -jnp.inf), axis=0, keepdims=True)
    lifted = jnp.where(chosen, jnp.exp(logits - top), 0.0)
    return lifted / jnp.sum(lifted, axis=0, keepdims=True)


def prep_kernel(tok_ref, gain_ref, router_ref, ra_ref, rm_ref, x_ref, gate_ref, cma_ref, cmm_ref, meta_ref):
    patches = tok_ref.shape[0]
    xhat, _ = norm_stats(tok_ref[...].astype(f32))
    normed = xhat * gain_ref[...]
    x_ref[...] = normed.astype(bf16)
    ids = lax.broadcasted_iota(jnp.int32, (SLOTS, patches), 0)
    before = (
        lax.broadcasted_iota(jnp.int32, (patches, patches), 0)
        < lax.broadcasted_iota(jnp.int32, (patches, patches), 1)
    )
    tri = jnp.where(before, 1.0, 0.0).astype(bf16)
    small = lax.broadcasted_iota(jnp.int32, (SLOTS, SLOTS), 1) < lax.broadcasted_iota(
        jnp.int32, (SLOTS, SLOTS), 0
    )
    lower = jnp.where(small, 1.0, 0.0)
    for routes, cm_ref, at in ((ra_ref, cma_ref, 0), (rm_ref, cmm_ref, 2)):
        named = jnp.zeros((SLOTS, patches), f32)
        for k in range(TOP):
            named = named + jnp.where(routes[k : k + 1, :] == ids, 1.0, 0.0)
        ranks = nn(named.astype(bf16), tri)
        cm_ref[...] = jnp.where(named > 0.0, ranks, -1.0).astype(jnp.int32)
        count = jnp.sum(named, axis=1, keepdims=True)
        packed = jnp.ceil(count * (1.0 / PACK)) * PACK
        packed = jnp.broadcast_to(packed, (SLOTS, 128))
        offs = jnp.dot(lower, packed, precision=highest, preferred_element_type=f32)
        meta_ref[at] = offs.astype(jnp.int32)
        meta_ref[at + 1] = jnp.broadcast_to(count, (SLOTS, 128)).astype(jnp.int32)
    logits = lax.dot_general(
        router_ref[...], normed, (((1,), (1,)), ((), ())), precision=highest, preferred_element_type=f32
    )
    gate_ref[...] = dense_gates(logits, cma_ref[...] >= 0)


def prep(tokens, gain, router_t, ra_t, rm_t):
    patches, width = tokens.shape
    return pl.pallas_call(
        prep_kernel,
        out_shape=(
            sds((patches, width), bf16),
            sds((SLOTS, patches), f32),
            sds((SLOTS, patches), jnp.int32),
            sds((SLOTS, patches), jnp.int32),
            sds((4, SLOTS, 128), jnp.int32),
        ),
        in_specs=[vspec()] * 5,
        out_specs=[vspec()] * 5,
        compiler_params=params(),
        cost_estimate=cost(8e9, 4e6),
        name="prep",
    )(tokens, gain, router_t, ra_t, rm_t)


def one_hot(cm_row, rows):
    return cm_row == lax.broadcasted_iota(jnp.int32, (rows, cm_row.shape[1]), 0)


def group(first):
    return range(first, min(first + GROUP, EXPERTS))


def masks(heads):
    lane = lax.broadcasted_iota(jnp.int32, (1, WIDE), 1)
    return [(lane >= h * HDIM) & (lane < (h + 1) * HDIM) for h in range(heads)], lane


def assemble(chips, pieces, out, first, count):
    for i, piece in enumerate(pieces):
        rows = piece.shape[1]
        at = pl.multiple_of(chips[i] * rows, rows)
        out[first : first + count, pl.ds(at, rows), :] = piece[:count]


def attend_kernel(pieces, heads, meta, chips, x_ref, cm_ref, *rest):
    parts, values = rest[:pieces], rest[pieces : 2 * pieces]
    (o_ref, lse_ref, k_ref, v_ref, q_out, rows_out, weights_out,
     km, vt, wide, hots, got, q_ref, rows_ref, weights, sems) = rest[2 * pieces :]
    local = heads * HDIM
    assemble(chips, parts, weights, 0, SLOTS)
    assemble(chips, values, weights, SLOTS, 1)
    send_weights = pltpu.make_async_copy(weights, weights_out, sems.at[0])
    send_weights.start()
    x = x_ref[...]
    head_mask, _ = masks(heads)
    wide[...] = jnp.zeros(wide.shape, bf16)
    wide[:, :local] = weights[EXPERTS]
    k = nn(x, wide[...]).astype(bf16)
    wide[:, :local] = weights[EXPERTS + 1]
    v = nn(x, wide[...])
    k_ref[...] = k
    v_ref[...] = v.astype(bf16)
    v_t = v.T
    ones = jnp.ones((EXTRA, v_t.shape[1]), bf16)
    for h in range(heads):
        km[h] = jnp.where(head_mask[h], k.astype(f32), 0.0).astype(bf16)
        vt[h, :HDIM, :] = v_t[h * HDIM : (h + 1) * HDIM, :].astype(bf16)
        vt[h, HDIM:, :] = ones
    q_ref[...] = jnp.zeros(q_ref.shape, bf16)
    for at, first in enumerate(range(0, SLOTS, GROUP)):
        slot = at % 2
        count = len(group(first)) * CAP
        for i, e in enumerate(group(first)):
            hot = one_hot(cm_ref[e : e + 1, :], CAP)
            hots[slot, i * CAP : (i + 1) * CAP, :] = jnp.where(hot, 1.0, 0.0).astype(bf16)
        got[slot, :count, :] = nn(hots[slot, :count, :], x).astype(bf16)
        for i, e in enumerate(group(first)):
            off = pl.multiple_of(meta[0, e], PACK)
            rows = got[slot, i * CAP : (i + 1) * CAP, :]
            rows_ref[e] = rows.T
            q_ref[pl.ds(off, CAP), :local] = nn(rows, weights[e]).astype(bf16)
    send_q = pltpu.make_async_copy(q_ref, q_out, sems.at[1])
    send_rows = pltpu.make_async_copy(rows_ref, rows_out, sems.at[2])
    send_q.start()
    send_rows.start()
    tiles = (meta[0, EXPERTS] + (QT2 - 1)) // QT2

    def tile(i, carry):
        start = pl.multiple_of(i * QT2, QT2)
        q = q_ref[pl.ds(start, QT2), :]
        scores = [nt(km[h], q) for h in range(heads)]
        outs = []
        stats = []
        for h in range(heads):
            s = scores[h]
            top = jnp.max(s.reshape(8, s.shape[0] // 8, QT2), axis=0)
            top = jnp.max(top, axis=0, keepdims=True) * score_scale
            p = jnp.exp2(s * score_scale - top).astype(bf16)
            oh = nn(vt[h], p)
            total = oh[HDIM : HDIM + 1, :]
            outs.append(oh[:HDIM] * (1.0 / total))
            stats.append(top + jnp.log2(total))
        outs.append(jnp.zeros((WIDE - local, QT2), f32))
        stats.append(jnp.zeros((128 - heads, QT2), f32))
        o_ref[pl.ds(start, QT2), :] = jnp.concatenate(outs, axis=0).astype(bf16).T
        lse_ref[pl.ds(start, QT2), :] = jnp.concatenate(stats, axis=0).T
        return carry

    o_ref[...] = jnp.zeros(o_ref.shape, bf16)
    lax.fori_loop(0, tiles, tile, 0)
    send_weights.wait()
    send_q.wait()
    send_rows.wait()


def packed_rows(patches):
    return -(-(patches * TOP + EXPERTS * PACK + CAP) // QT2) * QT2


def whole(*shape):
    return pl.BlockSpec(shape, lambda *_: (0,) * len(shape))


def attend(meta, chips, x, cm, pieces):
    patches, width = x.shape
    _, part, local = pieces[0].shape
    count = SLOTS + 1
    heads = local // HDIM
    rows = packed_rows(patches)
    anywhere = pl.BlockSpec(memory_space=pl.ANY)
    return pl.pallas_call(
        functools.partial(attend_kernel, len(pieces), heads),
        out_shape=(
            sds((rows, WIDE), bf16),
            sds((rows, 128), f32),
            sds((patches, WIDE), bf16),
            sds((patches, WIDE), bf16),
            sds((rows, WIDE), bf16),
            sds((SLOTS, width, CAP), bf16),
            sds((count, width, local), bf16),
        ),
        grid_spec=pltpu.PrefetchScalarGridSpec(
            num_scalar_prefetch=2,
            grid=(1,),
            in_specs=[whole(patches, width), whole(SLOTS, patches)]
            + [whole(SLOTS, part, local) for _ in pieces]
            + [pl.BlockSpec((1, part, local), lambda *_: (2 * SLOTS - 1, 0, 0)) for _ in pieces],
            out_specs=[whole(rows, WIDE), whole(rows, 128), whole(patches, WIDE), whole(patches, WIDE)]
            + [anywhere] * 3,
            scratch_shapes=[
                pltpu.VMEM((heads, patches, WIDE), bf16),
                pltpu.VMEM((heads, HDIM + EXTRA, patches), bf16),
                pltpu.VMEM((width, WIDE), bf16),
                pltpu.VMEM((2, GROUP * CAP, patches), bf16),
                pltpu.VMEM((2, GROUP * CAP, width), bf16),
                pltpu.VMEM((rows, WIDE), bf16),
                pltpu.VMEM((SLOTS, width, CAP), bf16),
                pltpu.VMEM((count, width, local), bf16),
                pltpu.SemaphoreType.DMA((3,)),
            ],
        ),
        compiler_params=params(),
        cost_estimate=cost(30e9, 2e7),
        name="attend",
    )(meta, chips, x, cm, *pieces, *pieces)


def out_kernel(pieces, meta, chips, o_ref, cm_ref, gate_ref, *rest):
    parts = rest[:pieces]
    part_ref, weights_out, acc, outs, hots, wo_ref, sems = rest[pieces:]
    local = wo_ref.shape[2]
    assemble(chips, parts, wo_ref, 0, EXPERTS)
    wo_ref[EXPERTS] = jnp.zeros(wo_ref.shape[1:], bf16)
    send = pltpu.make_async_copy(wo_ref, weights_out, sems.at[0])
    send.start()
    for at, first in enumerate(range(0, SLOTS, GROUP)):
        slot = at % 2
        count = len(group(first)) * CAP
        for i, e in enumerate(group(first)):
            rows = slice(i * CAP, (i + 1) * CAP)
            off = pl.multiple_of(meta[0, e], PACK)
            mixed = o_ref[pl.ds(off, CAP), :local]
            outs[slot, :, rows] = nt(wo_ref[e], mixed).astype(bf16)
            hot = one_hot(cm_ref[e : e + 1, :], CAP)
            hots[slot, rows, :] = jnp.where(hot, gate_ref[e : e + 1, :], 0.0).astype(bf16)
        part = nn(outs[slot, :, :count], hots[slot, :count, :])
        if at == 0:
            acc[...] = part
        else:
            acc[...] += part
    part_ref[...] = acc[...].T.astype(bf16)
    send.wait()


def out_project(meta, chips, o, cm, gates, pieces):
    patches = cm.shape[1]
    _, rows, local = pieces[0].shape
    width = rows * len(pieces)
    anywhere = pl.BlockSpec(memory_space=pl.ANY)
    return pl.pallas_call(
        functools.partial(out_kernel, len(pieces)),
        out_shape=(sds((patches, width), bf16), sds((SLOTS, width, local), bf16)),
        grid_spec=pltpu.PrefetchScalarGridSpec(
            num_scalar_prefetch=2,
            grid=(1,),
            in_specs=[whole(*o.shape), whole(SLOTS, patches), whole(SLOTS, patches)]
            + [pl.BlockSpec((SLOTS, rows, local), lambda *_: (1, 0, 0)) for _ in pieces],
            out_specs=[whole(patches, width), anywhere],
            scratch_shapes=[
                pltpu.VMEM((width, patches), f32),
                pltpu.VMEM((2, width, GROUP * CAP), bf16),
                pltpu.VMEM((2, GROUP * CAP, patches), bf16),
                pltpu.VMEM((SLOTS, width, local), bf16),
                pltpu.SemaphoreType.DMA((1,)),
            ],
        ),
        compiler_params=params(),
        cost_estimate=cost(8e9, 8e6),
        name="out_project",
    )(meta, chips, o, cm, gates, *pieces)


def middle_kernel(tok_ref, mine_ref, other_ref, gain_ref, router_ref, cm_ref, grad_ref, mid_ref, x_ref, gate_ref):
    width = tok_ref.shape[1]
    middle = tok_ref[...].astype(f32) + (mine_ref[...].astype(f32) + other_ref[...].astype(f32))
    mid_ref[...] = middle
    xhat, _ = norm_stats(middle)
    normed = xhat * gain_ref[...]
    x_ref[:, :width] = normed.astype(bf16)
    x_ref[:, width:] = grad_ref[...]
    logits = lax.dot_general(
        router_ref[...], normed, (((1,), (1,)), ((), ())), precision=highest, preferred_element_type=f32
    )
    gate_ref[...] = dense_gates(logits, cm_ref[...] >= 0)


def middle_step(tokens, mine, other, gain, router_t, cm, masked):
    patches, width = tokens.shape
    return pl.pallas_call(
        middle_kernel,
        out_shape=(
            sds((patches, width), f32),
            sds((patches, 2 * width), bf16),
            sds((SLOTS, patches), f32),
        ),
        in_specs=[vspec()] * 7,
        out_specs=[vspec()] * 3,
        compiler_params=params(),
        cost_estimate=cost(4e9, 6e6),
        name="middle",
    )(tokens, mine, other, gain, router_t, cm, masked)


def gelu_parts(x):
    c = 0.7978845608028654
    square = x * x
    t = jnp.tanh(x * (c + (c * 0.044715) * square))
    half = 0.5 * (1.0 + t)
    slope = half + (0.5 * x) * (1.0 - t * t) * (c + (3.0 * c * 0.044715) * square)
    return x * half, slope


def feed_kernel(
    first, last, rows_of, meta, x_ref, cm_ref, gate_ref, up_ref, down_ref, *rest
):
    if first:
        acc_in, gg_in, keep_ref, send_ref, out_ref, back_ref, gg_ref, acc = rest
    else:
        keep_ref, send_ref, acc, gg_ref = rest
    step = pl.program_id(0)
    e = step + first
    width = x_ref.shape[1] // 2
    size = keep_ref.shape[2]

    @pl.when(step == 0)
    def _():
        acc[...] = acc_in[...] if first else jnp.zeros(acc.shape, f32)
        gg_ref[...] = gg_in[...] if first else jnp.zeros(gg_ref.shape, f32)

    def work(rows_n):
        eq = one_hot(cm_ref[pl.ds(e, 1), :], rows_n)
        hot = jnp.where(eq, 1.0, 0.0).astype(bf16)
        gsel = jnp.where(eq, gate_ref[pl.ds(e, 1), :], 0.0)
        grow = jnp.sum(gsel, axis=1, keepdims=True)
        up = up_ref[0]
        down = down_ref[0]
        got = nn(hot, x_ref[...])
        rows = got[:, :width].astype(bf16)
        grads = got[:, width:]
        hidden = nn(rows, up)
        raw = nn(grads.astype(bf16), down)
        act, slope = gelu_parts(hidden)
        acts = act.astype(bf16)
        outs = nt(down, acts).astype(bf16)
        grad_down = nn((grads * grow).astype(bf16).T, acts).astype(bf16)
        hidden_grad = (raw * grow * slope).astype(bf16)
        back = nt(up, hidden_grad).astype(bf16)
        grad_up = nn(rows.T, hidden_grad).astype(bf16)
        acc[:width] += nn(outs, gsel.astype(bf16))
        acc[width:] += nn(back, hot)
        gg = jnp.sum(raw * acts.astype(f32), axis=1, keepdims=True)
        gg_ref[pl.ds(e, 1), :] = jnp.sum(jnp.where(eq, gg, 0.0), axis=0, keepdims=True)

        @pl.when(meta[2, 0] == 0)
        def _():
            for i, at in enumerate(rows_of):
                keep_ref[i, 0] = grad_up[at : at + size]
                send_ref[i, 0] = grad_down[at : at + size]

        @pl.when(meta[2, 0] != 0)
        def _():
            for i, at in enumerate(rows_of):
                keep_ref[i, 0] = grad_down[at : at + size]
                send_ref[i, 0] = grad_up[at : at + size]

    few = meta[1, e] <= 256

    @pl.when(few)
    def _():
        work(256)

    @pl.when(jnp.logical_not(few))
    def _():
        work(CAP)

    if first:

        @pl.when(e == last - 1)
        def _():
            out_ref[...] = acc[:width].T.astype(bf16)
            back_ref[...] = acc[width:].T.astype(bf16)


def feed(meta, x, cm, gates, weights, rows_of, first, last, carry=()):
    patches, double = x.shape
    width = double // 2
    hidden = weights.shape[2]
    parts = len(rows_of)
    whole = lambda *shape: pl.BlockSpec(shape, lambda e, m: (0,) * len(shape))
    sums = sds((parts, last - first, width // parts, hidden), bf16)
    sums_spec = pl.BlockSpec((parts, 1, width // parts, hidden), lambda e, m: (0, e, 0, 0))
    total, total_spec = sds((double, patches), f32), whole(double, patches)
    gg, gg_spec = sds((SLOTS, patches), f32), whole(SLOTS, patches)
    part, part_spec = sds((patches, width), bf16), whole(patches, width)
    return pl.pallas_call(
        functools.partial(feed_kernel, first, last, rows_of),
        out_shape=(sums, sums, part, part, gg) if first else (sums, sums, total, gg),
        grid_spec=pltpu.PrefetchScalarGridSpec(
            num_scalar_prefetch=1,
            grid=(last - first,),
            in_specs=[
                whole(patches, double),
                whole(SLOTS, patches),
                whole(SLOTS, patches),
                pl.BlockSpec((1, width, hidden), lambda e, m: (e + first, 0, 0)),
                pl.BlockSpec((1, width, hidden), lambda e, m: (e + first + EXPERTS, 0, 0)),
            ]
            + ([total_spec, gg_spec] if first else []),
            out_specs=[sums_spec, sums_spec]
            + ([part_spec, part_spec, gg_spec] if first else [total_spec, gg_spec]),
            scratch_shapes=[pltpu.VMEM((double, patches), f32)] if first else [],
        ),
        compiler_params=params(),
        cost_estimate=cost(20e9, 2e7),
        name="feed",
    )(meta, x, cm, gates, weights, weights, *carry)


def both_kernel(ka_ref, ga_ref, kb_ref, gb_ref, out_ref):
    e = pl.program_id(0)

    @pl.when(e < SPLIT // BATCH)
    def _():
        out_ref[...] = (ka_ref[...].astype(f32) + ga_ref[...].astype(f32)).astype(bf16)

    @pl.when(e >= SPLIT // BATCH)
    def _():
        out_ref[...] = (kb_ref[...].astype(f32) + gb_ref[...].astype(f32)).astype(bf16)


def both_cores(keep_a, got_a, keep_b, got_b):
    parts, _, rows, hidden = keep_a.shape
    block = (parts, BATCH, rows, hidden)
    turn = SPLIT // BATCH
    early = pl.BlockSpec(block, lambda e: (0, jnp.minimum(e, turn - 1), 0, 0))
    late = pl.BlockSpec(block, lambda e: (0, jnp.maximum(e - turn, 0), 0, 0))
    return pl.pallas_call(
        both_kernel,
        out_shape=sds((parts, EXPERTS, rows, hidden), bf16),
        grid=(EXPERTS // BATCH,),
        in_specs=[early, early, late, late],
        out_specs=pl.BlockSpec(block, lambda e: (0, e, 0, 0)),
        compiler_params=params(),
        cost_estimate=cost(5e6, 3e7),
        name="both_cores",
    )(keep_a, got_a, keep_b, got_b)


def gate_back(gates, gg):
    return gates * (gg - jnp.sum(gates * gg, axis=0, keepdims=True))


def norm_back(xhat, inv, grad, gain):
    lifted = grad * gain
    first = jnp.mean(lifted, axis=-1, keepdims=True)
    second = jnp.mean(lifted * xhat, axis=-1, keepdims=True)
    return inv * (lifted - first - xhat * second)


def tn_high(a, b):
    return lax.dot_general(a, b, (((0,), (0,)), ((), ())), precision=highest, preferred_element_type=f32)


def second_back_kernel(
    mid_ref, mine_ref, other_ref, ggm_ref, ggo_ref, gate_ref, router_ref, gain_ref, masked_ref,
    mg_ref, mgb_ref, groute_ref, ggain_ref,
):
    xhat, inv = norm_stats(mid_ref[...])
    logit_grad = gate_back(gate_ref[...], ggm_ref[...] + ggo_ref[...])
    grad = (mine_ref[...].astype(f32) + other_ref[...].astype(f32)) + tn_high(logit_grad, router_ref[...])
    groute_ref[...] = jnp.dot(
        logit_grad, xhat * gain_ref[...], precision=highest, preferred_element_type=f32
    )
    ggain_ref[...] = jnp.sum(grad * xhat, axis=0, keepdims=True)
    middle_grad = masked_ref[...].astype(f32) + norm_back(xhat, inv, grad, gain_ref[...])
    mg_ref[...] = middle_grad
    mgb_ref[...] = middle_grad.astype(bf16)


def second_back(middle, mine, other, gg_mine, gg_other, gates, router_t, gain, masked):
    patches, width = middle.shape
    return pl.pallas_call(
        second_back_kernel,
        out_shape=(
            sds((patches, width), f32),
            sds((patches, width), bf16),
            sds((SLOTS, width), f32),
            sds((1, width), f32),
        ),
        in_specs=[vspec()] * 9,
        out_specs=[vspec()] * 4,
        compiler_params=params(),
        cost_estimate=cost(4e9, 8e6),
        name="second_back",
    )(middle, mine, other, gg_mine, gg_other, gates, router_t, gain, masked)


def out_back_kernel(meta, mg_ref, cm_ref, gate_ref, wo_ref, o_ref, do_ref, delta_ref, gg_ref, grad_ref, hots, got, raws, turned, wide):
    step = pl.program_id(0)
    local = wo_ref.shape[2]
    width = mg_ref.shape[1]

    @pl.when(step == 0)
    def _():
        do_ref[...] = jnp.zeros(do_ref.shape, bf16)
        delta_ref[...] = jnp.zeros(delta_ref.shape, f32)
        gg_ref[...] = jnp.zeros(gg_ref.shape, f32)
        wide[:, :width] = mg_ref[...]
        gate = gate_ref[...]
        high = gate.astype(bf16)
        rest = gate - high.astype(f32)
        mid = rest.astype(bf16)
        low = (rest - mid.astype(f32)).astype(bf16)
        blank = jnp.zeros((128 - 3 * SLOTS, gate.shape[1]), f32)
        stack = jnp.concatenate([high.astype(f32), mid.astype(f32), low.astype(f32), blank], axis=0)
        wide[:, width:] = stack.T.astype(bf16)

    for i in range(GROUP):
        hot = one_hot(cm_ref[pl.ds(step * GROUP + i, 1), :], CAP)
        hots[i * CAP : (i + 1) * CAP, :] = jnp.where(hot, 1.0, 0.0).astype(bf16)
    got[...] = nn(hots[...], wide[...])
    lane = lax.broadcasted_iota(jnp.int32, (1, local), 1)
    lane_s = lax.broadcasted_iota(jnp.int32, (1, 128), 1)
    for i in range(GROUP):
        rows = slice(i * CAP, (i + 1) * CAP)
        raws[rows, :] = nn(got[rows, :width].astype(bf16), wo_ref[i])
    for i in range(GROUP):
        e = step * GROUP + i
        rows = slice(i * CAP, (i + 1) * CAP)
        gates = got[rows, width:]
        grow = jnp.sum(jnp.where(lane_s % SLOTS == e, gates, 0.0), axis=1, keepdims=True)
        turned[:, rows] = (got[rows, :width] * grow).astype(bf16).T
        off = pl.multiple_of(meta[0, e], PACK)
        mixed_f = o_ref[pl.ds(off, CAP), :local].astype(f32)
        raw = raws[rows, :]
        gg = jnp.sum(raw * mixed_f, axis=1, keepdims=True)
        eq = one_hot(cm_ref[pl.ds(e, 1), :], CAP)
        gg_ref[pl.ds(e, 1), :] = jnp.sum(jnp.where(eq, gg, 0.0), axis=0, keepdims=True)
        mixed_grad = (raw * grow).astype(bf16)
        do_ref[pl.ds(off, CAP), :local] = mixed_grad
        weighed = mixed_grad.astype(f32) * mixed_f
        delta = jnp.zeros((CAP, 128), f32)
        for h in range(local // HDIM):
            here = (lane >= h * HDIM) & (lane < (h + 1) * HDIM)
            total = jnp.sum(jnp.where(here, weighed, 0.0), axis=1, keepdims=True)
            delta = jnp.where(lane_s == h, total, delta)
        delta_ref[pl.ds(off, CAP), :] = delta
    for i in range(GROUP):
        off = pl.multiple_of(meta[0, step * GROUP + i], PACK)
        grad_ref[i] = nn(turned[:, i * CAP : (i + 1) * CAP], o_ref[pl.ds(off, CAP), :local]).astype(bf16)


def out_back(meta, mg, cm, gates, weights, o):
    patches, width = mg.shape
    local = weights.shape[2]
    rows = o.shape[0]
    return pl.pallas_call(
        out_back_kernel,
        out_shape=(
            sds((rows, WIDE), bf16),
            sds((rows, 128), f32),
            sds((SLOTS, patches), f32),
            sds((SLOTS, width, local), bf16),
        ),
        grid_spec=pltpu.PrefetchScalarGridSpec(
            num_scalar_prefetch=1,
            grid=(SLOTS // GROUP,),
            in_specs=[
                pl.BlockSpec((patches, width), lambda e, m: (0, 0)),
                pl.BlockSpec((SLOTS, patches), lambda e, m: (0, 0)),
                pl.BlockSpec((SLOTS, patches), lambda e, m: (0, 0)),
                pl.BlockSpec((GROUP, width, local), lambda e, m: (e, 0, 0)),
                pl.BlockSpec((rows, WIDE), lambda e, m: (0, 0)),
            ],
            out_specs=[
                pl.BlockSpec((rows, WIDE), lambda e, m: (0, 0)),
                pl.BlockSpec((rows, 128), lambda e, m: (0, 0)),
                pl.BlockSpec((SLOTS, patches), lambda e, m: (0, 0)),
                pl.BlockSpec((GROUP, width, local), lambda e, m: (e, 0, 0)),
            ],
            scratch_shapes=[
                pltpu.VMEM((GROUP * CAP, patches), bf16),
                pltpu.VMEM((GROUP * CAP, width + 128), f32),
                pltpu.VMEM((GROUP * CAP, local), f32),
                pltpu.VMEM((width, GROUP * CAP), bf16),
                pltpu.VMEM((patches, width + 128), bf16),
            ],
        ),
        compiler_params=params(),
        cost_estimate=cost(10e9, 2e7),
        name="out_back",
    )(meta, mg, cm, gates, weights, o)


def attend_back_kernel(
    meta, q_ref, do_ref, lse_ref, delta_ref, k_ref, v_ref, dq_ref, dk_ref, dv_ref, km, kt, vt, dk, dv
):
    heads = km.shape[0]
    head_mask, _ = masks(heads)
    k = k_ref[...].astype(f32)
    k_t = k.T
    v_t = v_ref[...].astype(f32).T
    row = lax.broadcasted_iota(jnp.int32, (WIDE, 1), 0)
    for h in range(heads):
        here = (row >= h * HDIM) & (row < (h + 1) * HDIM)
        km[h] = jnp.where(head_mask[h], k, 0.0).astype(bf16)
        kt[h] = jnp.where(here, k_t, 0.0).astype(bf16)
        vt[h] = jnp.where(here, v_t, 0.0).astype(bf16)
    dk[...] = jnp.zeros(dk.shape, f32)
    dv[...] = jnp.zeros(dv.shape, f32)
    dq_ref[...] = jnp.zeros(dq_ref.shape, bf16)
    tiles = (meta[0, EXPERTS] + (QT - 1)) // QT

    def tile(i, carry):
        start = pl.multiple_of(i * QT, QT)
        q = q_ref[pl.ds(start, QT), :]
        do = do_ref[pl.ds(start, QT), :]
        lse = lse_ref[pl.ds(start, QT), :]
        delta = delta_ref[pl.ds(start, QT), :]
        q_t = q.T
        do_t = do.T
        dq = jnp.zeros((QT, WIDE), f32)
        pairs = [(nn(q, kt[0]), nn(do, vt[0]))]
        for h in range(heads):
            at = slice(h * HDIM, (h + 1) * HDIM)
            if h + 1 < heads:
                pairs.append((nn(q, kt[h + 1]), nn(do, vt[h + 1])))
            s, dp = pairs[h]
            p = jnp.exp2(s * score_scale - lse[:, h : h + 1])
            ds = (p * (dp - delta[:, h : h + 1])).astype(bf16)
            dq = dq + nn(ds, km[h])
            dk[at, :] += nn(q_t[at, :], ds)
            dv[at, :] += nn(do_t[at, :], p.astype(bf16))
        dq_ref[pl.ds(start, QT), :] = (dq * 0.125).astype(bf16)
        return carry

    lax.fori_loop(0, tiles, tile, 0)
    dk_ref[...] = (dk[...] * 0.125).astype(bf16)
    dv_ref[...] = dv[...].astype(bf16)


def attend_back(meta, q, do, lse, delta, k, v, heads):
    rows = q.shape[0]
    patches = k.shape[0]
    return pl.pallas_call(
        attend_back_kernel,
        out_shape=(
            sds((rows, WIDE), bf16),
            sds((heads * HDIM, patches), bf16),
            sds((heads * HDIM, patches), bf16),
        ),
        in_specs=[pl.BlockSpec(memory_space=pltpu.SMEM)] + [vspec()] * 6,
        out_specs=[vspec()] * 3,
        scratch_shapes=[
            pltpu.VMEM((heads, patches, WIDE), bf16),
            pltpu.VMEM((heads, WIDE, patches), bf16),
            pltpu.VMEM((heads, WIDE, patches), bf16),
            pltpu.VMEM((heads * HDIM, patches), f32),
            pltpu.VMEM((heads * HDIM, patches), f32),
        ],
        compiler_params=params(),
        cost_estimate=cost(60e9, 2e7),
        name="attend_back",
    )(meta, q, do, lse, delta, k, v)


def in_back_kernel(
    rows_of, meta, dq_ref, dk_ref, dv_ref, rows_ref, x_ref, cm_ref, wq_ref, wv_ref, go_ref,
    keep_ref, send_ref, part_ref, acc, got, outs, hots,
):
    step = pl.program_id(0)
    local = wq_ref.shape[2]
    size = keep_ref.shape[2]

    def put(at, first, second):
        for i, row in enumerate(rows_of):
            keep_ref[i, at] = first[row : row + size]
            send_ref[i, at] = second[row : row + size]

    @pl.when(step == 0)
    def _():
        acc[...] = jnp.zeros(acc.shape, f32)

    for i in range(GROUP):
        e = step * GROUP + i
        rows = slice(i * CAP, (i + 1) * CAP)
        hot = one_hot(cm_ref[pl.ds(e, 1), :], CAP)
        hots[rows, :] = jnp.where(hot, 1.0, 0.0).astype(bf16)
        off = pl.multiple_of(meta[0, e], PACK)
        dq = dq_ref[pl.ds(off, CAP), :local]
        outs[:, rows] = nt(wq_ref[i], dq).astype(bf16)
        got[0, i] = nn(rows_ref[i], dq).astype(bf16)
        got[1, i] = go_ref[i]
    acc[...] += nn(outs[...], hots[...])

    @pl.when(step == SLOTS // GROUP - 1)
    def _():
        dk = dk_ref[...]
        dv = dv_ref[...]
        last = GROUP - 1
        acc[...] += nn(wq_ref[last], dk) + nn(wv_ref[0], dv)
        part_ref[...] = acc[...].T.astype(bf16)
        x = x_ref[...]
        got[0, last] = nn(dk, x).T.astype(bf16)
        got[1, last] = nn(dv, x).T.astype(bf16)

    @pl.when(meta[2, 0] == 0)
    def _():
        for i in range(GROUP):
            put(i, got[0, i], got[1, i])

    @pl.when(meta[2, 0] != 0)
    def _():
        for i in range(GROUP):
            put(i, got[1, i], got[0, i])


def in_back(meta, dq, dk, dv, rows_att, x, cm, weights, grad_out, rows_of):
    patches, width = x.shape
    local = weights.shape[2]
    rows = dq.shape[0]
    parts = len(rows_of)
    sums = sds((parts, SLOTS, width // parts, local), bf16)
    sums_spec = pl.BlockSpec((parts, GROUP, width // parts, local), lambda e, m: (0, e, 0, 0))
    return pl.pallas_call(
        functools.partial(in_back_kernel, rows_of),
        out_shape=(sums, sums, sds((patches, width), bf16)),
        grid_spec=pltpu.PrefetchScalarGridSpec(
            num_scalar_prefetch=1,
            grid=(SLOTS // GROUP,),
            in_specs=[
                pl.BlockSpec((rows, WIDE), lambda e, m: (0, 0)),
                pl.BlockSpec((local, patches), lambda e, m: (0, 0)),
                pl.BlockSpec((local, patches), lambda e, m: (0, 0)),
                pl.BlockSpec((GROUP, width, CAP), lambda e, m: (e, 0, 0)),
                pl.BlockSpec((patches, width), lambda e, m: (0, 0)),
                pl.BlockSpec((SLOTS, patches), lambda e, m: (0, 0)),
                pl.BlockSpec((GROUP, width, local), lambda e, m: (e, 0, 0)),
                pl.BlockSpec((1, width, local), lambda e, m: (EXPERTS + 1, 0, 0)),
                pl.BlockSpec((GROUP, width, local), lambda e, m: (e, 0, 0)),
            ],
            out_specs=[sums_spec, sums_spec, pl.BlockSpec((patches, width), lambda e, m: (0, 0))],
            scratch_shapes=[
                pltpu.VMEM((width, patches), f32),
                pltpu.VMEM((2, GROUP, width, local), bf16),
                pltpu.VMEM((width, GROUP * CAP), bf16),
                pltpu.VMEM((GROUP * CAP, patches), bf16),
            ],
        ),
        compiler_params=params(),
        cost_estimate=cost(10e9, 2e7),
        name="in_back",
    )(meta, dq, dk, dv, rows_att, x, cm, weights, weights, grad_out)


def route_back_kernel(tok_ref, ggm_ref, ggo_ref, gate_ref, gain_ref, router_ref, lg_ref, groute_ref, ggain_ref):
    xhat, _ = norm_stats(tok_ref[...].astype(f32))
    logit_grad = gate_back(gate_ref[...], ggm_ref[...] + ggo_ref[...])
    lg_ref[...] = logit_grad
    plain = jnp.dot(logit_grad, xhat, precision=highest, preferred_element_type=f32)
    groute_ref[...] = plain * gain_ref[...]
    ggain_ref[...] = 0.5 * jnp.sum(plain * router_ref[...], axis=0, keepdims=True)


def route_back(tokens, gg_mine, gg_other, gates, gain, router_t):
    patches, width = tokens.shape
    return pl.pallas_call(
        route_back_kernel,
        out_shape=(sds((SLOTS, patches), f32), sds((SLOTS, width), f32), sds((1, width), f32)),
        in_specs=[vspec()] * 6,
        out_specs=[vspec()] * 3,
        compiler_params=params(),
        cost_estimate=cost(3e9, 2e6),
        name="route_back",
    )(tokens, gg_mine, gg_other, gates, gain, router_t)


def first_gain_kernel(tok_ref, mine_ref, part_ref, ggain_ref):
    xhat, _ = norm_stats(tok_ref[...].astype(f32))
    ggain_ref[...] = part_ref[...] + jnp.sum(mine_ref[...].astype(f32) * xhat, axis=0, keepdims=True)


def first_gain(tokens, mine, part):
    return pl.pallas_call(
        first_gain_kernel,
        out_shape=sds(part.shape, f32),
        in_specs=[vspec()] * 3,
        out_specs=vspec(),
        compiler_params=params(),
        cost_estimate=cost(3e9, 3e6),
        name="first_gain",
    )(tokens, mine, part)


def first_back_kernel(tok_ref, mine_ref, other_ref, lg_ref, router_ref, gain_ref, mg_ref, gt_ref):
    xhat, inv = norm_stats(tok_ref[...].astype(f32))
    grad = (mine_ref[...].astype(f32) + other_ref[...].astype(f32)) + tn_high(lg_ref[...], router_ref[...])
    gt_ref[...] = mg_ref[...] + norm_back(xhat, inv, grad, gain_ref[...])


def first_back(tokens, mine, other, logit_grad, router_t, gain, middle_grad):
    patches, width = tokens.shape
    return pl.pallas_call(
        first_back_kernel,
        out_shape=sds((patches, width), f32),
        in_specs=[vspec()] * 7,
        out_specs=vspec(),
        compiler_params=params(),
        cost_estimate=cost(3e9, 6e6),
        name="first_back",
    )(tokens, mine, other, logit_grad, router_t, gain, middle_grad)


def tie(*values):
    return lax.optimization_barrier(values)


def after(value, first):
    return lax.optimization_barrier((value, first))[0]


def other_half(x):
    return lax.ppermute(x, "mp", [(0, 1), (1, 0)])


def cube_steps(size):
    steps = []
    step = 1
    while step < size:
        steps.append(step)
        step *= 2
    return steps


def wait_for(x, marks, at):
    return after(x, marks[at]) if 0 <= at < len(marks) else x


def cube_gather(x, size, marks):
    index = lax.axis_index("dp")
    x = x[None]
    for at, step in enumerate(cube_steps(size)):
        x = wait_for(x, marks, at - 1)
        got = lax.ppermute(x, "dp", [(i, i ^ step) for i in range(size)])
        upper = (index // step) % 2 == 1
        x = jnp.where(
            upper, jnp.concatenate([got, x], axis=0), jnp.concatenate([x, got], axis=0)
        )
    return x


class Ring:
    def __init__(self, size):
        self.size = size
        self.chips = size // 2
        half = self.chips // 2
        self.order = [2 * i for i in range(half)] + [2 * i + 1 for i in reversed(range(half))]
        self.groups = [[2 * chip + core for chip in self.order] for core in range(2)]
        self.next = []
        for at, chip in enumerate(self.order):
            self.next.append((2 * chip, 2 * self.order[(at + 1) % self.chips]))
            self.next.append((2 * chip + 1, 2 * self.order[at - 1] + 1))
        self.back = [(b, a) for a, b in self.next]
        self.swap = [(i, i ^ 1) for i in range(size)]
        index = lax.axis_index("dp")
        self.core = index % 2
        chip = index // 2
        place = jnp.where(chip % 2 == 0, chip // 2, self.chips - 1 - chip // 2)
        self.place = jnp.where(self.core == 0, place, self.chips - place)

    def chip(self, place):
        place = jnp.where(self.core == 0, place, -place) % self.chips
        return jnp.where(place < self.chips // 2, 2 * place, 2 * (self.chips - 1 - place) + 1)

    def cross(self, x):
        return lax.ppermute(x, "dp", self.swap)

    def step(self, x):
        return lax.ppermute(x, "dp", self.next)

    def chip_rows(self, shard, got):
        first = jnp.where(self.core == 0, shard, got)
        second = jnp.where(self.core == 0, got, shard)
        return jnp.concatenate([first, second], axis=1)

    def sources(self):
        places = [self.place]
        for step in range(1, self.chips // 2 + 1):
            places.append(self.place - step)
            if step < self.chips // 2:
                places.append(self.place + step)
        return jnp.stack([self.chip(p) for p in places]).astype(jnp.int32)

    def before(self, keep, got):
        return (keep.astype(f32) + got.astype(f32)).astype(bf16)

    def finish(self, total):
        count, rows, columns = total.shape
        total = total.reshape(count, 2, rows // 2, columns)
        mine = lax.dynamic_index_in_dim(total, self.core, 1, keepdims=False)
        theirs = lax.dynamic_index_in_dim(total, 1 - self.core, 1, keepdims=False)
        theirs = self.cross(theirs)
        first = jnp.where(self.core == 0, mine, theirs).astype(f32)
        second = jnp.where(self.core == 0, theirs, mine).astype(f32)
        return first, second

    def offload(self, total):
        return lax.psum_scatter(
            total, "dp", scatter_dimension=0, tiled=True, axis_index_groups=self.groups
        )[0]

    def scatter_start(self, keep, got):
        def own(place):
            place = jnp.where(self.core == 0, place, -place) % self.chips
            pick = lambda g: lax.dynamic_index_in_dim(g, place, 0, keepdims=False).astype(f32)
            return pick(keep) + pick(got)

        half = self.chips // 2
        return own(self.place + half).astype(bf16), own(self.place - half + 1).astype(bf16), own

    def scatter(self, far, near, own):
        half = self.chips // 2
        marks = [far]
        for step in range(1, half):
            far = self.step(far)
            near = lax.ppermute(near, "dp", self.back)
            far = (far.astype(f32) + own(self.place + half - step)).astype(bf16)
            if step < half - 1:
                near = (near.astype(f32) + own(self.place - half + 1 + step)).astype(bf16)
            marks.append(far)
        far = self.step(far)
        return (far.astype(f32) + (near.astype(f32) + own(self.place))).astype(bf16), marks


def body(dp_size, tokens, cotangent, task_ids, att_routes, mlp_routes, valid, gain_one, w_query, w_key,
         w_value, w_out, router_att, gain_two, w_up, w_down, router_mlp):
    tokens = tokens[0]
    patches, width = tokens.shape
    local = w_key.shape[1]
    heads = local // HDIM
    tasks = router_att.shape[0]

    att_shard = jnp.concatenate([w_query, w_key[None], jnp.swapaxes(w_out, 1, 2), w_value[None]], axis=0)
    feed_shard = jnp.concatenate([w_up, jnp.swapaxes(w_down, 1, 2)], axis=0)
    ring = Ring(dp_size) if dp_size == 16 else None
    if ring is None:
        chips = jnp.zeros((1,), jnp.int32)
        pieces = [lax.all_gather(att_shard, "dp", axis=1, tiled=True)]
    else:
        chips = ring.sources()
        piece = ring.chip_rows(att_shard, ring.cross(att_shard))
        pieces = [piece]
        for step in range(1, ring.chips // 2 + 1):
            piece = ring.step(piece)
            pieces.append(piece)
            if step < ring.chips // 2:
                pieces.append(ring.cross(piece))
            if step == HOLD:
                feed_shard = after(feed_shard, piece)
    feed_full = lax.all_gather(feed_shard, "dp", axis=1, tiled=True)

    gain_1 = gain_one[None]
    gain_2 = gain_two[None]
    task = task_ids[0]
    pick = lambda router: jnp.pad(
        lax.dynamic_index_in_dim(router, task, 0, keepdims=False).T, ((0, SLOTS - EXPERTS), (0, 0))
    )
    route_1 = pick(router_att)
    route_2 = pick(router_mlp)
    masked = cotangent[0] * valid[0][:, None].astype(bf16)

    x_one, gates_1, cm_1, cm_2, meta = prep(tokens, gain_1, route_1, att_routes[0].T, mlp_routes[0].T)
    core = jnp.full((1, SLOTS), 0 if ring is None else ring.core, jnp.int32)
    meta_1 = jnp.concatenate([meta[0:2, :, 0], core], axis=0)
    meta_2 = jnp.concatenate([meta[2:4, :, 0], core], axis=0)

    o, lse, k, v, q, rows_att, in_full = attend(meta_1, chips, x_one, cm_1, pieces)
    part, out_full = out_project(meta_1, chips, o, cm_1, gates_1, pieces)
    middle, x_two, gates_2 = middle_step(tokens, part, other_half(part), gain_2, route_2, cm_2, masked)
    rows_of = [0] if ring is None else [chip * (width // ring.chips) for chip in ring.order]
    keep_a, send_a, total, gg_2 = feed(meta_2, x_two, cm_2, gates_2, feed_full, rows_of, 0, SPLIT)
    keep_b, send_b, part_two, back_two, gg_2 = feed(
        meta_2, x_two, cm_2, gates_2, feed_full, rows_of, SPLIT, EXPERTS, (total, gg_2)
    )
    back_two_other, gg_2_other = other_half(back_two), other_half(gg_2)
    if ring is not None:
        feed_sum = both_cores(keep_a, ring.cross(send_a), keep_b, ring.cross(send_b))
        middle_here = after(middle, feed_sum)
    else:
        middle_here = middle
    middle_grad, mg, groute_2, ggain_2 = second_back(
        middle_here, back_two, back_two_other, gg_2, gg_2_other, gates_2, route_2, gain_2, masked
    )
    if ring is not None:
        feed_sum = ring.offload(after(feed_sum, mg))
    part_other = other_half(after(part_two, mg))
    layer_out = (middle + (part_two.astype(f32) + part_other.astype(f32))).astype(bf16)
    do, delta, gg_1, grad_out = out_back(meta_1, mg, cm_1, gates_1, out_full, o)
    gg_other = other_half(gg_1)
    dq, dk, dv = attend_back(meta_1, q, do, lse, delta, k, v, heads)
    dq, gg_other = tie(dq, gg_other)
    logit_grad, groute_1, ggain_1 = route_back(tokens, gg_1, gg_other, gates_1, gain_1, route_1)
    mark = (jnp.arange(width) == task).astype(f32)[None]
    small = jnp.concatenate([groute_1[:EXPERTS], mark, groute_2[:EXPERTS], ggain_2], axis=0).astype(bf16)
    dq, small, ggain_1 = tie(dq, small, ggain_1)
    keep_att, send_att, back_one = in_back(
        meta_1, dq, dk, dv, rows_att, x_one, cm_1, in_full, grad_out, rows_of
    )
    back_other = other_half(back_one)
    ggain_1 = first_gain(tokens, back_one, ggain_1)
    small = jnp.concatenate([small, ggain_1.astype(bf16)], axis=0)
    if ring is None:
        marks = []
        scatter = lambda g: lax.psum_scatter(g[0], "dp", scatter_dimension=1, tiled=True).astype(f32)
        q_mine, o_mine = scatter(keep_att), scatter(send_att)
        up_mine = scatter(jnp.concatenate([keep_a, keep_b], axis=1))
        down_mine = scatter(jnp.concatenate([send_a, send_b], axis=1))
    else:
        far, near, add = ring.scatter_start(keep_att, after(ring.cross(send_att), ggain_1))
        att_sum, marks = ring.scatter(far, near, add)
        middle_grad = after(middle_grad, marks[3])
        q_mine, o_mine = ring.finish(att_sum)
        up_mine, down_mine = ring.finish(feed_sum)
    grad_tokens = first_back(
        tokens, back_one, back_other, logit_grad, route_1, gain_1, middle_grad
    )

    every = cube_gather(small, dp_size, marks[:3]).astype(f32)
    named = every[:, EXPERTS, :tasks]
    route_sum = lambda g: jnp.swapaxes(
        jnp.einsum("it,ied->ted", named, g, precision=highest, preferred_element_type=f32), 1, 2
    )
    grad_router_att = route_sum(every[:, :EXPERTS])
    grad_router_mlp = route_sum(every[:, SLOTS : SLOTS + EXPERTS])
    gains = jnp.sum(every[:, 2 * SLOTS - 1 :], axis=0)
    grad_gain_two = gains[0]
    grad_gain_one = gains[1] + other_half(gains[1:])[0]
    return (
        layer_out[None],
        grad_tokens[None],
        grad_gain_one,
        q_mine[:EXPERTS],
        q_mine[EXPERTS],
        o_mine[EXPERTS],
        jnp.swapaxes(o_mine[:EXPERTS], 1, 2),
        grad_router_att,
        grad_gain_two,
        up_mine,
        jnp.swapaxes(down_mine, 1, 2),
        grad_router_mlp,
    )


def solution(mesh):
    dp_size = mesh.shape["dp"]

    def run(*args):
        return body(dp_size, *args)

    return jax.shard_map(
        run,
        mesh=mesh,
        in_specs=(
            P("dp", None, None), P("dp", None, None), P("dp"), P("dp", None, None), P("dp", None, None),
            P("dp", None), P(), P(None, "dp", "mp"), P("dp", "mp"), P("dp", "mp"), P(None, "mp", "dp"),
            P(), P(), P(None, "dp", "mp"), P(None, "mp", "dp"), P(),
        ),
        out_specs=(
            P("dp", None, None), P("dp", None, None), P(), P(None, "dp", "mp"), P("dp", "mp"), P("dp", "mp"),
            P(None, "mp", "dp"), P(), P(), P(None, "dp", "mp"), P(None, "mp", "dp"), P(),
        ),
        check_vma=False,
    )
```

```python
import functools

import jax
import jax.numpy as jnp
from jax import lax
from jax.experimental import pallas as pl
from jax.experimental.pallas import tpu as pltpu
from jax.sharding import PartitionSpec as P

HDIM = 64
EXPERTS = 15
SLOTS = 16
TOP = 4
CAP = 384
PACK = 16
QT = 256
WIDE = 256
HOLD = 3
SPLIT = 9
BATCH = 3
GROUP = 4
QT2 = 512
EXTRA = 16

norm_eps = 1e-06
f32 = jnp.float32
bf16 = jnp.bfloat16
highest = lax.Precision.HIGHEST
log2e = 1.4426950408889634
score_scale = 0.125 * log2e
vmem_bytes = 60 * 1024 * 1024


def nn(a, b):
    return jnp.dot(a, b, preferred_element_type=f32)


def nt(a, b):
    return lax.dot_general(a, b, (((1,), (1,)), ((), ())), preferred_element_type=f32)


def params(limit=vmem_bytes):
    return pltpu.CompilerParams(vmem_limit_bytes=limit)


def cost(flops, moved):
    return pl.CostEstimate(flops=int(flops), bytes_accessed=int(moved), transcendentals=0)


def vspec():
    return pl.BlockSpec(memory_space=pltpu.VMEM)


def sds(shape, dtype):
    return jax.ShapeDtypeStruct(shape, dtype)


def norm_stats(x):
    centre = jnp.mean(x, axis=-1, keepdims=True)
    shifted = x - centre
    spread = jnp.mean(shifted * shifted, axis=-1, keepdims=True)
    inv = lax.rsqrt(spread + norm_eps)
    return shifted * inv, inv


def dense_gates(logits, chosen):
    top = jnp.max(jnp.where(chosen, logits, -jnp.inf), axis=0, keepdims=True)
    lifted = jnp.where(chosen, jnp.exp(logits - top), 0.0)
    return lifted / jnp.sum(lifted, axis=0, keepdims=True)


def prep_kernel(tok_ref, gain_ref, router_ref, ra_ref, rm_ref, x_ref, gate_ref, cma_ref, cmm_ref, meta_ref):
    patches = tok_ref.shape[0]
    xhat, _ = norm_stats(tok_ref[...].astype(f32))
    normed = xhat * gain_ref[...]
    x_ref[...] = normed.astype(bf16)
    ids = lax.broadcasted_iota(jnp.int32, (SLOTS, patches), 0)
    before = (
        lax.broadcasted_iota(jnp.int32, (patches, patches), 0)
        < lax.broadcasted_iota(jnp.int32, (patches, patches), 1)
    )
    tri = jnp.where(before, 1.0, 0.0).astype(bf16)
    small = lax.broadcasted_iota(jnp.int32, (SLOTS, SLOTS), 1) < lax.broadcasted_iota(
        jnp.int32, (SLOTS, SLOTS), 0
    )
    lower = jnp.where(small, 1.0, 0.0)
    for routes, cm_ref, at in ((ra_ref, cma_ref, 0), (rm_ref, cmm_ref, 2)):
        named = jnp.zeros((SLOTS, patches), f32)
        for k in range(TOP):
            named = named + jnp.where(routes[k : k + 1, :] == ids, 1.0, 0.0)
        ranks = nn(named.astype(bf16), tri)
        cm_ref[...] = jnp.where(named > 0.0, ranks, -1.0).astype(jnp.int32)
        count = jnp.sum(named, axis=1, keepdims=True)
        packed = jnp.ceil(count * (1.0 / PACK)) * PACK
        packed = jnp.broadcast_to(packed, (SLOTS, 128))
        offs = jnp.dot(lower, packed, precision=highest, preferred_element_type=f32)
        meta_ref[at] = offs.astype(jnp.int32)
        meta_ref[at + 1] = jnp.broadcast_to(count, (SLOTS, 128)).astype(jnp.int32)
    logits = lax.dot_general(
        router_ref[...], normed, (((1,), (1,)), ((), ())), precision=highest, preferred_element_type=f32
    )
    gate_ref[...] = dense_gates(logits, cma_ref[...] >= 0)


def prep(tokens, gain, router_t, ra_t, rm_t):
    patches, width = tokens.shape
    return pl.pallas_call(
        prep_kernel,
        out_shape=(
            sds((patches, width), bf16),
            sds((SLOTS, patches), f32),
            sds((SLOTS, patches), jnp.int32),
            sds((SLOTS, patches), jnp.int32),
            sds((4, SLOTS, 128), jnp.int32),
        ),
        in_specs=[vspec()] * 5,
        out_specs=[vspec()] * 5,
        compiler_params=params(),
        cost_estimate=cost(8e9, 4e6),
        name="prep",
    )(tokens, gain, router_t, ra_t, rm_t)


def one_hot(cm_row, rows):
    return cm_row == lax.broadcasted_iota(jnp.int32, (rows, cm_row.shape[1]), 0)


def group(first):
    return range(first, min(first + GROUP, EXPERTS))


def masks(heads):
    lane = lax.broadcasted_iota(jnp.int32, (1, WIDE), 1)
    return [(lane >= h * HDIM) & (lane < (h + 1) * HDIM) for h in range(heads)], lane


def assemble(chips, pieces, out, first, count):
    for i, piece in enumerate(pieces):
        rows = piece.shape[1]
        at = pl.multiple_of(chips[i] * rows, rows)
        out[first : first + count, pl.ds(at, rows), :] = piece[:count]


def attend_kernel(pieces, heads, meta, chips, x_ref, cm_ref, *rest):
    parts, values = rest[:pieces], rest[pieces : 2 * pieces]
    (o_ref, lse_ref, k_ref, v_ref, q_out, rows_out, weights_out,
     km, vt, wide, hots, got, q_ref, rows_ref, weights, sems) = rest[2 * pieces :]
    local = heads * HDIM
    assemble(chips, parts, weights, 0, SLOTS)
    assemble(chips, values, weights, SLOTS, 1)
    send_weights = pltpu.make_async_copy(weights, weights_out, sems.at[0])
    send_weights.start()
    x = x_ref[...]
    head_mask, _ = masks(heads)
    wide[...] = jnp.zeros(wide.shape, bf16)
    wide[:, :local] = weights[EXPERTS]
    k = nn(x, wide[...]).astype(bf16)
    wide[:, :local] = weights[EXPERTS + 1]
    v = nn(x, wide[...])
    k_ref[...] = k
    v_ref[...] = v.astype(bf16)
    v_t = v.T
    ones = jnp.ones((EXTRA, v_t.shape[1]), bf16)
    for h in range(heads):
        km[h] = jnp.where(head_mask[h], k.astype(f32), 0.0).astype(bf16)
        vt[h, :HDIM, :] = v_t[h * HDIM : (h + 1) * HDIM, :].astype(bf16)
        vt[h, HDIM:, :] = ones
    q_ref[...] = jnp.zeros(q_ref.shape, bf16)
    for at, first in enumerate(range(0, SLOTS, GROUP)):
        slot = at % 2
        count = len(group(first)) * CAP
        for i, e in enumerate(group(first)):
            hot = one_hot(cm_ref[e : e + 1, :], CAP)
            hots[slot, i * CAP : (i + 1) * CAP, :] = jnp.where(hot, 1.0, 0.0).astype(bf16)
        got[slot, :count, :] = nn(hots[slot, :count, :], x).astype(bf16)
        for i, e in enumerate(group(first)):
            off = pl.multiple_of(meta[0, e], PACK)
            rows = got[slot, i * CAP : (i + 1) * CAP, :]
            rows_ref[e] = rows.T
            q_ref[pl.ds(off, CAP), :local] = nn(rows, weights[e]).astype(bf16)
    send_q = pltpu.make_async_copy(q_ref, q_out, sems.at[1])
    send_rows = pltpu.make_async_copy(rows_ref, rows_out, sems.at[2])
    send_q.start()
    send_rows.start()
    tiles = (meta[0, EXPERTS] + (QT2 - 1)) // QT2

    def tile(i, carry):
        start = pl.multiple_of(i * QT2, QT2)
        q = q_ref[pl.ds(start, QT2), :]
        scores = [nt(km[h], q) for h in range(heads)]
        outs = []
        stats = []
        for h in range(heads):
            s = scores[h]
            top = jnp.max(s.reshape(8, s.shape[0] // 8, QT2), axis=0)
            top = jnp.max(top, axis=0, keepdims=True) * score_scale
            p = jnp.exp2(s * score_scale - top).astype(bf16)
            oh = nn(vt[h], p)
            total = oh[HDIM : HDIM + 1, :]
            outs.append(oh[:HDIM] * (1.0 / total))
            stats.append(top + jnp.log2(total))
        outs.append(jnp.zeros((WIDE - local, QT2), f32))
        stats.append(jnp.zeros((128 - heads, QT2), f32))
        o_ref[pl.ds(start, QT2), :] = jnp.concatenate(outs, axis=0).astype(bf16).T
        lse_ref[pl.ds(start, QT2), :] = jnp.concatenate(stats, axis=0).T
        return carry

    o_ref[...] = jnp.zeros(o_ref.shape, bf16)
    lax.fori_loop(0, tiles, tile, 0)
    send_weights.wait()
    send_q.wait()
    send_rows.wait()


def packed_rows(patches):
    return -(-(patches * TOP + EXPERTS * PACK + CAP) // QT2) * QT2


def whole(*shape):
    return pl.BlockSpec(shape, lambda *_: (0,) * len(shape))


def attend(meta, chips, x, cm, pieces):
    patches, width = x.shape
    _, part, local = pieces[0].shape
    count = SLOTS + 1
    heads = local // HDIM
    rows = packed_rows(patches)
    anywhere = pl.BlockSpec(memory_space=pl.ANY)
    return pl.pallas_call(
        functools.partial(attend_kernel, len(pieces), heads),
        out_shape=(
            sds((rows, WIDE), bf16),
            sds((rows, 128), f32),
            sds((patches, WIDE), bf16),
            sds((patches, WIDE), bf16),
            sds((rows, WIDE), bf16),
            sds((SLOTS, width, CAP), bf16),
            sds((count, width, local), bf16),
        ),
        grid_spec=pltpu.PrefetchScalarGridSpec(
            num_scalar_prefetch=2,
            grid=(1,),
            in_specs=[whole(patches, width), whole(SLOTS, patches)]
            + [whole(SLOTS, part, local) for _ in pieces]
            + [pl.BlockSpec((1, part, local), lambda *_: (2 * SLOTS - 1, 0, 0)) for _ in pieces],
            out_specs=[whole(rows, WIDE), whole(rows, 128), whole(patches, WIDE), whole(patches, WIDE)]
            + [anywhere] * 3,
            scratch_shapes=[
                pltpu.VMEM((heads, patches, WIDE), bf16),
                pltpu.VMEM((heads, HDIM + EXTRA, patches), bf16),
                pltpu.VMEM((width, WIDE), bf16),
                pltpu.VMEM((2, GROUP * CAP, patches), bf16),
                pltpu.VMEM((2, GROUP * CAP, width), bf16),
                pltpu.VMEM((rows, WIDE), bf16),
                pltpu.VMEM((SLOTS, width, CAP), bf16),
                pltpu.VMEM((count, width, local), bf16),
                pltpu.SemaphoreType.DMA((3,)),
            ],
        ),
        compiler_params=params(),
        cost_estimate=cost(30e9, 2e7),
        name="attend",
    )(meta, chips, x, cm, *pieces, *pieces)


def out_kernel(pieces, meta, chips, o_ref, cm_ref, gate_ref, *rest):
    parts = rest[:pieces]
    part_ref, weights_out, acc, outs, hots, wo_ref, sems = rest[pieces:]
    local = wo_ref.shape[2]
    assemble(chips, parts, wo_ref, 0, EXPERTS)
    wo_ref[EXPERTS] = jnp.zeros(wo_ref.shape[1:], bf16)
    send = pltpu.make_async_copy(wo_ref, weights_out, sems.at[0])
    send.start()
    for at, first in enumerate(range(0, SLOTS, GROUP)):
        slot = at % 2
        count = len(group(first)) * CAP
        for i, e in enumerate(group(first)):
            rows = slice(i * CAP, (i + 1) * CAP)
            off = pl.multiple_of(meta[0, e], PACK)
            mixed = o_ref[pl.ds(off, CAP), :local]
            outs[slot, :, rows] = nt(wo_ref[e], mixed).astype(bf16)
            hot = one_hot(cm_ref[e : e + 1, :], CAP)
            hots[slot, rows, :] = jnp.where(hot, gate_ref[e : e + 1, :], 0.0).astype(bf16)
        part = nn(outs[slot, :, :count], hots[slot, :count, :])
        if at == 0:
            acc[...] = part
        else:
            acc[...] += part
    part_ref[...] = acc[...].T.astype(bf16)
    send.wait()


def out_project(meta, chips, o, cm, gates, pieces):
    patches = cm.shape[1]
    _, rows, local = pieces[0].shape
    width = rows * len(pieces)
    anywhere = pl.BlockSpec(memory_space=pl.ANY)
    return pl.pallas_call(
        functools.partial(out_kernel, len(pieces)),
        out_shape=(sds((patches, width), bf16), sds((SLOTS, width, local), bf16)),
        grid_spec=pltpu.PrefetchScalarGridSpec(
            num_scalar_prefetch=2,
            grid=(1,),
            in_specs=[whole(*o.shape), whole(SLOTS, patches), whole(SLOTS, patches)]
            + [pl.BlockSpec((SLOTS, rows, local), lambda *_: (1, 0, 0)) for _ in pieces],
            out_specs=[whole(patches, width), anywhere],
            scratch_shapes=[
                pltpu.VMEM((width, patches), f32),
                pltpu.VMEM((2, width, GROUP * CAP), bf16),
                pltpu.VMEM((2, GROUP * CAP, patches), bf16),
                pltpu.VMEM((SLOTS, width, local), bf16),
                pltpu.SemaphoreType.DMA((1,)),
            ],
        ),
        compiler_params=params(),
        cost_estimate=cost(8e9, 8e6),
        name="out_project",
    )(meta, chips, o, cm, gates, *pieces)


def middle_kernel(tok_ref, mine_ref, other_ref, gain_ref, router_ref, cm_ref, grad_ref, mid_ref, x_ref, gate_ref):
    width = tok_ref.shape[1]
    middle = tok_ref[...].astype(f32) + (mine_ref[...].astype(f32) + other_ref[...].astype(f32))
    mid_ref[...] = middle
    xhat, _ = norm_stats(middle)
    normed = xhat * gain_ref[...]
    x_ref[:, :width] = normed.astype(bf16)
    x_ref[:, width:] = grad_ref[...]
    logits = lax.dot_general(
        router_ref[...], normed, (((1,), (1,)), ((), ())), precision=highest, preferred_element_type=f32
    )
    gate_ref[...] = dense_gates(logits, cm_ref[...] >= 0)


def middle_step(tokens, mine, other, gain, router_t, cm, masked):
    patches, width = tokens.shape
    return pl.pallas_call(
        middle_kernel,
        out_shape=(
            sds((patches, width), f32),
            sds((patches, 2 * width), bf16),
            sds((SLOTS, patches), f32),
        ),
        in_specs=[vspec()] * 7,
        out_specs=[vspec()] * 3,
        compiler_params=params(),
        cost_estimate=cost(4e9, 6e6),
        name="middle",
    )(tokens, mine, other, gain, router_t, cm, masked)


def gelu_parts(x):
    c = 0.7978845608028654
    square = x * x
    t = jnp.tanh(x * (c + (c * 0.044715) * square))
    half = 0.5 * (1.0 + t)
    slope = half + (0.5 * x) * (1.0 - t * t) * (c + (3.0 * c * 0.044715) * square)
    return x * half, slope


def feed_kernel(
    first, last, rows_of, meta, x_ref, cm_ref, gate_ref, up_ref, down_ref, *rest
):
    if first:
        acc_in, gg_in, keep_ref, send_ref, out_ref, back_ref, gg_ref, acc = rest
    else:
        keep_ref, send_ref, acc, gg_ref = rest
    step = pl.program_id(0)
    e = step + first
    width = x_ref.shape[1] // 2
    size = keep_ref.shape[2]

    @pl.when(step == 0)
    def _():
        acc[...] = acc_in[...] if first else jnp.zeros(acc.shape, f32)
        gg_ref[...] = gg_in[...] if first else jnp.zeros(gg_ref.shape, f32)

    def work(rows_n):
        eq = one_hot(cm_ref[pl.ds(e, 1), :], rows_n)
        hot = jnp.where(eq, 1.0, 0.0).astype(bf16)
        gsel = jnp.where(eq, gate_ref[pl.ds(e, 1), :], 0.0)
        grow = jnp.sum(gsel, axis=1, keepdims=True)
        up = up_ref[0]
        down = down_ref[0]
        got = nn(hot, x_ref[...])
        rows = got[:, :width].astype(bf16)
        grads = got[:, width:]
        hidden = nn(rows, up)
        raw = nn(grads.astype(bf16), down)
        act, slope = gelu_parts(hidden)
        acts = act.astype(bf16)
        outs = nt(down, acts).astype(bf16)
        grad_down = nn((grads * grow).astype(bf16).T, acts).astype(bf16)
        hidden_grad = (raw * grow * slope).astype(bf16)
        back = nt(up, hidden_grad).astype(bf16)
        grad_up = nn(rows.T, hidden_grad).astype(bf16)
        acc[:width] += nn(outs, gsel.astype(bf16))
        acc[width:] += nn(back, hot)
        gg = jnp.sum(raw * acts.astype(f32), axis=1, keepdims=True)
        gg_ref[pl.ds(e, 1), :] = jnp.sum(jnp.where(eq, gg, 0.0), axis=0, keepdims=True)

        @pl.when(meta[2, 0] == 0)
        def _():
            for i, at in enumerate(rows_of):
                keep_ref[i, 0] = grad_up[at : at + size]
                send_ref[i, 0] = grad_down[at : at + size]

        @pl.when(meta[2, 0] != 0)
        def _():
            for i, at in enumerate(rows_of):
                keep_ref[i, 0] = grad_down[at : at + size]
                send_ref[i, 0] = grad_up[at : at + size]

    few = meta[1, e] <= 256

    @pl.when(few)
    def _():
        work(256)

    @pl.when(jnp.logical_not(few))
    def _():
        work(CAP)

    if first:

        @pl.when(e == last - 1)
        def _():
            out_ref[...] = acc[:width].T.astype(bf16)
            back_ref[...] = acc[width:].T.astype(bf16)


def feed(meta, x, cm, gates, weights, rows_of, first, last, carry=()):
    patches, double = x.shape
    width = double // 2
    hidden = weights.shape[2]
    parts = len(rows_of)
    whole = lambda *shape: pl.BlockSpec(shape, lambda e, m: (0,) * len(shape))
    sums = sds((parts, last - first, width // parts, hidden), bf16)
    sums_spec = pl.BlockSpec((parts, 1, width // parts, hidden), lambda e, m: (0, e, 0, 0))
    total, total_spec = sds((double, patches), f32), whole(double, patches)
    gg, gg_spec = sds((SLOTS, patches), f32), whole(SLOTS, patches)
    part, part_spec = sds((patches, width), bf16), whole(patches, width)
    return pl.pallas_call(
        functools.partial(feed_kernel, first, last, rows_of),
        out_shape=(sums, sums, part, part, gg) if first else (sums, sums, total, gg),
        grid_spec=pltpu.PrefetchScalarGridSpec(
            num_scalar_prefetch=1,
            grid=(last - first,),
            in_specs=[
                whole(patches, double),
                whole(SLOTS, patches),
                whole(SLOTS, patches),
                pl.BlockSpec((1, width, hidden), lambda e, m: (e + first, 0, 0)),
                pl.BlockSpec((1, width, hidden), lambda e, m: (e + first + EXPERTS, 0, 0)),
            ]
            + ([total_spec, gg_spec] if first else []),
            out_specs=[sums_spec, sums_spec]
            + ([part_spec, part_spec, gg_spec] if first else [total_spec, gg_spec]),
            scratch_shapes=[pltpu.VMEM((double, patches), f32)] if first else [],
        ),
        compiler_params=params(),
        cost_estimate=cost(20e9, 2e7),
        name="feed",
    )(meta, x, cm, gates, weights, weights, *carry)


def both_kernel(ka_ref, ga_ref, kb_ref, gb_ref, out_ref):
    e = pl.program_id(0)

    @pl.when(e < SPLIT // BATCH)
    def _():
        out_ref[...] = (ka_ref[...].astype(f32) + ga_ref[...].astype(f32)).astype(bf16)

    @pl.when(e >= SPLIT // BATCH)
    def _():
        out_ref[...] = (kb_ref[...].astype(f32) + gb_ref[...].astype(f32)).astype(bf16)


def both_cores(keep_a, got_a, keep_b, got_b):
    parts, _, rows, hidden = keep_a.shape
    block = (parts, BATCH, rows, hidden)
    turn = SPLIT // BATCH
    early = pl.BlockSpec(block, lambda e: (0, jnp.minimum(e, turn - 1), 0, 0))
    late = pl.BlockSpec(block, lambda e: (0, jnp.maximum(e - turn, 0), 0, 0))
    return pl.pallas_call(
        both_kernel,
        out_shape=sds((parts, EXPERTS, rows, hidden), bf16),
        grid=(EXPERTS // BATCH,),
        in_specs=[early, early, late, late],
        out_specs=pl.BlockSpec(block, lambda e: (0, e, 0, 0)),
        compiler_params=params(),
        cost_estimate=cost(5e6, 3e7),
        name="both_cores",
    )(keep_a, got_a, keep_b, got_b)


def both_att_kernel(keep_ref, got_ref, _, out_ref):
    out_ref[...] = (keep_ref[...].astype(f32) + got_ref[...].astype(f32)).astype(bf16)


def both_att(keep, got, earlier):
    parts, count, rows, columns = keep.shape
    block = pl.BlockSpec((parts, GROUP, rows, columns), lambda e: (0, e, 0, 0))
    return pl.pallas_call(
        both_att_kernel,
        out_shape=sds(keep.shape, bf16),
        grid=(count // GROUP,),
        in_specs=[block, block, pl.BlockSpec(memory_space=pl.ANY)],
        out_specs=block,
        compiler_params=params(),
        cost_estimate=cost(1e6, 7e6),
        name="both_att",
    )(keep, got, earlier)


def gate_back(gates, gg):
    return gates * (gg - jnp.sum(gates * gg, axis=0, keepdims=True))


def norm_back(xhat, inv, grad, gain):
    lifted = grad * gain
    first = jnp.mean(lifted, axis=-1, keepdims=True)
    second = jnp.mean(lifted * xhat, axis=-1, keepdims=True)
    return inv * (lifted - first - xhat * second)


def tn_high(a, b):
    return lax.dot_general(a, b, (((0,), (0,)), ((), ())), precision=highest, preferred_element_type=f32)


def second_back_kernel(
    mid_ref, mine_ref, other_ref, ggm_ref, ggo_ref, gate_ref, router_ref, gain_ref, masked_ref,
    mg_ref, mgb_ref, groute_ref, ggain_ref,
):
    xhat, inv = norm_stats(mid_ref[...])
    logit_grad = gate_back(gate_ref[...], ggm_ref[...] + ggo_ref[...])
    grad = (mine_ref[...].astype(f32) + other_ref[...].astype(f32)) + tn_high(logit_grad, router_ref[...])
    groute_ref[...] = jnp.dot(
        logit_grad, xhat * gain_ref[...], precision=highest, preferred_element_type=f32
    )
    ggain_ref[...] = jnp.sum(grad * xhat, axis=0, keepdims=True)
    middle_grad = masked_ref[...].astype(f32) + norm_back(xhat, inv, grad, gain_ref[...])
    mg_ref[...] = middle_grad
    mgb_ref[...] = middle_grad.astype(bf16)


def second_back(middle, mine, other, gg_mine, gg_other, gates, router_t, gain, masked):
    patches, width = middle.shape
    return pl.pallas_call(
        second_back_kernel,
        out_shape=(
            sds((patches, width), f32),
            sds((patches, width), bf16),
            sds((SLOTS, width), f32),
            sds((1, width), f32),
        ),
        in_specs=[vspec()] * 9,
        out_specs=[vspec()] * 4,
        compiler_params=params(),
        cost_estimate=cost(4e9, 8e6),
        name="second_back",
    )(middle, mine, other, gg_mine, gg_other, gates, router_t, gain, masked)


def out_back_kernel(meta, mg_ref, cm_ref, gate_ref, wo_ref, o_ref, do_ref, delta_ref, gg_ref, grad_ref, hots, got, raws, turned, wide):
    step = pl.program_id(0)
    local = wo_ref.shape[2]
    width = mg_ref.shape[1]

    @pl.when(step == 0)
    def _():
        do_ref[...] = jnp.zeros(do_ref.shape, bf16)
        delta_ref[...] = jnp.zeros(delta_ref.shape, f32)
        gg_ref[...] = jnp.zeros(gg_ref.shape, f32)
        wide[:, :width] = mg_ref[...]
        gate = gate_ref[...]
        high = gate.astype(bf16)
        rest = gate - high.astype(f32)
        mid = rest.astype(bf16)
        low = (rest - mid.astype(f32)).astype(bf16)
        blank = jnp.zeros((128 - 3 * SLOTS, gate.shape[1]), f32)
        stack = jnp.concatenate([high.astype(f32), mid.astype(f32), low.astype(f32), blank], axis=0)
        wide[:, width:] = stack.T.astype(bf16)

    for i in range(GROUP):
        hot = one_hot(cm_ref[pl.ds(step * GROUP + i, 1), :], CAP)
        hots[i * CAP : (i + 1) * CAP, :] = jnp.where(hot, 1.0, 0.0).astype(bf16)
    got[...] = nn(hots[...], wide[...])
    lane = lax.broadcasted_iota(jnp.int32, (1, local), 1)
    lane_s = lax.broadcasted_iota(jnp.int32, (1, 128), 1)
    for i in range(GROUP):
        rows = slice(i * CAP, (i + 1) * CAP)
        raws[rows, :] = nn(got[rows, :width].astype(bf16), wo_ref[i])
    for i in range(GROUP):
        e = step * GROUP + i
        rows = slice(i * CAP, (i + 1) * CAP)
        gates = got[rows, width:]
        grow = jnp.sum(jnp.where(lane_s % SLOTS == e, gates, 0.0), axis=1, keepdims=True)
        turned[:, rows] = (got[rows, :width] * grow).astype(bf16).T
        off = pl.multiple_of(meta[0, e], PACK)
        mixed_f = o_ref[pl.ds(off, CAP), :local].astype(f32)
        raw = raws[rows, :]
        gg = jnp.sum(raw * mixed_f, axis=1, keepdims=True)
        eq = one_hot(cm_ref[pl.ds(e, 1), :], CAP)
        gg_ref[pl.ds(e, 1), :] = jnp.sum(jnp.where(eq, gg, 0.0), axis=0, keepdims=True)
        mixed_grad = (raw * grow).astype(bf16)
        do_ref[pl.ds(off, CAP), :local] = mixed_grad
        weighed = mixed_grad.astype(f32) * mixed_f
        delta = jnp.zeros((CAP, 128), f32)
        for h in range(local // HDIM):
            here = (lane >= h * HDIM) & (lane < (h + 1) * HDIM)
            total = jnp.sum(jnp.where(here, weighed, 0.0), axis=1, keepdims=True)
            delta = jnp.where(lane_s == h, total, delta)
        delta_ref[pl.ds(off, CAP), :] = delta
    for i in range(GROUP):
        off = pl.multiple_of(meta[0, step * GROUP + i], PACK)
        grad_ref[i] = nn(turned[:, i * CAP : (i + 1) * CAP], o_ref[pl.ds(off, CAP), :local]).astype(bf16)


def out_back(meta, mg, cm, gates, weights, o):
    patches, width = mg.shape
    local = weights.shape[2]
    rows = o.shape[0]
    return pl.pallas_call(
        out_back_kernel,
        out_shape=(
            sds((rows, WIDE), bf16),
            sds((rows, 128), f32),
            sds((SLOTS, patches), f32),
            sds((SLOTS, width, local), bf16),
        ),
        grid_spec=pltpu.PrefetchScalarGridSpec(
            num_scalar_prefetch=1,
            grid=(SLOTS // GROUP,),
            in_specs=[
                pl.BlockSpec((patches, width), lambda e, m: (0, 0)),
                pl.BlockSpec((SLOTS, patches), lambda e, m: (0, 0)),
                pl.BlockSpec((SLOTS, patches), lambda e, m: (0, 0)),
                pl.BlockSpec((GROUP, width, local), lambda e, m: (e, 0, 0)),
                pl.BlockSpec((rows, WIDE), lambda e, m: (0, 0)),
            ],
            out_specs=[
                pl.BlockSpec((rows, WIDE), lambda e, m: (0, 0)),
                pl.BlockSpec((rows, 128), lambda e, m: (0, 0)),
                pl.BlockSpec((SLOTS, patches), lambda e, m: (0, 0)),
                pl.BlockSpec((GROUP, width, local), lambda e, m: (e, 0, 0)),
            ],
            scratch_shapes=[
                pltpu.VMEM((GROUP * CAP, patches), bf16),
                pltpu.VMEM((GROUP * CAP, width + 128), f32),
                pltpu.VMEM((GROUP * CAP, local), f32),
                pltpu.VMEM((width, GROUP * CAP), bf16),
                pltpu.VMEM((patches, width + 128), bf16),
            ],
        ),
        compiler_params=params(),
        cost_estimate=cost(10e9, 2e7),
        name="out_back",
    )(meta, mg, cm, gates, weights, o)


def attend_back_kernel(
    meta, q_ref, do_ref, lse_ref, delta_ref, k_ref, v_ref, dq_ref, dk_ref, dv_ref, km, kt, vt, dk, dv
):
    heads = km.shape[0]
    head_mask, _ = masks(heads)
    k = k_ref[...].astype(f32)
    k_t = k.T
    v_t = v_ref[...].astype(f32).T
    row = lax.broadcasted_iota(jnp.int32, (WIDE, 1), 0)
    for h in range(heads):
        here = (row >= h * HDIM) & (row < (h + 1) * HDIM)
        km[h] = jnp.where(head_mask[h], k, 0.0).astype(bf16)
        kt[h] = jnp.where(here, k_t, 0.0).astype(bf16)
        vt[h] = jnp.where(here, v_t, 0.0).astype(bf16)
    dk[...] = jnp.zeros(dk.shape, f32)
    dv[...] = jnp.zeros(dv.shape, f32)
    dq_ref[...] = jnp.zeros(dq_ref.shape, bf16)
    tiles = (meta[0, EXPERTS] + (QT - 1)) // QT

    def tile(i, carry):
        start = pl.multiple_of(i * QT, QT)
        q = q_ref[pl.ds(start, QT), :]
        do = do_ref[pl.ds(start, QT), :]
        lse = lse_ref[pl.ds(start, QT), :]
        delta = delta_ref[pl.ds(start, QT), :]
        q_t = q.T
        do_t = do.T
        dq = jnp.zeros((QT, WIDE), f32)
        pairs = [(nn(q, kt[0]), nn(do, vt[0]))]
        for h in range(heads):
            at = slice(h * HDIM, (h + 1) * HDIM)
            if h + 1 < heads:
                pairs.append((nn(q, kt[h + 1]), nn(do, vt[h + 1])))
            s, dp = pairs[h]
            p = jnp.exp2(s * score_scale - lse[:, h : h + 1])
            ds = (p * (dp - delta[:, h : h + 1])).astype(bf16)
            dq = dq + nn(ds, km[h])
            dk[at, :] += nn(q_t[at, :], ds)
            dv[at, :] += nn(do_t[at, :], p.astype(bf16))
        dq_ref[pl.ds(start, QT), :] = (dq * 0.125).astype(bf16)
        return carry

    lax.fori_loop(0, tiles, tile, 0)
    dk_ref[...] = (dk[...] * 0.125).astype(bf16)
    dv_ref[...] = dv[...].astype(bf16)


def attend_back(meta, q, do, lse, delta, k, v, heads):
    rows = q.shape[0]
    patches = k.shape[0]
    return pl.pallas_call(
        attend_back_kernel,
        out_shape=(
            sds((rows, WIDE), bf16),
            sds((heads * HDIM, patches), bf16),
            sds((heads * HDIM, patches), bf16),
        ),
        in_specs=[pl.BlockSpec(memory_space=pltpu.SMEM)] + [vspec()] * 6,
        out_specs=[vspec()] * 3,
        scratch_shapes=[
            pltpu.VMEM((heads, patches, WIDE), bf16),
            pltpu.VMEM((heads, WIDE, patches), bf16),
            pltpu.VMEM((heads, WIDE, patches), bf16),
            pltpu.VMEM((heads * HDIM, patches), f32),
            pltpu.VMEM((heads * HDIM, patches), f32),
        ],
        compiler_params=params(),
        cost_estimate=cost(60e9, 2e7),
        name="attend_back",
    )(meta, q, do, lse, delta, k, v)


def in_back_kernel(
    rows_of, meta, dq_ref, dk_ref, dv_ref, rows_ref, x_ref, cm_ref, wq_ref, wv_ref, go_ref,
    keep_ref, send_ref, part_ref, acc, got, outs, hots,
):
    step = pl.program_id(0)
    local = wq_ref.shape[2]
    size = keep_ref.shape[2]

    def put(at, first, second):
        for i, row in enumerate(rows_of):
            keep_ref[i, at] = first[row : row + size]
            send_ref[i, at] = second[row : row + size]

    @pl.when(step == 0)
    def _():
        acc[...] = jnp.zeros(acc.shape, f32)

    for i in range(GROUP):
        e = step * GROUP + i
        rows = slice(i * CAP, (i + 1) * CAP)
        hot = one_hot(cm_ref[pl.ds(e, 1), :], CAP)
        hots[rows, :] = jnp.where(hot, 1.0, 0.0).astype(bf16)
        off = pl.multiple_of(meta[0, e], PACK)
        dq = dq_ref[pl.ds(off, CAP), :local]
        outs[:, rows] = nt(wq_ref[i], dq).astype(bf16)
        got[0, i] = nn(rows_ref[i], dq).astype(bf16)
        got[1, i] = go_ref[i]
    acc[...] += nn(outs[...], hots[...])

    @pl.when(step == SLOTS // GROUP - 1)
    def _():
        dk = dk_ref[...]
        dv = dv_ref[...]
        last = GROUP - 1
        acc[...] += nn(wq_ref[last], dk) + nn(wv_ref[0], dv)
        part_ref[...] = acc[...].T.astype(bf16)
        x = x_ref[...]
        got[0, last] = nn(dk, x).T.astype(bf16)
        got[1, last] = nn(dv, x).T.astype(bf16)

    @pl.when(meta[2, 0] == 0)
    def _():
        for i in range(GROUP):
            put(i, got[0, i], got[1, i])

    @pl.when(meta[2, 0] != 0)
    def _():
        for i in range(GROUP):
            put(i, got[1, i], got[0, i])


def in_back(meta, dq, dk, dv, rows_att, x, cm, weights, grad_out, rows_of):
    patches, width = x.shape
    local = weights.shape[2]
    rows = dq.shape[0]
    parts = len(rows_of)
    sums = sds((parts, SLOTS, width // parts, local), bf16)
    sums_spec = pl.BlockSpec((parts, GROUP, width // parts, local), lambda e, m: (0, e, 0, 0))
    return pl.pallas_call(
        functools.partial(in_back_kernel, rows_of),
        out_shape=(sums, sums, sds((patches, width), bf16)),
        grid_spec=pltpu.PrefetchScalarGridSpec(
            num_scalar_prefetch=1,
            grid=(SLOTS // GROUP,),
            in_specs=[
                pl.BlockSpec((rows, WIDE), lambda e, m: (0, 0)),
                pl.BlockSpec((local, patches), lambda e, m: (0, 0)),
                pl.BlockSpec((local, patches), lambda e, m: (0, 0)),
                pl.BlockSpec((GROUP, width, CAP), lambda e, m: (e, 0, 0)),
                pl.BlockSpec((patches, width), lambda e, m: (0, 0)),
                pl.BlockSpec((SLOTS, patches), lambda e, m: (0, 0)),
                pl.BlockSpec((GROUP, width, local), lambda e, m: (e, 0, 0)),
                pl.BlockSpec((1, width, local), lambda e, m: (EXPERTS + 1, 0, 0)),
                pl.BlockSpec((GROUP, width, local), lambda e, m: (e, 0, 0)),
            ],
            out_specs=[sums_spec, sums_spec, pl.BlockSpec((patches, width), lambda e, m: (0, 0))],
            scratch_shapes=[
                pltpu.VMEM((width, patches), f32),
                pltpu.VMEM((2, GROUP, width, local), bf16),
                pltpu.VMEM((width, GROUP * CAP), bf16),
                pltpu.VMEM((GROUP * CAP, patches), bf16),
            ],
        ),
        compiler_params=params(),
        cost_estimate=cost(10e9, 2e7),
        name="in_back",
    )(meta, dq, dk, dv, rows_att, x, cm, weights, weights, grad_out)


def route_back_kernel(tok_ref, ggm_ref, ggo_ref, gate_ref, gain_ref, router_ref, lg_ref, groute_ref, ggain_ref):
    xhat, _ = norm_stats(tok_ref[...].astype(f32))
    logit_grad = gate_back(gate_ref[...], ggm_ref[...] + ggo_ref[...])
    lg_ref[...] = logit_grad
    plain = jnp.dot(logit_grad, xhat, precision=highest, preferred_element_type=f32)
    groute_ref[...] = plain * gain_ref[...]
    ggain_ref[...] = 0.5 * jnp.sum(plain * router_ref[...], axis=0, keepdims=True)


def route_back(tokens, gg_mine, gg_other, gates, gain, router_t):
    patches, width = tokens.shape
    return pl.pallas_call(
        route_back_kernel,
        out_shape=(sds((SLOTS, patches), f32), sds((SLOTS, width), f32), sds((1, width), f32)),
        in_specs=[vspec()] * 6,
        out_specs=[vspec()] * 3,
        compiler_params=params(),
        cost_estimate=cost(3e9, 2e6),
        name="route_back",
    )(tokens, gg_mine, gg_other, gates, gain, router_t)


def first_gain_kernel(tok_ref, mine_ref, part_ref, ggain_ref):
    xhat, _ = norm_stats(tok_ref[...].astype(f32))
    ggain_ref[...] = part_ref[...] + jnp.sum(mine_ref[...].astype(f32) * xhat, axis=0, keepdims=True)


def first_gain(tokens, mine, part):
    return pl.pallas_call(
        first_gain_kernel,
        out_shape=sds(part.shape, f32),
        in_specs=[vspec()] * 3,
        out_specs=vspec(),
        compiler_params=params(),
        cost_estimate=cost(3e9, 3e6),
        name="first_gain",
    )(tokens, mine, part)


def first_back_kernel(tok_ref, mine_ref, other_ref, lg_ref, router_ref, gain_ref, mg_ref, gt_ref):
    xhat, inv = norm_stats(tok_ref[...].astype(f32))
    grad = (mine_ref[...].astype(f32) + other_ref[...].astype(f32)) + tn_high(lg_ref[...], router_ref[...])
    gt_ref[...] = mg_ref[...] + norm_back(xhat, inv, grad, gain_ref[...])


def first_back(tokens, mine, other, logit_grad, router_t, gain, middle_grad):
    patches, width = tokens.shape
    return pl.pallas_call(
        first_back_kernel,
        out_shape=sds((patches, width), f32),
        in_specs=[vspec()] * 7,
        out_specs=vspec(),
        compiler_params=params(),
        cost_estimate=cost(3e9, 6e6),
        name="first_back",
    )(tokens, mine, other, logit_grad, router_t, gain, middle_grad)


def tie(*values):
    return lax.optimization_barrier(values)


def after(value, first):
    return lax.optimization_barrier((value, first))[0]


def other_half(x):
    return lax.ppermute(x, "mp", [(0, 1), (1, 0)])


def cube_steps(size):
    steps = []
    step = 1
    while step < size:
        steps.append(step)
        step *= 2
    return steps


def cube_gather(x, size, between):
    index = lax.axis_index("dp")
    x = x[None]
    for at, step in enumerate(reversed(cube_steps(size))):
        if at == 1:
            x = after(x, between)
        got = lax.ppermute(x, "dp", [(i, i ^ step) for i in range(size)])
        upper = (index // step) % 2 == 1
        x = jnp.where(
            upper, jnp.concatenate([got, x], axis=0), jnp.concatenate([x, got], axis=0)
        )
    return x


class Ring:
    def __init__(self, size):
        self.size = size
        self.chips = size // 2
        half = self.chips // 2
        self.order = [2 * i for i in range(half)] + [2 * i + 1 for i in reversed(range(half))]
        self.groups = [[2 * chip + core for chip in self.order] for core in range(2)]
        self.next = []
        for at, chip in enumerate(self.order):
            self.next.append((2 * chip, 2 * self.order[(at + 1) % self.chips]))
            self.next.append((2 * chip + 1, 2 * self.order[at - 1] + 1))
        self.back = [(b, a) for a, b in self.next]
        self.swap = [(i, i ^ 1) for i in range(size)]
        index = lax.axis_index("dp")
        self.core = index % 2
        chip = index // 2
        place = jnp.where(chip % 2 == 0, chip // 2, self.chips - 1 - chip // 2)
        self.place = jnp.where(self.core == 0, place, self.chips - place)

    def chip(self, place):
        place = jnp.where(self.core == 0, place, -place) % self.chips
        return jnp.where(place < self.chips // 2, 2 * place, 2 * (self.chips - 1 - place) + 1)

    def cross(self, x):
        return lax.ppermute(x, "dp", self.swap)

    def step(self, x):
        return lax.ppermute(x, "dp", self.next)

    def chip_rows(self, shard, got):
        first = jnp.where(self.core == 0, shard, got)
        second = jnp.where(self.core == 0, got, shard)
        return jnp.concatenate([first, second], axis=1)

    def sources(self):
        places = [self.place]
        for step in range(1, self.chips // 2 + 1):
            places.append(self.place - step)
            if step < self.chips // 2:
                places.append(self.place + step)
        return jnp.stack([self.chip(p) for p in places]).astype(jnp.int32)

    def finish(self, total):
        count, rows, columns = total.shape
        total = total.reshape(count, 2, rows // 2, columns)
        mine = lax.dynamic_index_in_dim(total, self.core, 1, keepdims=False)
        theirs = lax.dynamic_index_in_dim(total, 1 - self.core, 1, keepdims=False)
        theirs = self.cross(theirs)
        first = jnp.where(self.core == 0, mine, theirs).astype(f32)
        second = jnp.where(self.core == 0, theirs, mine).astype(f32)
        return first, second

    def offload(self, total):
        return lax.psum_scatter(
            total, "dp", scatter_dimension=0, tiled=True, axis_index_groups=self.groups
        )[0]


def body(dp_size, tokens, cotangent, task_ids, att_routes, mlp_routes, valid, gain_one, w_query, w_key,
         w_value, w_out, router_att, gain_two, w_up, w_down, router_mlp):
    tokens = tokens[0]
    patches, width = tokens.shape
    local = w_key.shape[1]
    heads = local // HDIM
    tasks = router_att.shape[0]

    att_shard = jnp.concatenate([w_query, w_key[None], jnp.swapaxes(w_out, 1, 2), w_value[None]], axis=0)
    feed_shard = jnp.concatenate([w_up, jnp.swapaxes(w_down, 1, 2)], axis=0)
    ring = Ring(dp_size) if dp_size == 16 else None
    if ring is None:
        chips = jnp.zeros((1,), jnp.int32)
        pieces = [lax.all_gather(att_shard, "dp", axis=1, tiled=True)]
    else:
        chips = ring.sources()
        piece = ring.chip_rows(att_shard, ring.cross(att_shard))
        pieces = [piece]
        for step in range(1, ring.chips // 2 + 1):
            piece = ring.step(piece)
            pieces.append(piece)
            if step < ring.chips // 2:
                pieces.append(ring.cross(piece))
            if step == HOLD:
                feed_shard = after(feed_shard, piece)
    feed_full = lax.all_gather(feed_shard, "dp", axis=1, tiled=True)

    gain_1 = gain_one[None]
    gain_2 = gain_two[None]
    task = task_ids[0]
    pick = lambda router: jnp.pad(
        lax.dynamic_index_in_dim(router, task, 0, keepdims=False).T, ((0, SLOTS - EXPERTS), (0, 0))
    )
    route_1 = pick(router_att)
    route_2 = pick(router_mlp)
    masked = cotangent[0] * valid[0][:, None].astype(bf16)

    x_one, gates_1, cm_1, cm_2, meta = prep(tokens, gain_1, route_1, att_routes[0].T, mlp_routes[0].T)
    core = jnp.full((1, SLOTS), 0 if ring is None else ring.core, jnp.int32)
    meta_1 = jnp.concatenate([meta[0:2, :, 0], core], axis=0)
    meta_2 = jnp.concatenate([meta[2:4, :, 0], core], axis=0)

    o, lse, k, v, q, rows_att, in_full = attend(meta_1, chips, x_one, cm_1, pieces)
    part, out_full = out_project(meta_1, chips, o, cm_1, gates_1, pieces)
    middle, x_two, gates_2 = middle_step(tokens, part, other_half(part), gain_2, route_2, cm_2, masked)
    rows_of = [0] if ring is None else [chip * (width // ring.chips) for chip in ring.order]
    keep_a, send_a, total, gg_2 = feed(meta_2, x_two, cm_2, gates_2, feed_full, rows_of, 0, SPLIT)
    keep_b, send_b, part_two, back_two, gg_2 = feed(
        meta_2, x_two, cm_2, gates_2, feed_full, rows_of, SPLIT, EXPERTS, (total, gg_2)
    )
    back_two_other, gg_2_other = other_half(back_two), other_half(gg_2)
    if ring is not None:
        feed_sum = both_cores(keep_a, ring.cross(send_a), keep_b, ring.cross(send_b))
        middle_here = after(middle, feed_sum)
    else:
        middle_here = middle
    middle_grad, mg, groute_2, ggain_2 = second_back(
        middle_here, back_two, back_two_other, gg_2, gg_2_other, gates_2, route_2, gain_2, masked
    )
    if ring is not None:
        feed_sum = ring.offload(after(feed_sum, mg))
    part_other = other_half(after(part_two, mg))
    layer_out = (middle + (part_two.astype(f32) + part_other.astype(f32))).astype(bf16)
    do, delta, gg_1, grad_out = out_back(meta_1, mg, cm_1, gates_1, out_full, o)
    gg_other = other_half(gg_1)
    dq, dk, dv = attend_back(meta_1, q, do, lse, delta, k, v, heads)
    dq, gg_other = tie(dq, gg_other)
    logit_grad, groute_1, ggain_1 = route_back(tokens, gg_1, gg_other, gates_1, gain_1, route_1)
    mark = (jnp.arange(width) == task).astype(f32)[None]
    small = jnp.concatenate([groute_1[:EXPERTS], mark, groute_2[:EXPERTS], ggain_2], axis=0).astype(bf16)
    dq, small, ggain_1 = tie(dq, small, ggain_1)
    keep_att, send_att, back_one = in_back(
        meta_1, dq, dk, dv, rows_att, x_one, cm_1, in_full, grad_out, rows_of
    )
    back_other = other_half(back_one)
    ggain_1 = first_gain(tokens, back_one, ggain_1)
    small = jnp.concatenate([small, ggain_1.astype(bf16)], axis=0)
    if ring is None:
        scatter = lambda g: lax.psum_scatter(g[0], "dp", scatter_dimension=1, tiled=True).astype(f32)
        q_mine, o_mine = scatter(keep_att), scatter(send_att)
        up_mine = scatter(jnp.concatenate([keep_a, keep_b], axis=1))
        down_mine = scatter(jnp.concatenate([send_a, send_b], axis=1))
    else:
        att_sum = ring.offload(both_att(keep_att, ring.cross(send_att), feed_sum))
        q_mine, o_mine = ring.finish(att_sum)
        up_mine, down_mine = ring.finish(feed_sum)
    grad_tokens = first_back(
        tokens, back_one, back_other, logit_grad, route_1, gain_1, middle_grad
    )

    every = cube_gather(small, dp_size, grad_tokens).astype(f32)
    named = every[:, EXPERTS, :tasks]
    route_sum = lambda g: jnp.swapaxes(
        jnp.einsum("it,ied->ted", named, g, precision=highest, preferred_element_type=f32), 1, 2
    )
    grad_router_att = route_sum(every[:, :EXPERTS])
    grad_router_mlp = route_sum(every[:, SLOTS : SLOTS + EXPERTS])
    gains = jnp.sum(every[:, 2 * SLOTS - 1 :], axis=0)
    grad_gain_two = gains[0]
    grad_gain_one = gains[1] + other_half(gains[1:])[0]
    return (
        layer_out[None],
        grad_tokens[None],
        grad_gain_one,
        q_mine[:EXPERTS],
        q_mine[EXPERTS],
        o_mine[EXPERTS],
        jnp.swapaxes(o_mine[:EXPERTS], 1, 2),
        grad_router_att,
        grad_gain_two,
        up_mine,
        jnp.swapaxes(down_mine, 1, 2),
        grad_router_mlp,
    )


def solution(mesh):
    dp_size = mesh.shape["dp"]

    def run(*args):
        return body(dp_size, *args)

    return jax.shard_map(
        run,
        mesh=mesh,
        in_specs=(
            P("dp", None, None), P("dp", None, None), P("dp"), P("dp", None, None), P("dp", None, None),
            P("dp", None), P(), P(None, "dp", "mp"), P("dp", "mp"), P("dp", "mp"), P(None, "mp", "dp"),
            P(), P(), P(None, "dp", "mp"), P(None, "mp", "dp"), P(),
        ),
        out_specs=(
            P("dp", None, None), P("dp", None, None), P(), P(None, "dp", "mp"), P("dp", "mp"), P("dp", "mp"),
            P(None, "mp", "dp"), P(), P(), P(None, "dp", "mp"), P(None, "mp", "dp"), P(),
        ),
        check_vma=False,
    )
```

```python
import functools

import jax
import jax.numpy as jnp
from jax import lax
from jax.experimental import pallas as pl
from jax.experimental.pallas import tpu as pltpu
from jax.sharding import PartitionSpec as P

HDIM = 64
EXPERTS = 15
SLOTS = 16
TOP = 4
CAP = 384
PACK = 16
QT = 256
WIDE = 256
HOLD = 3
SPLIT = 9
BATCH = 3
STAT = 8
GROUP = 4
QT2 = 512
EXTRA = 16

norm_eps = 1e-06
f32 = jnp.float32
bf16 = jnp.bfloat16
highest = lax.Precision.HIGHEST
log2e = 1.4426950408889634
score_scale = 0.125 * log2e
vmem_bytes = 60 * 1024 * 1024


def nn(a, b):
    return jnp.dot(a, b, preferred_element_type=f32)


def nt(a, b):
    return lax.dot_general(a, b, (((1,), (1,)), ((), ())), preferred_element_type=f32)


def params(limit=vmem_bytes):
    return pltpu.CompilerParams(vmem_limit_bytes=limit)


def cost(flops, moved):
    return pl.CostEstimate(flops=int(flops), bytes_accessed=int(moved), transcendentals=0)


def vspec():
    return pl.BlockSpec(memory_space=pltpu.VMEM)


def sds(shape, dtype):
    return jax.ShapeDtypeStruct(shape, dtype)


def norm_stats(x):
    centre = jnp.mean(x, axis=-1, keepdims=True)
    shifted = x - centre
    spread = jnp.mean(shifted * shifted, axis=-1, keepdims=True)
    inv = lax.rsqrt(spread + norm_eps)
    return shifted * inv, inv


def dense_gates(logits, chosen):
    top = jnp.max(jnp.where(chosen, logits, -jnp.inf), axis=0, keepdims=True)
    lifted = jnp.where(chosen, jnp.exp(logits - top), 0.0)
    return lifted / jnp.sum(lifted, axis=0, keepdims=True)


def prep_kernel(tok_ref, gain_ref, router_ref, ra_ref, rm_ref, x_ref, gate_ref, cma_ref, cmm_ref, meta_ref):
    patches = tok_ref.shape[0]
    xhat, _ = norm_stats(tok_ref[...].astype(f32))
    normed = xhat * gain_ref[...]
    x_ref[...] = normed.astype(bf16)
    ids = lax.broadcasted_iota(jnp.int32, (SLOTS, patches), 0)
    before = (
        lax.broadcasted_iota(jnp.int32, (patches, patches), 0)
        < lax.broadcasted_iota(jnp.int32, (patches, patches), 1)
    )
    tri = jnp.where(before, 1.0, 0.0).astype(bf16)
    small = lax.broadcasted_iota(jnp.int32, (SLOTS, SLOTS), 1) < lax.broadcasted_iota(
        jnp.int32, (SLOTS, SLOTS), 0
    )
    lower = jnp.where(small, 1.0, 0.0)
    for routes, cm_ref, at in ((ra_ref, cma_ref, 0), (rm_ref, cmm_ref, 2)):
        named = jnp.zeros((SLOTS, patches), f32)
        for k in range(TOP):
            named = named + jnp.where(routes[k : k + 1, :] == ids, 1.0, 0.0)
        ranks = nn(named.astype(bf16), tri)
        cm_ref[...] = jnp.where(named > 0.0, ranks, -1.0).astype(jnp.int32)
        count = jnp.sum(named, axis=1, keepdims=True)
        packed = jnp.ceil(count * (1.0 / PACK)) * PACK
        packed = jnp.broadcast_to(packed, (SLOTS, 128))
        offs = jnp.dot(lower, packed, precision=highest, preferred_element_type=f32)
        meta_ref[at] = offs.astype(jnp.int32)
        meta_ref[at + 1] = jnp.broadcast_to(count, (SLOTS, 128)).astype(jnp.int32)
    logits = lax.dot_general(
        router_ref[...], normed, (((1,), (1,)), ((), ())), precision=highest, preferred_element_type=f32
    )
    gate_ref[...] = dense_gates(logits, cma_ref[...] >= 0)


def prep(tokens, gain, router_t, ra_t, rm_t):
    patches, width = tokens.shape
    return pl.pallas_call(
        prep_kernel,
        out_shape=(
            sds((patches, width), bf16),
            sds((SLOTS, patches), f32),
            sds((SLOTS, patches), jnp.int32),
            sds((SLOTS, patches), jnp.int32),
            sds((4, SLOTS, 128), jnp.int32),
        ),
        in_specs=[vspec()] * 5,
        out_specs=[vspec()] * 5,
        compiler_params=params(),
        cost_estimate=cost(8e9, 4e6),
        name="prep",
    )(tokens, gain, router_t, ra_t, rm_t)


def one_hot(cm_row, rows):
    return cm_row == lax.broadcasted_iota(jnp.int32, (rows, cm_row.shape[1]), 0)


def group(first):
    return range(first, min(first + GROUP, EXPERTS))


def masks(heads):
    lane = lax.broadcasted_iota(jnp.int32, (1, WIDE), 1)
    return [(lane >= h * HDIM) & (lane < (h + 1) * HDIM) for h in range(heads)], lane


def assemble(chips, pieces, out, first, count):
    for i, piece in enumerate(pieces):
        rows = piece.shape[1]
        at = pl.multiple_of(chips[i] * rows, rows)
        out[first : first + count, pl.ds(at, rows), :] = piece[:count]


def attend_kernel(pieces, heads, meta, chips, x_ref, cm_ref, *rest):
    parts, values = rest[:pieces], rest[pieces : 2 * pieces]
    (o_ref, k_ref, v_ref, q_out, rows_out, weights_out,
     km, vt, wide, hots, got, q_ref, rows_ref, weights, sems) = rest[2 * pieces :]
    local = heads * HDIM
    assemble(chips, parts, weights, 0, SLOTS)
    assemble(chips, values, weights, SLOTS, 1)
    send_weights = pltpu.make_async_copy(weights, weights_out, sems.at[0])
    send_weights.start()
    x = x_ref[...]
    head_mask, _ = masks(heads)
    wide[...] = jnp.zeros(wide.shape, bf16)
    wide[:, :local] = weights[EXPERTS]
    k = nn(x, wide[...]).astype(bf16)
    wide[:, :local] = weights[EXPERTS + 1]
    v = nn(x, wide[...])
    k_ref[...] = k
    v_ref[...] = v.astype(bf16)
    v_t = v.T
    ones = jnp.ones((EXTRA, v_t.shape[1]), bf16)
    for h in range(heads):
        km[h] = jnp.where(head_mask[h], k.astype(f32), 0.0).astype(bf16)
        vt[h, :HDIM, :] = v_t[h * HDIM : (h + 1) * HDIM, :].astype(bf16)
        vt[h, HDIM:, :] = ones
    q_ref[...] = jnp.zeros(q_ref.shape, bf16)
    for at, first in enumerate(range(0, SLOTS, GROUP)):
        slot = at % 2
        count = len(group(first)) * CAP
        for i, e in enumerate(group(first)):
            hot = one_hot(cm_ref[e : e + 1, :], CAP)
            hots[slot, i * CAP : (i + 1) * CAP, :] = jnp.where(hot, 1.0, 0.0).astype(bf16)
        got[slot, :count, :] = nn(hots[slot, :count, :], x).astype(bf16)
        for i, e in enumerate(group(first)):
            off = pl.multiple_of(meta[0, e], PACK)
            rows = got[slot, i * CAP : (i + 1) * CAP, :]
            rows_ref[e] = rows.T
            q_ref[pl.ds(off, CAP), :local] = nn(rows, weights[e]).astype(bf16)
    send_q = pltpu.make_async_copy(q_ref, q_out, sems.at[1])
    send_rows = pltpu.make_async_copy(rows_ref, rows_out, sems.at[2])
    send_q.start()
    send_rows.start()
    tiles = (meta[0, EXPERTS] + (QT2 - 1)) // QT2

    def tile(i, carry):
        start = pl.multiple_of(i * QT2, QT2)
        q = q_ref[pl.ds(start, QT2), :]
        scores = [nt(km[h], q) for h in range(heads)]
        outs = []
        stats = []
        for h in range(heads):
            s = scores[h]
            top = jnp.max(s.reshape(8, s.shape[0] // 8, QT2), axis=0)
            top = jnp.max(top, axis=0, keepdims=True) * score_scale
            p = jnp.exp2(s * score_scale - top).astype(bf16)
            oh = nn(vt[h], p)
            total = oh[HDIM : HDIM + 1, :]
            outs.append(oh[:HDIM] * (1.0 / total))
            stats.append(top + jnp.log2(total))
        spare = jnp.zeros((WIDE - local, QT2), f32)
        row = lax.broadcasted_iota(jnp.int32, spare.shape, 0)
        for h in range(heads):
            rest = stats[h]
            for part in range(3):
                piece = rest.astype(bf16).astype(f32)
                spare = jnp.where(row == STAT * part + h, piece, spare)
                rest = rest - piece
        outs.append(spare)
        o_ref[pl.ds(start, QT2), :] = jnp.concatenate(outs, axis=0).astype(bf16).T
        return carry

    o_ref[...] = jnp.zeros(o_ref.shape, bf16)
    lax.fori_loop(0, tiles, tile, 0)
    send_weights.wait()
    send_q.wait()
    send_rows.wait()


def packed_rows(patches):
    return -(-(patches * TOP + EXPERTS * PACK + CAP) // QT2) * QT2


def whole(*shape):
    return pl.BlockSpec(shape, lambda *_: (0,) * len(shape))


def attend(meta, chips, x, cm, pieces):
    patches, width = x.shape
    _, part, local = pieces[0].shape
    count = SLOTS + 1
    heads = local // HDIM
    rows = packed_rows(patches)
    anywhere = pl.BlockSpec(memory_space=pl.ANY)
    return pl.pallas_call(
        functools.partial(attend_kernel, len(pieces), heads),
        out_shape=(
            sds((rows, WIDE), bf16),
            sds((patches, WIDE), bf16),
            sds((patches, WIDE), bf16),
            sds((rows, WIDE), bf16),
            sds((SLOTS, width, CAP), bf16),
            sds((count, width, local), bf16),
        ),
        grid_spec=pltpu.PrefetchScalarGridSpec(
            num_scalar_prefetch=2,
            grid=(1,),
            in_specs=[whole(patches, width), whole(SLOTS, patches)]
            + [whole(SLOTS, part, local) for _ in pieces]
            + [pl.BlockSpec((1, part, local), lambda *_: (2 * SLOTS - 1, 0, 0)) for _ in pieces],
            out_specs=[whole(rows, WIDE), whole(patches, WIDE), whole(patches, WIDE)]
            + [anywhere] * 3,
            scratch_shapes=[
                pltpu.VMEM((heads, patches, WIDE), bf16),
                pltpu.VMEM((heads, HDIM + EXTRA, patches), bf16),
                pltpu.VMEM((width, WIDE), bf16),
                pltpu.VMEM((2, GROUP * CAP, patches), bf16),
                pltpu.VMEM((2, GROUP * CAP, width), bf16),
                pltpu.VMEM((rows, WIDE), bf16),
                pltpu.VMEM((SLOTS, width, CAP), bf16),
                pltpu.VMEM((count, width, local), bf16),
                pltpu.SemaphoreType.DMA((3,)),
            ],
        ),
        compiler_params=params(),
        cost_estimate=cost(30e9, 2e7),
        name="attend",
    )(meta, chips, x, cm, *pieces, *pieces)


def out_kernel(pieces, meta, chips, o_ref, cm_ref, gate_ref, *rest):
    parts = rest[:pieces]
    part_ref, weights_out, acc, outs, hots, wo_ref, sems = rest[pieces:]
    local = wo_ref.shape[2]
    assemble(chips, parts, wo_ref, 0, EXPERTS)
    wo_ref[EXPERTS] = jnp.zeros(wo_ref.shape[1:], bf16)
    send = pltpu.make_async_copy(wo_ref, weights_out, sems.at[0])
    send.start()
    for at, first in enumerate(range(0, SLOTS, GROUP)):
        slot = at % 2
        count = len(group(first)) * CAP
        for i, e in enumerate(group(first)):
            rows = slice(i * CAP, (i + 1) * CAP)
            off = pl.multiple_of(meta[0, e], PACK)
            mixed = o_ref[pl.ds(off, CAP), :local]
            outs[slot, :, rows] = nt(wo_ref[e], mixed).astype(bf16)
            hot = one_hot(cm_ref[e : e + 1, :], CAP)
            hots[slot, rows, :] = jnp.where(hot, gate_ref[e : e + 1, :], 0.0).astype(bf16)
        part = nn(outs[slot, :, :count], hots[slot, :count, :])
        if at == 0:
            acc[...] = part
        else:
            acc[...] += part
    part_ref[...] = acc[...].T.astype(bf16)
    send.wait()


def out_project(meta, chips, o, cm, gates, pieces):
    patches = cm.shape[1]
    _, rows, local = pieces[0].shape
    width = rows * len(pieces)
    anywhere = pl.BlockSpec(memory_space=pl.ANY)
    return pl.pallas_call(
        functools.partial(out_kernel, len(pieces)),
        out_shape=(sds((patches, width), bf16), sds((SLOTS, width, local), bf16)),
        grid_spec=pltpu.PrefetchScalarGridSpec(
            num_scalar_prefetch=2,
            grid=(1,),
            in_specs=[whole(*o.shape), whole(SLOTS, patches), whole(SLOTS, patches)]
            + [pl.BlockSpec((SLOTS, rows, local), lambda *_: (1, 0, 0)) for _ in pieces],
            out_specs=[whole(patches, width), anywhere],
            scratch_shapes=[
                pltpu.VMEM((width, patches), f32),
                pltpu.VMEM((2, width, GROUP * CAP), bf16),
                pltpu.VMEM((2, GROUP * CAP, patches), bf16),
                pltpu.VMEM((SLOTS, width, local), bf16),
                pltpu.SemaphoreType.DMA((1,)),
            ],
        ),
        compiler_params=params(),
        cost_estimate=cost(8e9, 8e6),
        name="out_project",
    )(meta, chips, o, cm, gates, *pieces)


def middle_kernel(tok_ref, mine_ref, other_ref, gain_ref, router_ref, cm_ref, grad_ref, mid_ref, x_ref, gate_ref):
    width = tok_ref.shape[1]
    middle = tok_ref[...].astype(f32) + (mine_ref[...].astype(f32) + other_ref[...].astype(f32))
    mid_ref[...] = middle
    xhat, _ = norm_stats(middle)
    normed = xhat * gain_ref[...]
    x_ref[:, :width] = normed.astype(bf16)
    x_ref[:, width:] = grad_ref[...]
    logits = lax.dot_general(
        router_ref[...], normed, (((1,), (1,)), ((), ())), precision=highest, preferred_element_type=f32
    )
    gate_ref[...] = dense_gates(logits, cm_ref[...] >= 0)


def middle_step(tokens, mine, other, gain, router_t, cm, masked):
    patches, width = tokens.shape
    return pl.pallas_call(
        middle_kernel,
        out_shape=(
            sds((patches, width), f32),
            sds((patches, 2 * width), bf16),
            sds((SLOTS, patches), f32),
        ),
        in_specs=[vspec()] * 7,
        out_specs=[vspec()] * 3,
        compiler_params=params(),
        cost_estimate=cost(4e9, 6e6),
        name="middle",
    )(tokens, mine, other, gain, router_t, cm, masked)


def gelu_parts(x):
    c = 0.7978845608028654
    square = x * x
    t = jnp.tanh(x * (c + (c * 0.044715) * square))
    half = 0.5 * (1.0 + t)
    slope = half + (0.5 * x) * (1.0 - t * t) * (c + (3.0 * c * 0.044715) * square)
    return x * half, slope


def feed_kernel(
    first, last, rows_of, meta, x_ref, cm_ref, gate_ref, up_ref, down_ref, *rest
):
    if first:
        acc_in, gg_in, keep_ref, send_ref, out_ref, back_ref, gg_ref, acc = rest
    else:
        keep_ref, send_ref, acc, gg_ref = rest
    step = pl.program_id(0)
    e = step + first
    width = x_ref.shape[1] // 2
    size = keep_ref.shape[2]

    @pl.when(step == 0)
    def _():
        acc[...] = acc_in[...] if first else jnp.zeros(acc.shape, f32)
        gg_ref[...] = gg_in[...] if first else jnp.zeros(gg_ref.shape, f32)

    def work(rows_n):
        eq = one_hot(cm_ref[pl.ds(e, 1), :], rows_n)
        hot = jnp.where(eq, 1.0, 0.0).astype(bf16)
        gsel = jnp.where(eq, gate_ref[pl.ds(e, 1), :], 0.0)
        grow = jnp.sum(gsel, axis=1, keepdims=True)
        up = up_ref[0]
        down = down_ref[0]
        got = nn(hot, x_ref[...])
        rows = got[:, :width].astype(bf16)
        grads = got[:, width:]
        hidden = nn(rows, up)
        raw = nn(grads.astype(bf16), down)
        act, slope = gelu_parts(hidden)
        acts = act.astype(bf16)
        outs = nt(down, acts).astype(bf16)
        grad_down = nn((grads * grow).astype(bf16).T, acts).astype(bf16)
        hidden_grad = (raw * grow * slope).astype(bf16)
        back = nt(up, hidden_grad).astype(bf16)
        grad_up = nn(rows.T, hidden_grad).astype(bf16)
        acc[:width] += nn(outs, gsel.astype(bf16))
        acc[width:] += nn(back, hot)
        gg = jnp.sum(raw * acts.astype(f32), axis=1, keepdims=True)
        gg_ref[pl.ds(e, 1), :] = jnp.sum(jnp.where(eq, gg, 0.0), axis=0, keepdims=True)

        @pl.when(meta[2, 0] == 0)
        def _():
            for i, at in enumerate(rows_of):
                keep_ref[i, 0] = grad_up[at : at + size]
                send_ref[i, 0] = grad_down[at : at + size]

        @pl.when(meta[2, 0] != 0)
        def _():
            for i, at in enumerate(rows_of):
                keep_ref[i, 0] = grad_down[at : at + size]
                send_ref[i, 0] = grad_up[at : at + size]

    few = meta[1, e] <= 256

    @pl.when(few)
    def _():
        work(256)

    @pl.when(jnp.logical_not(few))
    def _():
        work(CAP)

    if first:

        @pl.when(e == last - 1)
        def _():
            out_ref[...] = acc[:width].T.astype(bf16)
            back_ref[...] = acc[width:].T.astype(bf16)


def feed(meta, x, cm, gates, weights, rows_of, first, last, carry=()):
    patches, double = x.shape
    width = double // 2
    hidden = weights.shape[2]
    parts = len(rows_of)
    whole = lambda *shape: pl.BlockSpec(shape, lambda e, m: (0,) * len(shape))
    sums = sds((parts, last - first, width // parts, hidden), bf16)
    sums_spec = pl.BlockSpec((parts, 1, width // parts, hidden), lambda e, m: (0, e, 0, 0))
    total, total_spec = sds((double, patches), f32), whole(double, patches)
    gg, gg_spec = sds((SLOTS, patches), f32), whole(SLOTS, patches)
    part, part_spec = sds((patches, width), bf16), whole(patches, width)
    return pl.pallas_call(
        functools.partial(feed_kernel, first, last, rows_of),
        out_shape=(sums, sums, part, part, gg) if first else (sums, sums, total, gg),
        grid_spec=pltpu.PrefetchScalarGridSpec(
            num_scalar_prefetch=1,
            grid=(last - first,),
            in_specs=[
                whole(patches, double),
                whole(SLOTS, patches),
                whole(SLOTS, patches),
                pl.BlockSpec((1, width, hidden), lambda e, m: (e + first, 0, 0)),
                pl.BlockSpec((1, width, hidden), lambda e, m: (e + first + EXPERTS, 0, 0)),
            ]
            + ([total_spec, gg_spec] if first else []),
            out_specs=[sums_spec, sums_spec]
            + ([part_spec, part_spec, gg_spec] if first else [total_spec, gg_spec]),
            scratch_shapes=[pltpu.VMEM((double, patches), f32)] if first else [],
        ),
        compiler_params=params(),
        cost_estimate=cost(20e9, 2e7),
        name="feed",
    )(meta, x, cm, gates, weights, weights, *carry)


def both_kernel(ka_ref, ga_ref, kb_ref, gb_ref, out_ref):
    e = pl.program_id(0)

    @pl.when(e < SPLIT // BATCH)
    def _():
        out_ref[...] = (ka_ref[...].astype(f32) + ga_ref[...].astype(f32)).astype(bf16)

    @pl.when(e >= SPLIT // BATCH)
    def _():
        out_ref[...] = (kb_ref[...].astype(f32) + gb_ref[...].astype(f32)).astype(bf16)


def both_cores(keep_a, got_a, keep_b, got_b):
    parts, _, rows, hidden = keep_a.shape
    block = (parts, BATCH, rows, hidden)
    turn = SPLIT // BATCH
    early = pl.BlockSpec(block, lambda e: (0, jnp.minimum(e, turn - 1), 0, 0))
    late = pl.BlockSpec(block, lambda e: (0, jnp.maximum(e - turn, 0), 0, 0))
    return pl.pallas_call(
        both_kernel,
        out_shape=sds((parts, EXPERTS, rows, hidden), bf16),
        grid=(EXPERTS // BATCH,),
        in_specs=[early, early, late, late],
        out_specs=pl.BlockSpec(block, lambda e: (0, e, 0, 0)),
        compiler_params=params(),
        cost_estimate=cost(5e6, 3e7),
        name="both_cores",
    )(keep_a, got_a, keep_b, got_b)


def both_att_kernel(keep_ref, got_ref, _, out_ref):
    out_ref[...] = (keep_ref[...].astype(f32) + got_ref[...].astype(f32)).astype(bf16)


def both_att(keep, got, ready):
    parts, kinds, count, rows, columns = keep.shape
    block = pl.BlockSpec((parts, kinds, 2 * GROUP, rows, columns), lambda e: (0, 0, e, 0, 0))
    anywhere = pl.BlockSpec(memory_space=pl.ANY)
    return pl.pallas_call(
        both_att_kernel,
        out_shape=sds(keep.shape, bf16),
        grid=(count // (2 * GROUP),),
        in_specs=[block, block, anywhere],
        out_specs=block,
        compiler_params=params(),
        cost_estimate=cost(1e6, 7e6),
        name="both_att",
    )(keep, got, ready)


def in_turn_kernel(*refs):
    pass


def in_turn(value, *earlier):
    anywhere = pl.BlockSpec(memory_space=pl.ANY)
    return pl.pallas_call(
        in_turn_kernel,
        out_shape=sds(value.shape, value.dtype),
        in_specs=[anywhere] * (1 + len(earlier)),
        out_specs=anywhere,
        input_output_aliases={0: 0},
        compiler_params=params(),
        name="in_turn",
    )(value, *earlier)


def gate_back(gates, gg):
    return gates * (gg - jnp.sum(gates * gg, axis=0, keepdims=True))


def norm_back(xhat, inv, grad, gain):
    lifted = grad * gain
    first = jnp.mean(lifted, axis=-1, keepdims=True)
    second = jnp.mean(lifted * xhat, axis=-1, keepdims=True)
    return inv * (lifted - first - xhat * second)


def tn_high(a, b):
    return lax.dot_general(a, b, (((0,), (0,)), ((), ())), precision=highest, preferred_element_type=f32)


def second_back_kernel(
    mid_ref, mine_ref, other_ref, ggm_ref, ggo_ref, gate_ref, router_ref, gain_ref, masked_ref,
    mg_ref, mgb_ref, groute_ref, ggain_ref,
):
    xhat, inv = norm_stats(mid_ref[...])
    logit_grad = gate_back(gate_ref[...], ggm_ref[...] + ggo_ref[...])
    grad = (mine_ref[...].astype(f32) + other_ref[...].astype(f32)) + tn_high(logit_grad, router_ref[...])
    groute_ref[...] = jnp.dot(
        logit_grad, xhat * gain_ref[...], precision=highest, preferred_element_type=f32
    )
    ggain_ref[...] = jnp.sum(grad * xhat, axis=0, keepdims=True)
    middle_grad = masked_ref[...].astype(f32) + norm_back(xhat, inv, grad, gain_ref[...])
    mg_ref[...] = middle_grad
    mgb_ref[...] = middle_grad.astype(bf16)


def second_back(middle, mine, other, gg_mine, gg_other, gates, router_t, gain, masked):
    patches, width = middle.shape
    return pl.pallas_call(
        second_back_kernel,
        out_shape=(
            sds((patches, width), f32),
            sds((patches, width), bf16),
            sds((SLOTS, width), f32),
            sds((1, width), f32),
        ),
        in_specs=[vspec()] * 9,
        out_specs=[vspec()] * 4,
        compiler_params=params(),
        cost_estimate=cost(4e9, 8e6),
        name="second_back",
    )(middle, mine, other, gg_mine, gg_other, gates, router_t, gain, masked)


def out_back_kernel(meta, mg_ref, cm_ref, gate_ref, wo_ref, o_ref, do_ref, gg_ref, grad_ref, hots, got, raws, turned, wide):
    step = pl.program_id(0)
    local = wo_ref.shape[2]
    width = mg_ref.shape[1]

    @pl.when(step == 0)
    def _():
        do_ref[...] = jnp.zeros(do_ref.shape, bf16)
        raws[...] = jnp.zeros(raws.shape, f32)
        gg_ref[...] = jnp.zeros(gg_ref.shape, f32)
        wide[:, :width] = mg_ref[...]
        gate = gate_ref[...]
        high = gate.astype(bf16)
        rest = gate - high.astype(f32)
        mid = rest.astype(bf16)
        low = (rest - mid.astype(f32)).astype(bf16)
        blank = jnp.zeros((128 - 3 * SLOTS, gate.shape[1]), f32)
        stack = jnp.concatenate([high.astype(f32), mid.astype(f32), low.astype(f32), blank], axis=0)
        wide[:, width:] = stack.T.astype(bf16)

    for i in range(GROUP):
        hot = one_hot(cm_ref[pl.ds(step * GROUP + i, 1), :], CAP)
        hots[i * CAP : (i + 1) * CAP, :] = jnp.where(hot, 1.0, 0.0).astype(bf16)
    got[...] = nn(hots[...], wide[...])
    lane = lax.broadcasted_iota(jnp.int32, (1, WIDE), 1)
    carried = (lane >= local) & (lane < local + 3 * STAT)
    lane_s = lax.broadcasted_iota(jnp.int32, (1, 128), 1)
    for i in range(GROUP):
        rows = slice(i * CAP, (i + 1) * CAP)
        raws[rows, :local] = nn(got[rows, :width].astype(bf16), wo_ref[i])
    for i in range(GROUP):
        e = step * GROUP + i
        rows = slice(i * CAP, (i + 1) * CAP)
        gates = got[rows, width:]
        grow = jnp.sum(jnp.where(lane_s % SLOTS == e, gates, 0.0), axis=1, keepdims=True)
        turned[:, rows] = (got[rows, :width] * grow).astype(bf16).T
        off = pl.multiple_of(meta[0, e], PACK)
        mixed_f = o_ref[pl.ds(off, CAP), :].astype(f32)
        raw = raws[rows, :]
        gg = jnp.sum(raw * mixed_f, axis=1, keepdims=True)
        eq = one_hot(cm_ref[pl.ds(e, 1), :], CAP)
        gg_ref[pl.ds(e, 1), :] = jnp.sum(jnp.where(eq, gg, 0.0), axis=0, keepdims=True)
        mixed_grad = (raw * grow).astype(bf16).astype(f32)
        weighed = mixed_grad * mixed_f
        row = jnp.where(carried, mixed_f, mixed_grad)
        for h in range(local // HDIM):
            here = (lane >= h * HDIM) & (lane < (h + 1) * HDIM)
            total = jnp.sum(jnp.where(here, weighed, 0.0), axis=1, keepdims=True)
            high = total.astype(bf16).astype(f32)
            row = jnp.where(lane == local + 3 * STAT + h, high, row)
            row = jnp.where(lane == local + 4 * STAT + h, total - high, row)
        do_ref[pl.ds(off, CAP), :] = row.astype(bf16)
    for i in range(GROUP):
        off = pl.multiple_of(meta[0, step * GROUP + i], PACK)
        grad_ref[i] = nn(turned[:, i * CAP : (i + 1) * CAP], o_ref[pl.ds(off, CAP), :local]).astype(bf16)


def out_back(meta, mg, cm, gates, weights, o):
    patches, width = mg.shape
    local = weights.shape[2]
    rows = o.shape[0]
    return pl.pallas_call(
        out_back_kernel,
        out_shape=(
            sds((rows, WIDE), bf16),
            sds((SLOTS, patches), f32),
            sds((SLOTS, width, local), bf16),
        ),
        grid_spec=pltpu.PrefetchScalarGridSpec(
            num_scalar_prefetch=1,
            grid=(SLOTS // GROUP,),
            in_specs=[
                pl.BlockSpec((patches, width), lambda e, m: (0, 0)),
                pl.BlockSpec((SLOTS, patches), lambda e, m: (0, 0)),
                pl.BlockSpec((SLOTS, patches), lambda e, m: (0, 0)),
                pl.BlockSpec((GROUP, width, local), lambda e, m: (e, 0, 0)),
                pl.BlockSpec((rows, WIDE), lambda e, m: (0, 0)),
            ],
            out_specs=[
                pl.BlockSpec((rows, WIDE), lambda e, m: (0, 0)),
                pl.BlockSpec((SLOTS, patches), lambda e, m: (0, 0)),
                pl.BlockSpec((GROUP, width, local), lambda e, m: (e, 0, 0)),
            ],
            scratch_shapes=[
                pltpu.VMEM((GROUP * CAP, patches), bf16),
                pltpu.VMEM((GROUP * CAP, width + 128), f32),
                pltpu.VMEM((GROUP * CAP, WIDE), f32),
                pltpu.VMEM((width, GROUP * CAP), bf16),
                pltpu.VMEM((patches, width + 128), bf16),
            ],
        ),
        compiler_params=params(),
        cost_estimate=cost(10e9, 2e7),
        name="out_back",
    )(meta, mg, cm, gates, weights, o)


def attend_back_kernel(
    meta, q_in, do_in, k_ref, v_ref, dq_ref, dk_ref, dv_ref, km, kt, vt, dk, dv, q_ref, do_ref, sems
):
    heads = km.shape[0]
    local = heads * HDIM
    copies = [
        pltpu.make_async_copy(q_in, q_ref, sems.at[0]),
        pltpu.make_async_copy(do_in, do_ref, sems.at[1]),
    ]
    for copy in copies:
        copy.start()
    at_row = lax.broadcasted_iota(jnp.int32, (WIDE, 128), 0) - local
    at_lane = lax.broadcasted_iota(jnp.int32, (WIDE, 128), 1)
    totals = (at_row < 3 * STAT) & (at_lane < STAT)
    sums = (at_row >= 3 * STAT) & (at_row < 5 * STAT) & (at_lane >= STAT) & (at_lane < 2 * STAT)
    same = (at_row >= 0) & ((at_row - at_lane) % STAT == 0)
    pick = jnp.where(same & (totals | sums), 1.0, 0.0).astype(bf16)
    head_mask, _ = masks(heads)
    k = k_ref[...].astype(f32)
    k_t = k.T
    v_t = v_ref[...].astype(f32).T
    row = lax.broadcasted_iota(jnp.int32, (WIDE, 1), 0)
    for h in range(heads):
        here = (row >= h * HDIM) & (row < (h + 1) * HDIM)
        km[h] = jnp.where(head_mask[h], k, 0.0).astype(bf16)
        kt[h] = jnp.where(here, k_t, 0.0).astype(bf16)
        vt[h] = jnp.where(here, v_t, 0.0).astype(bf16)
    dk[...] = jnp.zeros(dk.shape, f32)
    dv[...] = jnp.zeros(dv.shape, f32)
    dq_ref[...] = jnp.zeros(dq_ref.shape, bf16)
    for copy in copies:
        copy.wait()
    tiles = (meta[0, EXPERTS] + (QT - 1)) // QT

    def tile(i, carry):
        start = pl.multiple_of(i * QT, QT)
        q = q_ref[pl.ds(start, QT), :]
        do = do_ref[pl.ds(start, QT), :]
        stats = nn(do, pick)
        q_t = q.T
        do_t = do.T
        dq = jnp.zeros((QT, WIDE), f32)
        pairs = [(nn(q, kt[0]), nn(do, vt[0]))]
        for h in range(heads):
            at = slice(h * HDIM, (h + 1) * HDIM)
            if h + 1 < heads:
                pairs.append((nn(q, kt[h + 1]), nn(do, vt[h + 1])))
            s, dp = pairs[h]
            p = jnp.exp2(s * score_scale - stats[:, h : h + 1])
            ds = (p * (dp - stats[:, STAT + h : STAT + h + 1])).astype(bf16)
            dq = dq + nn(ds, km[h])
            dk[at, :] += nn(q_t[at, :], ds)
            dv[at, :] += nn(do_t[at, :], p.astype(bf16))
        dq_ref[pl.ds(start, QT), :] = (dq * 0.125).astype(bf16)
        return carry

    lax.fori_loop(0, tiles, tile, 0)
    dk_ref[...] = (dk[...] * 0.125).astype(bf16)
    dv_ref[...] = dv[...].astype(bf16)


def attend_back(meta, q, do, k, v, heads):
    rows = q.shape[0]
    patches = k.shape[0]
    return pl.pallas_call(
        attend_back_kernel,
        out_shape=(
            sds((rows, WIDE), bf16),
            sds((heads * HDIM, patches), bf16),
            sds((heads * HDIM, patches), bf16),
        ),
        in_specs=[pl.BlockSpec(memory_space=pltpu.SMEM)]
        + [pl.BlockSpec(memory_space=pl.ANY)] * 2
        + [vspec()] * 2,
        out_specs=[vspec()] * 3,
        scratch_shapes=[
            pltpu.VMEM((heads, patches, WIDE), bf16),
            pltpu.VMEM((heads, WIDE, patches), bf16),
            pltpu.VMEM((heads, WIDE, patches), bf16),
            pltpu.VMEM((heads * HDIM, patches), f32),
            pltpu.VMEM((heads * HDIM, patches), f32),
            pltpu.VMEM((rows, WIDE), bf16),
            pltpu.VMEM((rows, WIDE), bf16),
            pltpu.SemaphoreType.DMA((2,)),
        ],
        compiler_params=params(),
        cost_estimate=cost(60e9, 2e7),
        name="attend_back",
    )(meta, q, do, k, v)


def width_of(ref):
    return ref.shape[1]


def in_back_kernel(
    rows_of, meta, dq_ref, dk_ref, dv_ref, rows_ref, x_ref, cm_ref, wq_ref, wv_ref, go_ref,
    keep_ref, send_ref, part_ref, acc, got, outs, hots,
):
    step = pl.program_id(0)
    local = wq_ref.shape[2]
    size = keep_ref.shape[3]
    cores = width_of(x_ref) // (size * len(rows_of))

    def put(ref, at, core):
        for i, row in enumerate(rows_of):
            start = pl.multiple_of(row + size * core, 8)
            for kind in range(2):
                ref[i, kind, at] = got[kind, at, pl.ds(start, size), :].astype(bf16)

    @pl.when(step == 0)
    def _():
        acc[...] = jnp.zeros(acc.shape, f32)

    for i in range(GROUP):
        e = step * GROUP + i
        rows = slice(i * CAP, (i + 1) * CAP)
        hot = one_hot(cm_ref[pl.ds(e, 1), :], CAP)
        hots[rows, :] = jnp.where(hot, 1.0, 0.0).astype(bf16)
        off = pl.multiple_of(meta[0, e], PACK)
        dq = dq_ref[pl.ds(off, CAP), :local]
        outs[:, rows] = nt(wq_ref[i], dq).astype(bf16)
        got[0, i] = nn(rows_ref[i], dq)
        got[1, i] = go_ref[i].astype(f32)
    acc[...] += nn(outs[...], hots[...])

    @pl.when(step == SLOTS // GROUP - 1)
    def _():
        dk = dk_ref[...]
        dv = dv_ref[...]
        last = GROUP - 1
        acc[...] += nn(wq_ref[last], dk) + nn(wv_ref[0], dv)
        part_ref[...] = acc[...].T.astype(bf16)
        x = x_ref[...]
        got[0, last] = nn(dk, x).T
        got[1, last] = nn(dv, x).T

    core = meta[2, 0]
    for i in range(GROUP):
        put(keep_ref, i, core)
        put(send_ref, i, cores - 1 - core)


def in_back(meta, dq, dk, dv, rows_att, x, cm, weights, grad_out, rows_of, cores):
    patches, width = x.shape
    local = weights.shape[2]
    rows = dq.shape[0]
    parts = len(rows_of)
    size = width // (parts * cores)
    sums = sds((parts, 2, SLOTS, size, local), bf16)
    sums_spec = pl.BlockSpec((parts, 2, GROUP, size, local), lambda e, m: (0, 0, e, 0, 0))
    return pl.pallas_call(
        functools.partial(in_back_kernel, rows_of),
        out_shape=(sums, sums, sds((patches, width), bf16)),
        grid_spec=pltpu.PrefetchScalarGridSpec(
            num_scalar_prefetch=1,
            grid=(SLOTS // GROUP,),
            in_specs=[
                pl.BlockSpec((rows, WIDE), lambda e, m: (0, 0)),
                pl.BlockSpec((local, patches), lambda e, m: (0, 0)),
                pl.BlockSpec((local, patches), lambda e, m: (0, 0)),
                pl.BlockSpec((GROUP, width, CAP), lambda e, m: (e, 0, 0)),
                pl.BlockSpec((patches, width), lambda e, m: (0, 0)),
                pl.BlockSpec((SLOTS, patches), lambda e, m: (0, 0)),
                pl.BlockSpec((GROUP, width, local), lambda e, m: (e, 0, 0)),
                pl.BlockSpec((1, width, local), lambda e, m: (EXPERTS + 1, 0, 0)),
                pl.BlockSpec((GROUP, width, local), lambda e, m: (e, 0, 0)),
            ],
            out_specs=[sums_spec, sums_spec, pl.BlockSpec((patches, width), lambda e, m: (0, 0))],
            scratch_shapes=[
                pltpu.VMEM((width, patches), f32),
                pltpu.VMEM((2, GROUP, width, local), f32),
                pltpu.VMEM((width, GROUP * CAP), bf16),
                pltpu.VMEM((GROUP * CAP, patches), bf16),
            ],
        ),
        compiler_params=params(),
        cost_estimate=cost(10e9, 2e7),
        name="in_back",
    )(meta, dq, dk, dv, rows_att, x, cm, weights, weights, grad_out)


def route_back_kernel(tok_ref, ggm_ref, ggo_ref, gate_ref, gain_ref, router_ref, lg_ref, groute_ref, ggain_ref):
    xhat, _ = norm_stats(tok_ref[...].astype(f32))
    logit_grad = gate_back(gate_ref[...], ggm_ref[...] + ggo_ref[...])
    lg_ref[...] = logit_grad
    plain = jnp.dot(logit_grad, xhat, precision=highest, preferred_element_type=f32)
    groute_ref[...] = plain * gain_ref[...]
    ggain_ref[...] = 0.5 * jnp.sum(plain * router_ref[...], axis=0, keepdims=True)


def route_back(tokens, gg_mine, gg_other, gates, gain, router_t):
    patches, width = tokens.shape
    return pl.pallas_call(
        route_back_kernel,
        out_shape=(sds((SLOTS, patches), f32), sds((SLOTS, width), f32), sds((1, width), f32)),
        in_specs=[vspec()] * 6,
        out_specs=[vspec()] * 3,
        compiler_params=params(),
        cost_estimate=cost(3e9, 2e6),
        name="route_back",
    )(tokens, gg_mine, gg_other, gates, gain, router_t)


def first_gain_kernel(tok_ref, mine_ref, part_ref, ggain_ref):
    xhat, _ = norm_stats(tok_ref[...].astype(f32))
    ggain_ref[...] = part_ref[...] + jnp.sum(mine_ref[...].astype(f32) * xhat, axis=0, keepdims=True)


def first_gain(tokens, mine, part):
    return pl.pallas_call(
        first_gain_kernel,
        out_shape=sds(part.shape, f32),
        in_specs=[vspec()] * 3,
        out_specs=vspec(),
        compiler_params=params(),
        cost_estimate=cost(3e9, 3e6),
        name="first_gain",
    )(tokens, mine, part)


def first_back_kernel(tok_ref, mine_ref, other_ref, lg_ref, router_ref, gain_ref, mg_ref, gt_ref):
    xhat, inv = norm_stats(tok_ref[...].astype(f32))
    grad = (mine_ref[...].astype(f32) + other_ref[...].astype(f32)) + tn_high(lg_ref[...], router_ref[...])
    gt_ref[...] = mg_ref[...] + norm_back(xhat, inv, grad, gain_ref[...])


def first_back(tokens, mine, other, logit_grad, router_t, gain, middle_grad):
    patches, width = tokens.shape
    return pl.pallas_call(
        first_back_kernel,
        out_shape=sds((patches, width), f32),
        in_specs=[vspec()] * 7,
        out_specs=vspec(),
        compiler_params=params(),
        cost_estimate=cost(3e9, 6e6),
        name="first_back",
    )(tokens, mine, other, logit_grad, router_t, gain, middle_grad)


def tie(*values):
    return lax.optimization_barrier(values)


def after(value, first):
    return lax.optimization_barrier((value, first))[0]


def other_half(x):
    return lax.ppermute(x, "mp", [(0, 1), (1, 0)])


def cube_steps(size):
    steps = []
    step = 1
    while step < size:
        steps.append(step)
        step *= 2
    return steps


def cube_gather(x, size, between):
    index = lax.axis_index("dp")
    x = x[None]
    for at, step in enumerate(reversed(cube_steps(size))):
        if at == 1:
            x = after(x, between)
        got = lax.ppermute(x, "dp", [(i, i ^ step) for i in range(size)])
        upper = (index // step) % 2 == 1
        x = jnp.where(
            upper, jnp.concatenate([got, x], axis=0), jnp.concatenate([x, got], axis=0)
        )
    return x


class Ring:
    def __init__(self, size):
        self.size = size
        self.chips = size // 2
        half = self.chips // 2
        self.order = [2 * i for i in range(half)] + [2 * i + 1 for i in reversed(range(half))]
        self.groups = [[2 * chip + core for chip in self.order] for core in range(2)]
        self.next = []
        for at, chip in enumerate(self.order):
            self.next.append((2 * chip, 2 * self.order[(at + 1) % self.chips]))
            self.next.append((2 * chip + 1, 2 * self.order[at - 1] + 1))
        self.back = [(b, a) for a, b in self.next]
        self.swap = [(i, i ^ 1) for i in range(size)]
        index = lax.axis_index("dp")
        self.core = index % 2
        chip = index // 2
        place = jnp.where(chip % 2 == 0, chip // 2, self.chips - 1 - chip // 2)
        self.place = jnp.where(self.core == 0, place, self.chips - place)

    def chip(self, place):
        place = jnp.where(self.core == 0, place, -place) % self.chips
        return jnp.where(place < self.chips // 2, 2 * place, 2 * (self.chips - 1 - place) + 1)

    def cross(self, x):
        return lax.ppermute(x, "dp", self.swap)

    def step(self, x):
        return lax.ppermute(x, "dp", self.next)

    def chip_rows(self, shard, got):
        first = jnp.where(self.core == 0, shard, got)
        second = jnp.where(self.core == 0, got, shard)
        return jnp.concatenate([first, second], axis=1)

    def sources(self):
        places = [self.place]
        for step in range(1, self.chips // 2 + 1):
            places.append(self.place - step)
            if step < self.chips // 2:
                places.append(self.place + step)
        return jnp.stack([self.chip(p) for p in places]).astype(jnp.int32)

    def finish(self, total):
        count, rows, columns = total.shape
        total = total.reshape(count, 2, rows // 2, columns)
        mine = lax.dynamic_index_in_dim(total, self.core, 1, keepdims=False)
        theirs = lax.dynamic_index_in_dim(total, 1 - self.core, 1, keepdims=False)
        theirs = self.cross(theirs)
        first = jnp.where(self.core == 0, mine, theirs).astype(f32)
        second = jnp.where(self.core == 0, theirs, mine).astype(f32)
        return first, second

    def offload(self, total):
        return lax.psum_scatter(
            total, "dp", scatter_dimension=0, tiled=True, axis_index_groups=self.groups
        )[0]


def body(dp_size, tokens, cotangent, task_ids, att_routes, mlp_routes, valid, gain_one, w_query, w_key,
         w_value, w_out, router_att, gain_two, w_up, w_down, router_mlp):
    tokens = tokens[0]
    patches, width = tokens.shape
    local = w_key.shape[1]
    heads = local // HDIM
    tasks = router_att.shape[0]

    att_shard = jnp.concatenate([w_query, w_key[None], jnp.swapaxes(w_out, 1, 2), w_value[None]], axis=0)
    feed_shard = jnp.concatenate([w_up, jnp.swapaxes(w_down, 1, 2)], axis=0)
    ring = Ring(dp_size) if dp_size == 16 else None
    if ring is None:
        chips = jnp.zeros((1,), jnp.int32)
        pieces = [lax.all_gather(att_shard, "dp", axis=1, tiled=True)]
    else:
        chips = ring.sources()
        piece = ring.chip_rows(att_shard, ring.cross(att_shard))
        pieces = [piece]
        for step in range(1, ring.chips // 2 + 1):
            piece = ring.step(piece)
            pieces.append(piece)
            if step < ring.chips // 2:
                pieces.append(ring.cross(piece))
            if step == HOLD:
                feed_shard = after(feed_shard, piece)
    feed_full = lax.all_gather(feed_shard, "dp", axis=1, tiled=True)

    gain_1 = gain_one[None]
    gain_2 = gain_two[None]
    task = task_ids[0]
    pick = lambda router: jnp.pad(
        lax.dynamic_index_in_dim(router, task, 0, keepdims=False).T, ((0, SLOTS - EXPERTS), (0, 0))
    )
    route_1 = pick(router_att)
    route_2 = pick(router_mlp)
    masked = cotangent[0] * valid[0][:, None].astype(bf16)

    x_one, gates_1, cm_1, cm_2, meta = prep(tokens, gain_1, route_1, att_routes[0].T, mlp_routes[0].T)
    core = jnp.full((1, SLOTS), 0 if ring is None else ring.core, jnp.int32)
    meta_1 = jnp.concatenate([meta[0:2, :, 0], core], axis=0)
    meta_2 = jnp.concatenate([meta[2:4, :, 0], core], axis=0)

    o, k, v, q, rows_att, in_full = attend(meta_1, chips, x_one, cm_1, pieces)
    part, out_full = out_project(meta_1, chips, o, cm_1, gates_1, pieces)
    middle, x_two, gates_2 = middle_step(tokens, part, other_half(part), gain_2, route_2, cm_2, masked)
    rows_of = [0] if ring is None else [chip * (width // ring.chips) for chip in ring.order]
    keep_a, send_a, total, gg_2 = feed(meta_2, x_two, cm_2, gates_2, feed_full, rows_of, 0, SPLIT)
    keep_b, send_b, part_two, back_two, gg_2 = feed(
        meta_2, x_two, cm_2, gates_2, feed_full, rows_of, SPLIT, EXPERTS, (total, gg_2)
    )
    back_two_other, gg_2_other = other_half(back_two), other_half(gg_2)
    if ring is not None:
        feed_sum = both_cores(keep_a, ring.cross(send_a), keep_b, ring.cross(send_b))
        feed_sum = in_turn(feed_sum, back_two_other, gg_2_other)
        middle_here = after(middle, feed_sum)
    else:
        middle_here = middle
    middle_grad, mg, groute_2, ggain_2 = second_back(
        middle_here, back_two, back_two_other, gg_2, gg_2_other, gates_2, route_2, gain_2, masked
    )
    if ring is not None:
        feed_sum = ring.offload(feed_sum)
    part_other = other_half(after(part_two, mg))
    layer_out = (middle + (part_two.astype(f32) + part_other.astype(f32))).astype(bf16)
    do, gg_1, grad_out = out_back(meta_1, mg, cm_1, gates_1, out_full, o)
    gg_other = other_half(gg_1)
    dq, dk, dv = attend_back(meta_1, q, do, k, v, heads)
    dq, gg_other = tie(dq, gg_other)
    keep_att, send_att, back_one = in_back(
        meta_1, dq, dk, dv, rows_att, x_one, cm_1, in_full, grad_out, rows_of, 1 if ring is None else 2
    )
    logit_grad, groute_1, ggain_1 = route_back(
        tokens, gg_1, gg_other, after(gates_1, back_one), gain_1, route_1
    )
    mark = (jnp.arange(width) == task).astype(f32)[None]
    small = jnp.concatenate([groute_1[:EXPERTS], mark, groute_2[:EXPERTS], ggain_2], axis=0).astype(bf16)
    back_other = other_half(back_one)
    gain_sum = first_gain(tokens, back_one, ggain_1)
    small = jnp.concatenate([small, gain_sum.astype(bf16)], axis=0)
    if ring is None:
        scatter = lambda g: lax.psum_scatter(g[0], "dp", scatter_dimension=1, tiled=True).astype(f32)
        q_mine, o_mine = scatter(keep_att[:, 0]), scatter(keep_att[:, 1])
        up_mine = scatter(jnp.concatenate([keep_a, keep_b], axis=1))
        down_mine = scatter(jnp.concatenate([send_a, send_b], axis=1))
    else:
        att_sum = both_att(keep_att, ring.cross(send_att), ggain_1)
        att_sum = ring.offload(in_turn(att_sum, feed_sum)).astype(f32)
        q_mine, o_mine = att_sum[0], att_sum[1]
        up_mine, down_mine = ring.finish(feed_sum)
    grad_tokens = first_back(
        tokens, back_one, back_other, logit_grad, route_1, gain_1, middle_grad
    )

    every = cube_gather(small, dp_size, grad_tokens).astype(f32)
    named = every[:, EXPERTS, :tasks]
    route_sum = lambda g: jnp.swapaxes(
        jnp.einsum("it,ied->ted", named, g, precision=highest, preferred_element_type=f32), 1, 2
    )
    grad_router_att = route_sum(every[:, :EXPERTS])
    grad_router_mlp = route_sum(every[:, SLOTS : SLOTS + EXPERTS])
    gains = jnp.sum(every[:, 2 * SLOTS - 1 :], axis=0)
    grad_gain_two = gains[0]
    grad_gain_one = gains[1] + other_half(gains[1:])[0]
    return (
        layer_out[None],
        grad_tokens[None],
        grad_gain_one,
        q_mine[:EXPERTS],
        q_mine[EXPERTS],
        o_mine[EXPERTS],
        jnp.swapaxes(o_mine[:EXPERTS], 1, 2),
        grad_router_att,
        grad_gain_two,
        up_mine,
        jnp.swapaxes(down_mine, 1, 2),
        grad_router_mlp,
    )


def solution(mesh):
    dp_size = mesh.shape["dp"]

    def run(*args):
        return body(dp_size, *args)

    return jax.shard_map(
        run,
        mesh=mesh,
        in_specs=(
            P("dp", None, None), P("dp", None, None), P("dp"), P("dp", None, None), P("dp", None, None),
            P("dp", None), P(), P(None, "dp", "mp"), P("dp", "mp"), P("dp", "mp"), P(None, "mp", "dp"),
            P(), P(), P(None, "dp", "mp"), P(None, "mp", "dp"), P(),
        ),
        out_specs=(
            P("dp", None, None), P("dp", None, None), P(), P(None, "dp", "mp"), P("dp", "mp"), P("dp", "mp"),
            P(None, "mp", "dp"), P(), P(), P(None, "dp", "mp"), P(None, "mp", "dp"), P(),
        ),
        check_vma=False,
    )
```

```python
import functools

import jax
import jax.numpy as jnp
from jax import lax
from jax.experimental import pallas as pl
from jax.experimental.pallas import tpu as pltpu
from jax.sharding import PartitionSpec as P

HDIM = 64
EXPERTS = 15
SLOTS = 16
TOP = 4
CAP = 384
PACK = 16
QT = 256
WIDE = 256
HOLD = 3
SPLIT = 9
BATCH = 3
STAT = 8
GROUP = 4
QT2 = 512
EXTRA = 16

norm_eps = 1e-06
f32 = jnp.float32
bf16 = jnp.bfloat16
highest = lax.Precision.HIGHEST
log2e = 1.4426950408889634
score_scale = 0.125 * log2e
vmem_bytes = 60 * 1024 * 1024


def nn(a, b):
    return jnp.dot(a, b, preferred_element_type=f32)


def nt(a, b):
    return lax.dot_general(a, b, (((1,), (1,)), ((), ())), preferred_element_type=f32)


def params(limit=vmem_bytes):
    return pltpu.CompilerParams(vmem_limit_bytes=limit)


def cost(flops, moved):
    return pl.CostEstimate(flops=int(flops), bytes_accessed=int(moved), transcendentals=0)


def vspec():
    return pl.BlockSpec(memory_space=pltpu.VMEM)


def sds(shape, dtype):
    return jax.ShapeDtypeStruct(shape, dtype)


def norm_stats(x):
    centre = jnp.mean(x, axis=-1, keepdims=True)
    shifted = x - centre
    spread = jnp.mean(shifted * shifted, axis=-1, keepdims=True)
    inv = lax.rsqrt(spread + norm_eps)
    return shifted * inv, inv


def dense_gates(logits, chosen):
    top = jnp.max(jnp.where(chosen, logits, -jnp.inf), axis=0, keepdims=True)
    lifted = jnp.where(chosen, jnp.exp(logits - top), 0.0)
    return lifted / jnp.sum(lifted, axis=0, keepdims=True)


def prep_kernel(tok_ref, gain_ref, router_ref, ra_ref, rm_ref, x_ref, gate_ref, cma_ref, cmm_ref, meta_ref):
    patches = tok_ref.shape[0]
    xhat, _ = norm_stats(tok_ref[...].astype(f32))
    normed = xhat * gain_ref[...]
    x_ref[...] = normed.astype(bf16)
    ids = lax.broadcasted_iota(jnp.int32, (SLOTS, patches), 0)
    before = (
        lax.broadcasted_iota(jnp.int32, (patches, patches), 0)
        < lax.broadcasted_iota(jnp.int32, (patches, patches), 1)
    )
    tri = jnp.where(before, 1.0, 0.0).astype(bf16)
    small = lax.broadcasted_iota(jnp.int32, (SLOTS, SLOTS), 1) < lax.broadcasted_iota(
        jnp.int32, (SLOTS, SLOTS), 0
    )
    lower = jnp.where(small, 1.0, 0.0)
    for routes, cm_ref, at in ((ra_ref, cma_ref, 0), (rm_ref, cmm_ref, 2)):
        named = jnp.zeros((SLOTS, patches), f32)
        for k in range(TOP):
            named = named + jnp.where(routes[k : k + 1, :] == ids, 1.0, 0.0)
        ranks = nn(named.astype(bf16), tri)
        cm_ref[...] = jnp.where(named > 0.0, ranks, -1.0).astype(jnp.int32)
        count = jnp.sum(named, axis=1, keepdims=True)
        packed = jnp.ceil(count * (1.0 / PACK)) * PACK
        packed = jnp.broadcast_to(packed, (SLOTS, 128))
        offs = jnp.dot(lower, packed, precision=highest, preferred_element_type=f32)
        meta_ref[at] = offs.astype(jnp.int32)
        meta_ref[at + 1] = jnp.broadcast_to(count, (SLOTS, 128)).astype(jnp.int32)
    logits = lax.dot_general(
        router_ref[...], normed, (((1,), (1,)), ((), ())), precision=highest, preferred_element_type=f32
    )
    gate_ref[...] = dense_gates(logits, cma_ref[...] >= 0)


def prep(tokens, gain, router_t, ra_t, rm_t):
    patches, width = tokens.shape
    return pl.pallas_call(
        prep_kernel,
        out_shape=(
            sds((patches, width), bf16),
            sds((SLOTS, patches), f32),
            sds((SLOTS, patches), jnp.int32),
            sds((SLOTS, patches), jnp.int32),
            sds((4, SLOTS, 128), jnp.int32),
        ),
        in_specs=[vspec()] * 5,
        out_specs=[vspec()] * 5,
        compiler_params=params(),
        cost_estimate=cost(8e9, 4e6),
        name="prep",
    )(tokens, gain, router_t, ra_t, rm_t)


def one_hot(cm_row, rows):
    return cm_row == lax.broadcasted_iota(jnp.int32, (rows, cm_row.shape[1]), 0)


def group(first):
    return range(first, min(first + GROUP, EXPERTS))


def masks(heads):
    lane = lax.broadcasted_iota(jnp.int32, (1, WIDE), 1)
    return [(lane >= h * HDIM) & (lane < (h + 1) * HDIM) for h in range(heads)], lane


def assemble(chips, pieces, out, first, count):
    for i, piece in enumerate(pieces):
        rows = piece.shape[1]
        at = pl.multiple_of(chips[i] * rows, rows)
        out[first : first + count, pl.ds(at, rows), :] = piece[:count]


def attend_kernel(pieces, heads, meta, chips, x_ref, cm_ref, *rest):
    parts, values = rest[:pieces], rest[pieces : 2 * pieces]
    (o_ref, k_ref, v_ref, q_out, rows_out, weights_out,
     km, vt, wide, hots, got, q_ref, rows_ref, weights, sems) = rest[2 * pieces :]
    local = heads * HDIM
    assemble(chips, parts, weights, 0, SLOTS)
    assemble(chips, values, weights, SLOTS, 1)
    send_weights = pltpu.make_async_copy(weights, weights_out, sems.at[0])
    send_weights.start()
    x = x_ref[...]
    head_mask, _ = masks(heads)
    wide[...] = jnp.zeros(wide.shape, bf16)
    wide[:, :local] = weights[EXPERTS]
    k = nn(x, wide[...]).astype(bf16)
    wide[:, :local] = weights[EXPERTS + 1]
    v = nn(x, wide[...])
    k_ref[...] = k
    v_ref[...] = v.astype(bf16)
    v_t = v.T
    ones = jnp.ones((EXTRA, v_t.shape[1]), bf16)
    for h in range(heads):
        km[h] = jnp.where(head_mask[h], k.astype(f32), 0.0).astype(bf16)
        vt[h, :HDIM, :] = v_t[h * HDIM : (h + 1) * HDIM, :].astype(bf16)
        vt[h, HDIM:, :] = ones
    q_ref[...] = jnp.zeros(q_ref.shape, bf16)
    for at, first in enumerate(range(0, SLOTS, GROUP)):
        slot = at % 2
        count = len(group(first)) * CAP
        for i, e in enumerate(group(first)):
            hot = one_hot(cm_ref[e : e + 1, :], CAP)
            hots[slot, i * CAP : (i + 1) * CAP, :] = jnp.where(hot, 1.0, 0.0).astype(bf16)
        got[slot, :count, :] = nn(hots[slot, :count, :], x).astype(bf16)
        for i, e in enumerate(group(first)):
            off = pl.multiple_of(meta[0, e], PACK)
            rows = got[slot, i * CAP : (i + 1) * CAP, :]
            rows_ref[e] = rows.T
            q_ref[pl.ds(off, CAP), :local] = nn(rows, weights[e]).astype(bf16)
    send_q = pltpu.make_async_copy(q_ref, q_out, sems.at[1])
    send_rows = pltpu.make_async_copy(rows_ref, rows_out, sems.at[2])
    send_q.start()
    send_rows.start()
    tiles = (meta[0, EXPERTS] + (QT2 - 1)) // QT2

    def tile(i, carry):
        start = pl.multiple_of(i * QT2, QT2)
        q = q_ref[pl.ds(start, QT2), :]
        scores = [nt(km[h], q) for h in range(heads)]
        outs = []
        stats = []
        for h in range(heads):
            s = scores[h]
            top = jnp.max(s.reshape(8, s.shape[0] // 8, QT2), axis=0)
            top = jnp.max(top, axis=0, keepdims=True) * score_scale
            p = jnp.exp2(s * score_scale - top).astype(bf16)
            oh = nn(vt[h], p)
            total = oh[HDIM : HDIM + 1, :]
            outs.append(oh[:HDIM] * (1.0 / total))
            stats.append(top + jnp.log2(total))
        spare = jnp.zeros((WIDE - local, QT2), f32)
        row = lax.broadcasted_iota(jnp.int32, spare.shape, 0)
        for h in range(heads):
            rest = stats[h]
            for part in range(3):
                piece = rest.astype(bf16).astype(f32)
                spare = jnp.where(row == STAT * part + h, piece, spare)
                rest = rest - piece
        outs.append(spare)
        o_ref[pl.ds(start, QT2), :] = jnp.concatenate(outs, axis=0).astype(bf16).T
        return carry

    o_ref[...] = jnp.zeros(o_ref.shape, bf16)
    lax.fori_loop(0, tiles, tile, 0)
    send_weights.wait()
    send_q.wait()
    send_rows.wait()


def packed_rows(patches):
    return -(-(patches * TOP + EXPERTS * PACK + CAP) // QT2) * QT2


def whole(*shape):
    return pl.BlockSpec(shape, lambda *_: (0,) * len(shape))


def attend(meta, chips, x, cm, pieces):
    patches, width = x.shape
    _, part, local = pieces[0].shape
    count = SLOTS + 1
    heads = local // HDIM
    rows = packed_rows(patches)
    anywhere = pl.BlockSpec(memory_space=pl.ANY)
    return pl.pallas_call(
        functools.partial(attend_kernel, len(pieces), heads),
        out_shape=(
            sds((rows, WIDE), bf16),
            sds((patches, WIDE), bf16),
            sds((patches, WIDE), bf16),
            sds((rows, WIDE), bf16),
            sds((SLOTS, width, CAP), bf16),
            sds((count, width, local), bf16),
        ),
        grid_spec=pltpu.PrefetchScalarGridSpec(
            num_scalar_prefetch=2,
            grid=(1,),
            in_specs=[whole(patches, width), whole(SLOTS, patches)]
            + [whole(SLOTS, part, local) for _ in pieces]
            + [pl.BlockSpec((1, part, local), lambda *_: (2 * SLOTS - 1, 0, 0)) for _ in pieces],
            out_specs=[whole(rows, WIDE), whole(patches, WIDE), whole(patches, WIDE)]
            + [anywhere] * 3,
            scratch_shapes=[
                pltpu.VMEM((heads, patches, WIDE), bf16),
                pltpu.VMEM((heads, HDIM + EXTRA, patches), bf16),
                pltpu.VMEM((width, WIDE), bf16),
                pltpu.VMEM((2, GROUP * CAP, patches), bf16),
                pltpu.VMEM((2, GROUP * CAP, width), bf16),
                pltpu.VMEM((rows, WIDE), bf16),
                pltpu.VMEM((SLOTS, width, CAP), bf16),
                pltpu.VMEM((count, width, local), bf16),
                pltpu.SemaphoreType.DMA((3,)),
            ],
        ),
        compiler_params=params(),
        cost_estimate=cost(30e9, 2e7),
        name="attend",
    )(meta, chips, x, cm, *pieces, *pieces)


def out_kernel(pieces, meta, chips, o_ref, cm_ref, gate_ref, *rest):
    parts = rest[:pieces]
    part_ref, weights_out, acc, outs, hots, wo_ref, sems = rest[pieces:]
    local = wo_ref.shape[2]
    assemble(chips, parts, wo_ref, 0, EXPERTS)
    wo_ref[EXPERTS] = jnp.zeros(wo_ref.shape[1:], bf16)
    send = pltpu.make_async_copy(wo_ref, weights_out, sems.at[0])
    send.start()
    for at, first in enumerate(range(0, SLOTS, GROUP)):
        slot = at % 2
        count = len(group(first)) * CAP
        for i, e in enumerate(group(first)):
            rows = slice(i * CAP, (i + 1) * CAP)
            off = pl.multiple_of(meta[0, e], PACK)
            mixed = o_ref[pl.ds(off, CAP), :local]
            outs[slot, :, rows] = nt(wo_ref[e], mixed).astype(bf16)
            hot = one_hot(cm_ref[e : e + 1, :], CAP)
            hots[slot, rows, :] = jnp.where(hot, gate_ref[e : e + 1, :], 0.0).astype(bf16)
        part = nn(outs[slot, :, :count], hots[slot, :count, :])
        if at == 0:
            acc[...] = part
        else:
            acc[...] += part
    part_ref[...] = acc[...].T.astype(bf16)
    send.wait()


def out_project(meta, chips, o, cm, gates, pieces):
    patches = cm.shape[1]
    _, rows, local = pieces[0].shape
    width = rows * len(pieces)
    anywhere = pl.BlockSpec(memory_space=pl.ANY)
    return pl.pallas_call(
        functools.partial(out_kernel, len(pieces)),
        out_shape=(sds((patches, width), bf16), sds((SLOTS, width, local), bf16)),
        grid_spec=pltpu.PrefetchScalarGridSpec(
            num_scalar_prefetch=2,
            grid=(1,),
            in_specs=[whole(*o.shape), whole(SLOTS, patches), whole(SLOTS, patches)]
            + [pl.BlockSpec((SLOTS, rows, local), lambda *_: (1, 0, 0)) for _ in pieces],
            out_specs=[whole(patches, width), anywhere],
            scratch_shapes=[
                pltpu.VMEM((width, patches), f32),
                pltpu.VMEM((2, width, GROUP * CAP), bf16),
                pltpu.VMEM((2, GROUP * CAP, patches), bf16),
                pltpu.VMEM((SLOTS, width, local), bf16),
                pltpu.SemaphoreType.DMA((1,)),
            ],
        ),
        compiler_params=params(),
        cost_estimate=cost(8e9, 8e6),
        name="out_project",
    )(meta, chips, o, cm, gates, *pieces)


def middle_kernel(tok_ref, mine_ref, other_ref, gain_ref, router_ref, cm_ref, grad_ref, mid_ref, x_ref, gate_ref):
    width = tok_ref.shape[1]
    middle = tok_ref[...].astype(f32) + (mine_ref[...].astype(f32) + other_ref[...].astype(f32))
    mid_ref[...] = middle
    xhat, _ = norm_stats(middle)
    normed = xhat * gain_ref[...]
    x_ref[:, :width] = normed.astype(bf16)
    x_ref[:, width:] = grad_ref[...]
    logits = lax.dot_general(
        router_ref[...], normed, (((1,), (1,)), ((), ())), precision=highest, preferred_element_type=f32
    )
    gate_ref[...] = dense_gates(logits, cm_ref[...] >= 0)


def middle_step(tokens, mine, other, gain, router_t, cm, masked):
    patches, width = tokens.shape
    return pl.pallas_call(
        middle_kernel,
        out_shape=(
            sds((patches, width), f32),
            sds((patches, 2 * width), bf16),
            sds((SLOTS, patches), f32),
        ),
        in_specs=[vspec()] * 7,
        out_specs=[vspec()] * 3,
        compiler_params=params(),
        cost_estimate=cost(4e9, 6e6),
        name="middle",
    )(tokens, mine, other, gain, router_t, cm, masked)


def gelu_parts(x):
    c = 0.7978845608028654
    square = x * x
    t = jnp.tanh(x * (c + (c * 0.044715) * square))
    half = 0.5 * (1.0 + t)
    slope = half + (0.5 * x) * (1.0 - t * t) * (c + (3.0 * c * 0.044715) * square)
    return x * half, slope


def feed_kernel(
    first, last, rows_of, meta, x_ref, cm_ref, gate_ref, up_ref, down_ref, *rest
):
    if first:
        acc_in, gg_in, keep_ref, send_ref, out_ref, back_ref, gg_ref, acc = rest
    else:
        keep_ref, send_ref, acc, gg_ref = rest
    step = pl.program_id(0)
    e = step + first
    width = x_ref.shape[1] // 2
    size = keep_ref.shape[2]

    @pl.when(step == 0)
    def _():
        acc[...] = acc_in[...] if first else jnp.zeros(acc.shape, f32)
        gg_ref[...] = gg_in[...] if first else jnp.zeros(gg_ref.shape, f32)

    def work(rows_n):
        eq = one_hot(cm_ref[pl.ds(e, 1), :], rows_n)
        hot = jnp.where(eq, 1.0, 0.0).astype(bf16)
        gsel = jnp.where(eq, gate_ref[pl.ds(e, 1), :], 0.0)
        grow = jnp.sum(gsel, axis=1, keepdims=True)
        up = up_ref[0]
        down = down_ref[0]
        got = nn(hot, x_ref[...])
        rows = got[:, :width].astype(bf16)
        grads = got[:, width:]
        hidden = nn(rows, up)
        raw = nn(grads.astype(bf16), down)
        act, slope = gelu_parts(hidden)
        acts = act.astype(bf16)
        outs = nt(down, acts).astype(bf16)
        grad_down = nn((grads * grow).astype(bf16).T, acts).astype(bf16)
        hidden_grad = (raw * grow * slope).astype(bf16)
        back = nt(up, hidden_grad).astype(bf16)
        grad_up = nn(rows.T, hidden_grad).astype(bf16)
        acc[:width] += nn(outs, gsel.astype(bf16))
        acc[width:] += nn(back, hot)
        gg = jnp.sum(raw * acts.astype(f32), axis=1, keepdims=True)
        gg_ref[pl.ds(e, 1), :] = jnp.sum(jnp.where(eq, gg, 0.0), axis=0, keepdims=True)

        @pl.when(meta[2, 0] == 0)
        def _():
            for i, at in enumerate(rows_of):
                keep_ref[i, 0] = grad_up[at : at + size]
                send_ref[i, 0] = grad_down[at : at + size]

        @pl.when(meta[2, 0] != 0)
        def _():
            for i, at in enumerate(rows_of):
                keep_ref[i, 0] = grad_down[at : at + size]
                send_ref[i, 0] = grad_up[at : at + size]

    few = meta[1, e] <= 256

    @pl.when(few)
    def _():
        work(256)

    @pl.when(jnp.logical_not(few))
    def _():
        work(CAP)

    if first:

        @pl.when(e == last - 1)
        def _():
            out_ref[...] = acc[:width].T.astype(bf16)
            back_ref[...] = acc[width:].T.astype(bf16)


def feed(meta, x, cm, gates, weights, rows_of, first, last, carry=()):
    patches, double = x.shape
    width = double // 2
    hidden = weights.shape[2]
    parts = len(rows_of)
    whole = lambda *shape: pl.BlockSpec(shape, lambda e, m: (0,) * len(shape))
    sums = sds((parts, last - first, width // parts, hidden), bf16)
    sums_spec = pl.BlockSpec((parts, 1, width // parts, hidden), lambda e, m: (0, e, 0, 0))
    total, total_spec = sds((double, patches), f32), whole(double, patches)
    gg, gg_spec = sds((SLOTS, patches), f32), whole(SLOTS, patches)
    part, part_spec = sds((patches, width), bf16), whole(patches, width)
    return pl.pallas_call(
        functools.partial(feed_kernel, first, last, rows_of),
        out_shape=(sums, sums, part, part, gg) if first else (sums, sums, total, gg),
        grid_spec=pltpu.PrefetchScalarGridSpec(
            num_scalar_prefetch=1,
            grid=(last - first,),
            in_specs=[
                whole(patches, double),
                whole(SLOTS, patches),
                whole(SLOTS, patches),
                pl.BlockSpec((1, width, hidden), lambda e, m: (e + first, 0, 0)),
                pl.BlockSpec((1, width, hidden), lambda e, m: (e + first + EXPERTS, 0, 0)),
            ]
            + ([total_spec, gg_spec] if first else []),
            out_specs=[sums_spec, sums_spec]
            + ([part_spec, part_spec, gg_spec] if first else [total_spec, gg_spec]),
            scratch_shapes=[pltpu.VMEM((double, patches), f32)] if first else [],
        ),
        compiler_params=params(),
        cost_estimate=cost(20e9, 2e7),
        name="feed",
    )(meta, x, cm, gates, weights, weights, *carry)


def both_kernel(ka_ref, ga_ref, kb_ref, gb_ref, out_ref):
    e = pl.program_id(0)

    @pl.when(e < SPLIT // BATCH)
    def _():
        out_ref[...] = (ka_ref[...].astype(f32) + ga_ref[...].astype(f32)).astype(bf16)

    @pl.when(e >= SPLIT // BATCH)
    def _():
        out_ref[...] = (kb_ref[...].astype(f32) + gb_ref[...].astype(f32)).astype(bf16)


def both_cores(keep_a, got_a, keep_b, got_b):
    parts, _, rows, hidden = keep_a.shape
    block = (parts, BATCH, rows, hidden)
    turn = SPLIT // BATCH
    early = pl.BlockSpec(block, lambda e: (0, jnp.minimum(e, turn - 1), 0, 0))
    late = pl.BlockSpec(block, lambda e: (0, jnp.maximum(e - turn, 0), 0, 0))
    return pl.pallas_call(
        both_kernel,
        out_shape=sds((parts, EXPERTS, rows, hidden), bf16),
        grid=(EXPERTS // BATCH,),
        in_specs=[early, early, late, late],
        out_specs=pl.BlockSpec(block, lambda e: (0, e, 0, 0)),
        compiler_params=params(),
        cost_estimate=cost(5e6, 3e7),
        name="both_cores",
    )(keep_a, got_a, keep_b, got_b)


def both_att_kernel(keep_ref, got_ref, _, out_ref):
    out_ref[...] = (keep_ref[...].astype(f32) + got_ref[...].astype(f32)).astype(bf16)


def both_att(keep, got, ready):
    parts, kinds, count, rows, columns = keep.shape
    block = pl.BlockSpec((parts, kinds, 2 * GROUP, rows, columns), lambda e: (0, 0, e, 0, 0))
    anywhere = pl.BlockSpec(memory_space=pl.ANY)
    return pl.pallas_call(
        both_att_kernel,
        out_shape=sds(keep.shape, bf16),
        grid=(count // (2 * GROUP),),
        in_specs=[block, block, anywhere],
        out_specs=block,
        compiler_params=params(),
        cost_estimate=cost(1e6, 7e6),
        name="both_att",
    )(keep, got, ready)


def in_turn_kernel(*refs):
    pass


def in_turn(value, *earlier):
    anywhere = pl.BlockSpec(memory_space=pl.ANY)
    return pl.pallas_call(
        in_turn_kernel,
        out_shape=sds(value.shape, value.dtype),
        in_specs=[anywhere] * (1 + len(earlier)),
        out_specs=anywhere,
        input_output_aliases={0: 0},
        compiler_params=params(),
        name="in_turn",
    )(value, *earlier)


def gate_back(gates, gg):
    return gates * (gg - jnp.sum(gates * gg, axis=0, keepdims=True))


def norm_back(xhat, inv, grad, gain):
    lifted = grad * gain
    first = jnp.mean(lifted, axis=-1, keepdims=True)
    second = jnp.mean(lifted * xhat, axis=-1, keepdims=True)
    return inv * (lifted - first - xhat * second)


def tn_high(a, b):
    return lax.dot_general(a, b, (((0,), (0,)), ((), ())), precision=highest, preferred_element_type=f32)


def second_back_kernel(
    mid_ref, mine_ref, other_ref, ggm_ref, ggo_ref, gate_ref, router_ref, gain_ref, masked_ref,
    mg_ref, mgb_ref, groute_ref, ggain_ref,
):
    xhat, inv = norm_stats(mid_ref[...])
    logit_grad = gate_back(gate_ref[...], ggm_ref[...] + ggo_ref[...])
    grad = (mine_ref[...].astype(f32) + other_ref[...].astype(f32)) + tn_high(logit_grad, router_ref[...])
    groute_ref[...] = jnp.dot(
        logit_grad, xhat * gain_ref[...], precision=highest, preferred_element_type=f32
    )
    ggain_ref[...] = jnp.sum(grad * xhat, axis=0, keepdims=True)
    middle_grad = masked_ref[...].astype(f32) + norm_back(xhat, inv, grad, gain_ref[...])
    mg_ref[...] = middle_grad
    mgb_ref[...] = middle_grad.astype(bf16)


def second_back(middle, mine, other, gg_mine, gg_other, gates, router_t, gain, masked):
    patches, width = middle.shape
    return pl.pallas_call(
        second_back_kernel,
        out_shape=(
            sds((patches, width), f32),
            sds((patches, width), bf16),
            sds((SLOTS, width), f32),
            sds((1, width), f32),
        ),
        in_specs=[vspec()] * 9,
        out_specs=[vspec()] * 4,
        compiler_params=params(),
        cost_estimate=cost(4e9, 8e6),
        name="second_back",
    )(middle, mine, other, gg_mine, gg_other, gates, router_t, gain, masked)


def out_back_kernel(meta, mg_ref, cm_ref, gate_ref, wo_ref, o_ref, do_ref, gg_ref, grad_ref, hots, got, raws, turned, wide):
    step = pl.program_id(0)
    local = wo_ref.shape[2]
    width = mg_ref.shape[1]

    @pl.when(step == 0)
    def _():
        do_ref[...] = jnp.zeros(do_ref.shape, bf16)
        raws[...] = jnp.zeros(raws.shape, f32)
        gg_ref[...] = jnp.zeros(gg_ref.shape, f32)
        wide[:, :width] = mg_ref[...]
        gate = gate_ref[...]
        high = gate.astype(bf16)
        rest = gate - high.astype(f32)
        mid = rest.astype(bf16)
        low = (rest - mid.astype(f32)).astype(bf16)
        blank = jnp.zeros((128 - 3 * SLOTS, gate.shape[1]), f32)
        stack = jnp.concatenate([high.astype(f32), mid.astype(f32), low.astype(f32), blank], axis=0)
        wide[:, width:] = stack.T.astype(bf16)

    for i in range(GROUP):
        hot = one_hot(cm_ref[pl.ds(step * GROUP + i, 1), :], CAP)
        hots[i * CAP : (i + 1) * CAP, :] = jnp.where(hot, 1.0, 0.0).astype(bf16)
    got[...] = nn(hots[...], wide[...])
    lane = lax.broadcasted_iota(jnp.int32, (1, WIDE), 1)
    carried = (lane >= local) & (lane < local + 3 * STAT)
    lane_s = lax.broadcasted_iota(jnp.int32, (1, 128), 1)
    for i in range(GROUP):
        rows = slice(i * CAP, (i + 1) * CAP)
        raws[rows, :local] = nn(got[rows, :width].astype(bf16), wo_ref[i])
    for i in range(GROUP):
        e = step * GROUP + i
        rows = slice(i * CAP, (i + 1) * CAP)
        gates = got[rows, width:]
        grow = jnp.sum(jnp.where(lane_s % SLOTS == e, gates, 0.0), axis=1, keepdims=True)
        turned[:, rows] = (got[rows, :width] * grow).astype(bf16).T
        off = pl.multiple_of(meta[0, e], PACK)
        mixed_f = o_ref[pl.ds(off, CAP), :].astype(f32)
        raw = raws[rows, :]
        gg = jnp.sum(raw * mixed_f, axis=1, keepdims=True)
        eq = one_hot(cm_ref[pl.ds(e, 1), :], CAP)
        gg_ref[pl.ds(e, 1), :] = jnp.sum(jnp.where(eq, gg, 0.0), axis=0, keepdims=True)
        mixed_grad = (raw * grow).astype(bf16).astype(f32)
        weighed = mixed_grad * mixed_f
        row = jnp.where(carried, mixed_f, mixed_grad)
        for h in range(local // HDIM):
            here = (lane >= h * HDIM) & (lane < (h + 1) * HDIM)
            total = jnp.sum(jnp.where(here, weighed, 0.0), axis=1, keepdims=True)
            high = total.astype(bf16).astype(f32)
            row = jnp.where(lane == local + 3 * STAT + h, high, row)
            row = jnp.where(lane == local + 4 * STAT + h, total - high, row)
        do_ref[pl.ds(off, CAP), :] = row.astype(bf16)
    for i in range(GROUP):
        off = pl.multiple_of(meta[0, step * GROUP + i], PACK)
        grad_ref[i] = nn(turned[:, i * CAP : (i + 1) * CAP], o_ref[pl.ds(off, CAP), :local]).astype(bf16)


def out_back(meta, mg, cm, gates, weights, o):
    patches, width = mg.shape
    local = weights.shape[2]
    rows = o.shape[0]
    return pl.pallas_call(
        out_back_kernel,
        out_shape=(
            sds((rows, WIDE), bf16),
            sds((SLOTS, patches), f32),
            sds((SLOTS, width, local), bf16),
        ),
        grid_spec=pltpu.PrefetchScalarGridSpec(
            num_scalar_prefetch=1,
            grid=(SLOTS // GROUP,),
            in_specs=[
                pl.BlockSpec((patches, width), lambda e, m: (0, 0)),
                pl.BlockSpec((SLOTS, patches), lambda e, m: (0, 0)),
                pl.BlockSpec((SLOTS, patches), lambda e, m: (0, 0)),
                pl.BlockSpec((GROUP, width, local), lambda e, m: (e, 0, 0)),
                pl.BlockSpec((rows, WIDE), lambda e, m: (0, 0)),
            ],
            out_specs=[
                pl.BlockSpec((rows, WIDE), lambda e, m: (0, 0)),
                pl.BlockSpec((SLOTS, patches), lambda e, m: (0, 0)),
                pl.BlockSpec((GROUP, width, local), lambda e, m: (e, 0, 0)),
            ],
            scratch_shapes=[
                pltpu.VMEM((GROUP * CAP, patches), bf16),
                pltpu.VMEM((GROUP * CAP, width + 128), f32),
                pltpu.VMEM((GROUP * CAP, WIDE), f32),
                pltpu.VMEM((width, GROUP * CAP), bf16),
                pltpu.VMEM((patches, width + 128), bf16),
            ],
        ),
        compiler_params=params(),
        cost_estimate=cost(10e9, 2e7),
        name="out_back",
    )(meta, mg, cm, gates, weights, o)


def attend_back_kernel(
    meta, q_in, do_in, k_ref, v_ref, dq_ref, dk_ref, dv_ref, km, kt, vt, dk, dv, q_ref, do_ref, sems
):
    heads = km.shape[0]
    local = heads * HDIM
    copies = [
        pltpu.make_async_copy(q_in, q_ref, sems.at[0]),
        pltpu.make_async_copy(do_in, do_ref, sems.at[1]),
    ]
    for copy in copies:
        copy.start()
    at_row = lax.broadcasted_iota(jnp.int32, (WIDE, 128), 0) - local
    at_lane = lax.broadcasted_iota(jnp.int32, (WIDE, 128), 1)
    totals = (at_row < 3 * STAT) & (at_lane < STAT)
    sums = (at_row >= 3 * STAT) & (at_row < 5 * STAT) & (at_lane >= STAT) & (at_lane < 2 * STAT)
    same = (at_row >= 0) & ((at_row - at_lane) % STAT == 0)
    pick = jnp.where(same & (totals | sums), 1.0, 0.0).astype(bf16)
    head_mask, _ = masks(heads)
    k = k_ref[...].astype(f32)
    k_t = k.T
    v_t = v_ref[...].astype(f32).T
    row = lax.broadcasted_iota(jnp.int32, (WIDE, 1), 0)
    for h in range(heads):
        here = (row >= h * HDIM) & (row < (h + 1) * HDIM)
        km[h] = jnp.where(head_mask[h], k, 0.0).astype(bf16)
        kt[h] = jnp.where(here, k_t, 0.0).astype(bf16)
        vt[h] = jnp.where(here, v_t, 0.0).astype(bf16)
    dk[...] = jnp.zeros(dk.shape, f32)
    dv[...] = jnp.zeros(dv.shape, f32)
    dq_ref[...] = jnp.zeros(dq_ref.shape, bf16)
    for copy in copies:
        copy.wait()
    tiles = (meta[0, EXPERTS] + (QT - 1)) // QT

    def tile(i, carry):
        start = pl.multiple_of(i * QT, QT)
        q = q_ref[pl.ds(start, QT), :]
        do = do_ref[pl.ds(start, QT), :]
        stats = nn(do, pick)
        q_t = q.T
        do_t = do.T
        dq = jnp.zeros((QT, WIDE), f32)
        pairs = [(nn(q, kt[0]), nn(do, vt[0]))]
        for h in range(heads):
            at = slice(h * HDIM, (h + 1) * HDIM)
            if h + 1 < heads:
                pairs.append((nn(q, kt[h + 1]), nn(do, vt[h + 1])))
            s, dp = pairs[h]
            p = jnp.exp2(s * score_scale - stats[:, h : h + 1])
            ds = (p * (dp - stats[:, STAT + h : STAT + h + 1])).astype(bf16)
            dq = dq + nn(ds, km[h])
            dk[at, :] += nn(q_t[at, :], ds)
            dv[at, :] += nn(do_t[at, :], p.astype(bf16))
        dq_ref[pl.ds(start, QT), :] = (dq * 0.125).astype(bf16)
        return carry

    lax.fori_loop(0, tiles, tile, 0)
    dk_ref[...] = (dk[...] * 0.125).astype(bf16)
    dv_ref[...] = dv[...].astype(bf16)


def attend_back(meta, q, do, k, v, heads):
    rows = q.shape[0]
    patches = k.shape[0]
    return pl.pallas_call(
        attend_back_kernel,
        out_shape=(
            sds((rows, WIDE), bf16),
            sds((heads * HDIM, patches), bf16),
            sds((heads * HDIM, patches), bf16),
        ),
        in_specs=[pl.BlockSpec(memory_space=pltpu.SMEM)]
        + [pl.BlockSpec(memory_space=pl.ANY)] * 2
        + [vspec()] * 2,
        out_specs=[vspec()] * 3,
        scratch_shapes=[
            pltpu.VMEM((heads, patches, WIDE), bf16),
            pltpu.VMEM((heads, WIDE, patches), bf16),
            pltpu.VMEM((heads, WIDE, patches), bf16),
            pltpu.VMEM((heads * HDIM, patches), f32),
            pltpu.VMEM((heads * HDIM, patches), f32),
            pltpu.VMEM((rows, WIDE), bf16),
            pltpu.VMEM((rows, WIDE), bf16),
            pltpu.SemaphoreType.DMA((2,)),
        ],
        compiler_params=params(),
        cost_estimate=cost(60e9, 2e7),
        name="attend_back",
    )(meta, q, do, k, v)


def width_of(ref):
    return ref.shape[1]


def in_back_kernel(
    rows_of, meta, dq_ref, dk_ref, dv_ref, rows_ref, x_ref, cm_ref, wq_ref, wv_ref, go_ref,
    keep_ref, send_ref, part_ref, acc, got, outs, hots,
):
    step = pl.program_id(0)
    local = wq_ref.shape[2]
    size = keep_ref.shape[3]
    cores = width_of(x_ref) // (size * len(rows_of))

    def put(ref, at, core):
        for i, row in enumerate(rows_of):
            start = pl.multiple_of(row + size * core, 8)
            for kind in range(2):
                ref[i, kind, at] = got[kind, at, pl.ds(start, size), :].astype(bf16)

    @pl.when(step == 0)
    def _():
        acc[...] = jnp.zeros(acc.shape, f32)

    for i in range(GROUP):
        e = step * GROUP + i
        rows = slice(i * CAP, (i + 1) * CAP)
        hot = one_hot(cm_ref[pl.ds(e, 1), :], CAP)
        hots[rows, :] = jnp.where(hot, 1.0, 0.0).astype(bf16)
        off = pl.multiple_of(meta[0, e], PACK)
        dq = dq_ref[pl.ds(off, CAP), :local]
        outs[:, rows] = nt(wq_ref[i], dq).astype(bf16)
        got[0, i] = nn(rows_ref[i], dq)
        got[1, i] = go_ref[i].astype(f32)
    acc[...] += nn(outs[...], hots[...])

    @pl.when(step == SLOTS // GROUP - 1)
    def _():
        dk = dk_ref[...]
        dv = dv_ref[...]
        last = GROUP - 1
        acc[...] += nn(wq_ref[last], dk) + nn(wv_ref[0], dv)
        part_ref[...] = acc[...].T.astype(bf16)
        x = x_ref[...]
        got[0, last] = nn(dk, x).T
        got[1, last] = nn(dv, x).T

    core = meta[2, 0]
    for i in range(GROUP):
        put(keep_ref, i, core)
        put(send_ref, i, cores - 1 - core)


def in_back(meta, dq, dk, dv, rows_att, x, cm, weights, grad_out, rows_of, cores):
    patches, width = x.shape
    local = weights.shape[2]
    rows = dq.shape[0]
    parts = len(rows_of)
    size = width // (parts * cores)
    sums = sds((parts, 2, SLOTS, size, local), bf16)
    sums_spec = pl.BlockSpec((parts, 2, GROUP, size, local), lambda e, m: (0, 0, e, 0, 0))
    return pl.pallas_call(
        functools.partial(in_back_kernel, rows_of),
        out_shape=(sums, sums, sds((patches, width), bf16)),
        grid_spec=pltpu.PrefetchScalarGridSpec(
            num_scalar_prefetch=1,
            grid=(SLOTS // GROUP,),
            in_specs=[
                pl.BlockSpec((rows, WIDE), lambda e, m: (0, 0)),
                pl.BlockSpec((local, patches), lambda e, m: (0, 0)),
                pl.BlockSpec((local, patches), lambda e, m: (0, 0)),
                pl.BlockSpec((GROUP, width, CAP), lambda e, m: (e, 0, 0)),
                pl.BlockSpec((patches, width), lambda e, m: (0, 0)),
                pl.BlockSpec((SLOTS, patches), lambda e, m: (0, 0)),
                pl.BlockSpec((GROUP, width, local), lambda e, m: (e, 0, 0)),
                pl.BlockSpec((1, width, local), lambda e, m: (EXPERTS + 1, 0, 0)),
                pl.BlockSpec((GROUP, width, local), lambda e, m: (e, 0, 0)),
            ],
            out_specs=[sums_spec, sums_spec, pl.BlockSpec((patches, width), lambda e, m: (0, 0))],
            scratch_shapes=[
                pltpu.VMEM((width, patches), f32),
                pltpu.VMEM((2, GROUP, width, local), f32),
                pltpu.VMEM((width, GROUP * CAP), bf16),
                pltpu.VMEM((GROUP * CAP, patches), bf16),
            ],
        ),
        compiler_params=params(),
        cost_estimate=cost(10e9, 2e7),
        name="in_back",
    )(meta, dq, dk, dv, rows_att, x, cm, weights, weights, grad_out)


def route_back_kernel(tok_ref, ggm_ref, ggo_ref, gate_ref, gain_ref, router_ref, lg_ref, groute_ref, ggain_ref):
    xhat, _ = norm_stats(tok_ref[...].astype(f32))
    logit_grad = gate_back(gate_ref[...], ggm_ref[...] + ggo_ref[...])
    lg_ref[...] = logit_grad
    plain = jnp.dot(logit_grad, xhat, precision=highest, preferred_element_type=f32)
    groute_ref[...] = plain * gain_ref[...]
    ggain_ref[...] = 0.5 * jnp.sum(plain * router_ref[...], axis=0, keepdims=True)


def route_back(tokens, gg_mine, gg_other, gates, gain, router_t):
    patches, width = tokens.shape
    return pl.pallas_call(
        route_back_kernel,
        out_shape=(sds((SLOTS, patches), f32), sds((SLOTS, width), f32), sds((1, width), f32)),
        in_specs=[vspec()] * 6,
        out_specs=[vspec()] * 3,
        compiler_params=params(),
        cost_estimate=cost(3e9, 2e6),
        name="route_back",
    )(tokens, gg_mine, gg_other, gates, gain, router_t)


def first_gain_kernel(tok_ref, mine_ref, part_ref, ggain_ref):
    xhat, _ = norm_stats(tok_ref[...].astype(f32))
    ggain_ref[...] = part_ref[...] + jnp.sum(mine_ref[...].astype(f32) * xhat, axis=0, keepdims=True)


def first_gain(tokens, mine, part):
    return pl.pallas_call(
        first_gain_kernel,
        out_shape=sds(part.shape, f32),
        in_specs=[vspec()] * 3,
        out_specs=vspec(),
        compiler_params=params(),
        cost_estimate=cost(3e9, 3e6),
        name="first_gain",
    )(tokens, mine, part)


def first_back_kernel(tok_ref, mine_ref, other_ref, lg_ref, router_ref, gain_ref, mg_ref, gt_ref):
    xhat, inv = norm_stats(tok_ref[...].astype(f32))
    grad = (mine_ref[...].astype(f32) + other_ref[...].astype(f32)) + tn_high(lg_ref[...], router_ref[...])
    gt_ref[...] = mg_ref[...] + norm_back(xhat, inv, grad, gain_ref[...])


def first_back(tokens, mine, other, logit_grad, router_t, gain, middle_grad):
    patches, width = tokens.shape
    return pl.pallas_call(
        first_back_kernel,
        out_shape=sds((patches, width), f32),
        in_specs=[vspec()] * 7,
        out_specs=vspec(),
        compiler_params=params(),
        cost_estimate=cost(3e9, 6e6),
        name="first_back",
    )(tokens, mine, other, logit_grad, router_t, gain, middle_grad)


def tie(*values):
    return lax.optimization_barrier(values)


def after(value, first):
    return lax.optimization_barrier((value, first))[0]


def other_half(x):
    return lax.ppermute(x, "mp", [(0, 1), (1, 0)])


def cube_steps(size):
    steps = []
    step = 1
    while step < size:
        steps.append(step)
        step *= 2
    return steps


def cube_gather(x, size, between):
    index = lax.axis_index("dp")
    x = x[None]
    for at, step in enumerate(reversed(cube_steps(size))):
        if at == 1:
            x = after(x, between)
        got = lax.ppermute(x, "dp", [(i, i ^ step) for i in range(size)])
        upper = (index // step) % 2 == 1
        x = jnp.where(
            upper, jnp.concatenate([got, x], axis=0), jnp.concatenate([x, got], axis=0)
        )
    return x


class Ring:
    def __init__(self, size):
        self.size = size
        self.chips = size // 2
        half = self.chips // 2
        self.order = [2 * i for i in range(half)] + [2 * i + 1 for i in reversed(range(half))]
        self.groups = [[2 * chip + core for chip in self.order] for core in range(2)]
        self.next = []
        for at, chip in enumerate(self.order):
            self.next.append((2 * chip, 2 * self.order[(at + 1) % self.chips]))
            self.next.append((2 * chip + 1, 2 * self.order[at - 1] + 1))
        self.back = [(b, a) for a, b in self.next]
        self.swap = [(i, i ^ 1) for i in range(size)]
        index = lax.axis_index("dp")
        self.core = index % 2
        chip = index // 2
        place = jnp.where(chip % 2 == 0, chip // 2, self.chips - 1 - chip // 2)
        self.place = jnp.where(self.core == 0, place, self.chips - place)

    def chip(self, place):
        place = jnp.where(self.core == 0, place, -place) % self.chips
        return jnp.where(place < self.chips // 2, 2 * place, 2 * (self.chips - 1 - place) + 1)

    def cross(self, x):
        return lax.ppermute(x, "dp", self.swap)

    def step(self, x):
        return lax.ppermute(x, "dp", self.next)

    def chip_rows(self, shard, got):
        first = jnp.where(self.core == 0, shard, got)
        second = jnp.where(self.core == 0, got, shard)
        return jnp.concatenate([first, second], axis=1)

    def sources(self):
        places = [self.place]
        for step in range(1, self.chips // 2 + 1):
            places.append(self.place - step)
            if step < self.chips // 2:
                places.append(self.place + step)
        return jnp.stack([self.chip(p) for p in places]).astype(jnp.int32)

    def finish(self, total):
        count, rows, columns = total.shape
        total = total.reshape(count, 2, rows // 2, columns)
        mine = lax.dynamic_index_in_dim(total, self.core, 1, keepdims=False)
        theirs = lax.dynamic_index_in_dim(total, 1 - self.core, 1, keepdims=False)
        theirs = self.cross(theirs)
        first = jnp.where(self.core == 0, mine, theirs).astype(f32)
        second = jnp.where(self.core == 0, theirs, mine).astype(f32)
        return first, second

    def offload(self, total):
        return lax.psum_scatter(
            total, "dp", scatter_dimension=0, tiled=True, axis_index_groups=self.groups
        )[0]


def body(dp_size, tokens, cotangent, task_ids, att_routes, mlp_routes, valid, gain_one, w_query, w_key,
         w_value, w_out, router_att, gain_two, w_up, w_down, router_mlp):
    tokens = tokens[0]
    patches, width = tokens.shape
    local = w_key.shape[1]
    heads = local // HDIM
    tasks = router_att.shape[0]

    att_shard = jnp.concatenate([w_query, w_key[None], jnp.swapaxes(w_out, 1, 2), w_value[None]], axis=0)
    feed_shard = jnp.concatenate([w_up, jnp.swapaxes(w_down, 1, 2)], axis=0)
    ring = Ring(dp_size) if dp_size == 16 else None
    if ring is None:
        chips = jnp.zeros((1,), jnp.int32)
        pieces = [lax.all_gather(att_shard, "dp", axis=1, tiled=True)]
    else:
        chips = ring.sources()
        piece = ring.chip_rows(att_shard, ring.cross(att_shard))
        pieces = [piece]
        for step in range(1, ring.chips // 2 + 1):
            piece = ring.step(piece)
            pieces.append(piece)
            if step < ring.chips // 2:
                pieces.append(ring.cross(piece))
            if step == HOLD:
                feed_shard = after(feed_shard, piece)
    feed_full = lax.all_gather(feed_shard, "dp", axis=1, tiled=True)

    gain_1 = gain_one[None]
    gain_2 = gain_two[None]
    task = task_ids[0]
    pick = lambda router: jnp.pad(
        lax.dynamic_index_in_dim(router, task, 0, keepdims=False).T, ((0, SLOTS - EXPERTS), (0, 0))
    )
    route_1 = pick(router_att)
    route_2 = pick(router_mlp)
    masked = cotangent[0] * valid[0][:, None].astype(bf16)

    x_one, gates_1, cm_1, cm_2, meta = prep(tokens, gain_1, route_1, att_routes[0].T, mlp_routes[0].T)
    core = jnp.full((1, SLOTS), 0 if ring is None else ring.core, jnp.int32)
    meta_1 = jnp.concatenate([meta[0:2, :, 0], core], axis=0)
    meta_2 = jnp.concatenate([meta[2:4, :, 0], core], axis=0)

    o, k, v, q, rows_att, in_full = attend(meta_1, chips, x_one, cm_1, pieces)
    part, out_full = out_project(meta_1, chips, o, cm_1, gates_1, pieces)
    middle, x_two, gates_2 = middle_step(tokens, part, other_half(part), gain_2, route_2, cm_2, masked)
    rows_of = [0] if ring is None else [chip * (width // ring.chips) for chip in ring.order]
    keep_a, send_a, total, gg_2 = feed(meta_2, x_two, cm_2, gates_2, feed_full, rows_of, 0, SPLIT)
    keep_b, send_b, part_two, back_two, gg_2 = feed(
        meta_2, x_two, cm_2, gates_2, feed_full, rows_of, SPLIT, EXPERTS, (total, gg_2)
    )
    back_two_other, gg_2_other = other_half(back_two), other_half(gg_2)
    if ring is not None:
        feed_sum = both_cores(keep_a, ring.cross(send_a), keep_b, ring.cross(send_b))
        feed_sum = in_turn(feed_sum, back_two_other, gg_2_other)
        middle_here = after(middle, feed_sum)
    else:
        middle_here = middle
    middle_grad, mg, groute_2, ggain_2 = second_back(
        middle_here, back_two, back_two_other, gg_2, gg_2_other, gates_2, route_2, gain_2, masked
    )
    if ring is not None:
        feed_sum = ring.offload(feed_sum)
    part_other = other_half(after(part_two, mg))
    layer_out = (middle + (part_two.astype(f32) + part_other.astype(f32))).astype(bf16)
    do, gg_1, grad_out = out_back(meta_1, mg, cm_1, gates_1, out_full, o)
    gg_other = other_half(gg_1)
    dq, dk, dv = attend_back(meta_1, q, do, k, v, heads)
    dq, gg_other = tie(dq, gg_other)
    keep_att, send_att, back_one = in_back(
        meta_1, dq, dk, dv, rows_att, x_one, cm_1, in_full, grad_out, rows_of, 1 if ring is None else 2
    )
    logit_grad, groute_1, ggain_1 = route_back(
        tokens, gg_1, gg_other, after(gates_1, back_one), gain_1, route_1
    )
    mark = (jnp.arange(width) == task).astype(f32)[None]
    small = jnp.concatenate([groute_1[:EXPERTS], mark, groute_2[:EXPERTS], ggain_2], axis=0).astype(bf16)
    back_other = other_half(back_one)
    gain_sum = first_gain(tokens, back_one, ggain_1)
    small = jnp.concatenate([small, gain_sum.astype(bf16)], axis=0)
    if ring is None:
        scatter = lambda g: lax.psum_scatter(g[0], "dp", scatter_dimension=1, tiled=True).astype(f32)
        q_mine, o_mine = scatter(keep_att[:, 0]), scatter(keep_att[:, 1])
        up_mine = scatter(jnp.concatenate([keep_a, keep_b], axis=1))
        down_mine = scatter(jnp.concatenate([send_a, send_b], axis=1))
    else:
        att_sum = both_att(keep_att, ring.cross(send_att), ggain_1)
        att_sum = ring.offload(in_turn(att_sum, feed_sum)).astype(f32)
        q_mine, o_mine = att_sum[0], att_sum[1]
        up_mine, down_mine = ring.finish(feed_sum)
        middle_grad = after(middle_grad, (up_mine, down_mine))
    grad_tokens = first_back(
        tokens, back_one, back_other, logit_grad, route_1, gain_1, middle_grad
    )

    every = cube_gather(small, dp_size, grad_tokens).astype(f32)
    named = every[:, EXPERTS, :tasks]
    route_sum = lambda g: jnp.swapaxes(
        jnp.einsum("it,ied->ted", named, g, precision=highest, preferred_element_type=f32), 1, 2
    )
    grad_router_att = route_sum(every[:, :EXPERTS])
    grad_router_mlp = route_sum(every[:, SLOTS : SLOTS + EXPERTS])
    gains = jnp.sum(every[:, 2 * SLOTS - 1 :], axis=0)
    grad_gain_two = gains[0]
    grad_gain_one = gains[1] + other_half(gains[1:])[0]
    return (
        layer_out[None],
        grad_tokens[None],
        grad_gain_one,
        q_mine[:EXPERTS],
        q_mine[EXPERTS],
        o_mine[EXPERTS],
        jnp.swapaxes(o_mine[:EXPERTS], 1, 2),
        grad_router_att,
        grad_gain_two,
        up_mine,
        jnp.swapaxes(down_mine, 1, 2),
        grad_router_mlp,
    )


def solution(mesh):
    dp_size = mesh.shape["dp"]

    def run(*args):
        return body(dp_size, *args)

    return jax.shard_map(
        run,
        mesh=mesh,
        in_specs=(
            P("dp", None, None), P("dp", None, None), P("dp"), P("dp", None, None), P("dp", None, None),
            P("dp", None), P(), P(None, "dp", "mp"), P("dp", "mp"), P("dp", "mp"), P(None, "mp", "dp"),
            P(), P(), P(None, "dp", "mp"), P(None, "mp", "dp"), P(),
        ),
        out_specs=(
            P("dp", None, None), P("dp", None, None), P(), P(None, "dp", "mp"), P("dp", "mp"), P("dp", "mp"),
            P(None, "mp", "dp"), P(), P(), P(None, "dp", "mp"), P(None, "mp", "dp"), P(),
        ),
        check_vma=False,
    )
```
